32 devices in a mesh: gx: 8 (over z, y), gy: 4 (over x, core).
Axes of the slice: x: 2, y: 2, z: 4, core: 2. Of those that a mesh axis runs over, the one named last changes fastest.
Arguments:
- cell_state: float32 [17, 64, 64, 256], P(None, 'gx', 'gy')
- evap_rate: float32 [8], replicated, may hold values from 0.05 to 0.5
- parcels: float32 [8, 524288], P(None, ('gx', 'gy'))
- crossing: int32 [2, 32768], P(None, ('gx', 'gy')), may hold values from 0 to 16383, as said below
- conv_mass: float32 [8, 65536], P(None, ('gx', 'gy')), may hold values from 0.5 to 2
- conv_owner: int32 [65536, 1], P(('gx', 'gy')), may hold values from 0 to 31; in each aligned block of 2048 rows (0 to 2047, 2048 to 4095, ...) at most 128 rows name the same one
- conv_cell: int32 [65536], P(('gx', 'gy')), may hold values from 0 to 32767
Outputs:
- new_cells: float32 [14, 64, 64, 256], P(None, 'gx', 'gy')
- new_parcels: float32 [8, 524288], P(None, ('gx', 'gy'))
The draws below stay inside these ranges and needn't reach their ends.
Inputs may be any that keep to these rules, and one draw needn't show every extreme that they name: On each device the 2048 entries of crossing are distinct local parcel slots. `conv_owner`: the rows of one device name one owner at most 128 times.
All inputs are finite; a program needn't handle non-finite values.
Results may differ from the reference program's by a relative error of at most 0.0003.
Values sent between devices are 32-bit elements; how exact they have to be, the bound alone decides.
No kernel may reach another device: no remote copies, remote signals or barrier semaphores. Data moves between devices by JAX's collectives and lax.ppermute only.
A program may use at most 64 MiB of HBM per device.

```python
import math
import jax
import jax.numpy as jnp
import numpy as np

SECTIONS = 8
SPECIES = 6
ATTRS = 8
CX = 8
CY = 16
CZ = 256
PAR_DEV = 16384
CONV_DEV = 2048
OWNERS = 32
CROSS = 1024
CAP = 128
CELLS_DEV = 32768
NX = 64
NY = 64
NZ = 256
PARCELS = 524288
CONV_ROWS = 65536
N_GX = 8
N_GY = 4


def draw_cell_state(key, part):
    key_sec, key_spe, key_vel = jax.random.split(key, 3)
    grid = (NX, NY, NZ)
    sections = jnp.exp(jax.random.uniform(key_sec, (SECTIONS,) + grid, jnp.float32, math.log(0.2), math.log(2.0)))
    species = jax.random.uniform(key_spe, (SPECIES,) + grid, jnp.float32, 0.1, 1.0)
    courant = jax.random.uniform(key_vel, (3,) + grid, jnp.float32, -0.15, 0.15)
    return jnp.concatenate([sections, species, courant], axis=0).astype(jnp.float32)


def draw_parcels(key, part):
    key_pos, key_vel, key_dia, key_tem = jax.random.split(key, 4)
    position = jax.random.normal(key_pos, (3, PARCELS), jnp.float32)
    velocity = jax.random.normal(key_vel, (3, PARCELS), jnp.float32)
    diameter = jax.random.uniform(key_dia, (1, PARCELS), jnp.float32, 0.5, 2.0)
    warmth = jax.random.uniform(key_tem, (1, PARCELS), jnp.float32, 0.5, 1.5)
    return jnp.concatenate([position, velocity, diameter, warmth], axis=0).astype(jnp.float32)


def draw_crossing(key, part):
    device_count = PARCELS // PAR_DEV
    keys = jax.random.split(jax.random.fold_in(key, 17), device_count)
    chosen = jax.vmap(lambda one_key: jax.random.permutation(one_key, PAR_DEV)[:2 * CROSS])(keys)
    chosen = chosen.reshape(device_count, 2, CROSS).transpose(1, 0, 2).reshape(2, device_count * CROSS)
    return chosen.astype(jnp.int32)


def with_ends(values, own_key, least, top_value):
    longest = values.shape.index(max(values.shape))
    spots = []
    for shift in (0, 1):
        where = [jax.random.randint(jax.random.fold_in(own_key, axis), (), 0, length) for axis, length in enumerate(values.shape)]
        where[longest] = (where[longest] + shift) % values.shape[longest]
        spots.append(tuple(where))
    return values.at[spots[0]].set(least).at[spots[1]].set(top_value)


def levels(own_key, dims, shards, smallest, high):
    def one(axis_at, blocks):
        heights = jax.random.uniform(jax.random.fold_in(jax.random.fold_in(own_key, 6), axis_at), (blocks,), jnp.float32, smallest / len(shards), high / len(shards))
        return jnp.repeat(jnp.exp(heights), dims[axis_at] // blocks).reshape((-1,) + (1,) * (len(dims) - axis_at - 1))

    factor_of = one(*shards[0])
    for cut in shards[1:]:
        factor_of = factor_of * one(*cut)
    return factor_of


def routed_block(rng, own, number, rows, count, top, bound, skew):
    ranking = jax.random.permutation(rng, count)
    heavy_load, common = load_shares(count, rows * top, bound, skew, True), load_shares(count, rows * top, bound, skew, False)
    places = jnp.arange(count)

    def named(sizes, offset_by):
        used = int((sizes > 0).sum())
        fixed = max(1, used // 4)
        moved = fixed + (places - fixed + offset_by * (used - fixed)) % max(1, count - fixed)
        return jnp.zeros((count,), jnp.int32).at[ranking[jnp.where(places < fixed, places, moved)]].set(jnp.asarray(sizes, jnp.int32))

    sizes = jnp.where(number % 4 == 0, named(heavy_load, number // 4), named(common, number - number // 4 - 1))
    mixed = jax.random.permutation(jax.random.fold_in(own, 3), count)
    source_of, sink = mixed[0:count // 2 * 2:2], mixed[1:count // 2 * 2:2]
    margin = jnp.minimum(sizes[source_of] - 1, bound - sizes[sink]) // 2
    margin = jnp.where((source_of == ranking[0]) | (sink == ranking[0]) | (sizes[sink] == 0), 0, jnp.maximum(margin, 0))
    moved = jax.random.randint(jax.random.fold_in(own, 4), (count // 2,), 0, 1 << 20) % (margin + 1)
    sizes = sizes.at[source_of].add(-moved).at[sink].add(moved)
    items = jnp.searchsorted(jnp.cumsum(sizes), jnp.arange(rows * top), side="right").astype(jnp.int32)
    table = items.reshape(top, rows).T
    table = table[jax.random.permutation(jax.random.fold_in(own, 1), rows)]
    offset_by = jax.random.randint(jax.random.fold_in(own, 2), (rows, 1), 0, top)
    return jnp.take_along_axis(table, (jnp.arange(top)[None, :] + offset_by) % top, axis=1)


def load_shares(count, total, reach, skew, full):
    portions = [(1 << 20) // math.isqrt(grade ** skew) + 1 for grade in range(1, count + 1)]
    largest = reach if full else min(reach, max(-(-total // count), total * portions[0] // sum(portions)))
    least = 1 if total - largest >= count - 1 else 0
    holding, rest = [largest] + [least] * (count - 1), total - largest - least * (count - 1)
    while rest > 0:
        candidates = [i for i in range(1, count) if holding[i] < largest] or [i for i in range(1, count) if holding[i] < reach]
        whole, left = sum([portions[i] for i in candidates]), rest
        for i in candidates:
            extra = min(reach - holding[i], max(1, left * portions[i] // whole), rest)
            holding[i] = holding[i] + extra
            rest = rest - extra
    return np.array(holding)


def setup_inputs(seed: int = 0) -> dict:
    key_list = jax.random.split(jax.random.key(seed), 8)
    cell_state = draw_cell_state(jax.random.fold_in(key_list[7], 71), 0)
    evap_rate = jnp.clip(jnp.exp(jax.random.uniform(key_list[1], (SECTIONS,), jnp.float32, math.log(0.05), math.log(0.5))), 0.05, 0.5)
    parcels = draw_parcels(jax.random.fold_in(key_list[7], 71), 0)
    crossing = draw_crossing(jax.random.fold_in(key_list[7], 71), 0)
    conv_mass = jnp.clip(jnp.exp(math.log(2.0) - 1.3862944 * jax.random.uniform(key_list[4], (SECTIONS, CONV_ROWS), jnp.float32) ** levels(key_list[4], (SECTIONS, CONV_ROWS), ((1, 32),), -0.2, 0.2)), 0.5, 2.0)
    conv_owner_keys = jax.random.split(jax.random.fold_in(key_list[5], 1), CONV_ROWS // CONV_DEV)
    conv_owner_turns = jax.random.permutation(jax.random.fold_in(key_list[5], 3), CONV_ROWS // CONV_DEV)
    conv_owner = jax.vmap(lambda own, number: routed_block(jax.random.fold_in(key_list[5], 2), own, number, CONV_DEV, OWNERS, 1, CAP, 2))(conv_owner_keys, conv_owner_turns).reshape((CONV_ROWS, 1))
    conv_cell = with_ends(jax.random.randint(key_list[6], (CONV_ROWS,), 0, CELLS_DEV), jax.random.fold_in(key_list[6], 1), 0, CELLS_DEV - 1).astype(jnp.int32)
    return {"cell_state": cell_state, "evap_rate": evap_rate, "parcels": parcels, "crossing": crossing, "conv_mass": conv_mass, "conv_owner": conv_owner, "conv_cell": conv_cell}


def advect(cell_state):
    amount = cell_state[:SECTIONS + SPECIES]
    courant = cell_state[SECTIONS + SPECIES:]
    face_x = 0.5 * (courant[0] + jnp.roll(courant[0], -1, axis=0))
    flux_x = jnp.maximum(face_x, 0.0) * amount + jnp.minimum(face_x, 0.0) * jnp.roll(amount, -1, axis=1)
    change_x = flux_x - jnp.roll(flux_x, 1, axis=1)
    face_y = 0.5 * (courant[1] + jnp.roll(courant[1], -1, axis=1))
    flux_y = jnp.maximum(face_y, 0.0) * amount + jnp.minimum(face_y, 0.0) * jnp.roll(amount, -1, axis=2)
    change_y = flux_y - jnp.roll(flux_y, 1, axis=2)
    face_z = 0.5 * (courant[2][:, :, :-1] + courant[2][:, :, 1:])
    flux_z = jnp.maximum(face_z, 0.0) * amount[:, :, :, :-1] + jnp.minimum(face_z, 0.0) * amount[:, :, :, 1:]
    flux_z = jnp.pad(flux_z, ((0, 0), (0, 0), (0, 0), (1, 1)))
    change_z = flux_z[:, :, :, 1:] - flux_z[:, :, :, :-1]
    return amount - change_x - change_y - change_z


def evaporate(moved, evap_rate):
    sections = moved[:SECTIONS]
    species = moved[SECTIONS:]
    vapour = species[0]
    loss = evap_rate[:, None, None, None] * sections / (1.0 + vapour)
    passed = jnp.concatenate([loss[1:], jnp.zeros_like(loss[:1])], axis=0)
    new_sections = sections - loss + 0.5 * passed
    new_fuel = vapour + loss[0] + 0.5 * jnp.sum(loss[1:], axis=0)
    new_species = jnp.concatenate([new_fuel[None], species[1:]], axis=0)
    return new_sections, new_species


def advance(parcels):
    position = parcels[0:3]
    velocity = parcels[3:6]
    diameter = parcels[6]
    warmth = parcels[7]
    factor = 0.8 / (1.0 + diameter * diameter)
    velocity_new = velocity * (1.0 - factor)
    position_new = position + 0.5 * (velocity + velocity_new)
    diameter_new = diameter * (1.0 - 0.05 * warmth)
    warmth_new = warmth + factor * (1.0 - warmth)
    return jnp.concatenate([position_new, velocity_new, diameter_new[None], warmth_new[None]], axis=0)


def reference(cell_state, evap_rate, parcels, crossing, conv_mass, conv_owner, conv_cell):
    moved = advect(cell_state)
    new_sections, new_species = evaporate(moved, evap_rate)
    owner = conv_owner[:, 0]
    owner_x = owner // N_GY
    owner_y = owner % N_GY
    local_x = conv_cell // (CY * CZ)
    local_y = (conv_cell // CZ) % CY
    local_z = conv_cell % CZ
    flat_cell = ((owner_x * CX + local_x) * NY + owner_y * CY + local_y) * NZ + local_z
    deposit = jnp.zeros((SECTIONS, NX * NY * NZ), jnp.float32).at[:, flat_cell.astype(jnp.int32)].add(conv_mass)
    deposit = deposit.reshape(SECTIONS, NX, NY, NZ)
    new_cells = jnp.concatenate([new_sections + deposit, new_species], axis=0)

    advanced = advance(parcels)
    grouped = advanced.reshape(ATTRS, N_GX, N_GY, PAR_DEV)
    lists = crossing.reshape(2, N_GX, N_GY, CROSS)
    up_sent = jnp.take_along_axis(grouped, jnp.broadcast_to(lists[0][None], (ATTRS, N_GX, N_GY, CROSS)), axis=3)
    down_sent = jnp.take_along_axis(grouped, jnp.broadcast_to(lists[1][None], (ATTRS, N_GX, N_GY, CROSS)), axis=3)
    arrive_up = jnp.roll(up_sent, 1, axis=1)
    arrive_down = jnp.roll(down_sent, -1, axis=1)
    device_base = (jnp.arange(N_GX * N_GY, dtype=jnp.int32) * PAR_DEV).reshape(N_GX, N_GY, 1)
    flat_up = (device_base + lists[0]).reshape(-1).astype(jnp.int32)
    flat_down = (device_base + lists[1]).reshape(-1).astype(jnp.int32)
    new_parcels = advanced.at[:, flat_up].set(arrive_up.reshape(ATTRS, -1))
    new_parcels = new_parcels.at[:, flat_down].set(arrive_down.reshape(ATTRS, -1))
    return new_cells, new_parcels
```

```python
import functools

import jax
import jax.numpy as jnp
from jax import lax
from jax.experimental import pallas as pl
from jax.experimental.pallas import tpu as pltpu
from jax.sharding import PartitionSpec as P

SECTIONS = 8
SPECIES = 6
COUNT = SECTIONS + SPECIES
LANES = 128
F32 = jnp.float32
BF16 = jnp.bfloat16
VMEM = pl.BlockSpec(memory_space=pltpu.VMEM)


def call(kernel, out_shape, operands, scratch=(), flops=0, moved_bytes=0, limit=24):
    return pl.pallas_call(
        kernel,
        out_shape=out_shape,
        in_specs=[VMEM] * len(operands),
        out_specs=jax.tree.map(lambda unused: VMEM, out_shape),
        scratch_shapes=list(scratch),
        compiler_params=pltpu.CompilerParams(vmem_limit_bytes=limit << 20),
        cost_estimate=pl.CostEstimate(flops=flops, bytes_accessed=moved_bytes, transcendentals=0),
    )(*operands)


def iota(shape, axis):
    return lax.broadcasted_iota(jnp.int32, shape, axis)


def lane_pick(values, index):
    return jnp.take_along_axis(values, index, axis=1, mode="promise_in_bounds")


def advance_block(block):
    diameter = block[6:7]
    warmth = block[7:8]
    velocity = block[3:6]
    factor = 0.8 / (1.0 + diameter * diameter)
    velocity_new = velocity * (1.0 - factor)
    position_new = block[0:3] + 0.5 * (velocity + velocity_new)
    diameter_new = diameter * (1.0 - 0.05 * warmth)
    warmth_new = warmth + factor * (1.0 - warmth)
    return jnp.concatenate([position_new, velocity_new, diameter_new, warmth_new], axis=0)


def advance_all(parcels_ref, advanced_ref):
    diameter = parcels_ref[6:7, :]
    warmth = parcels_ref[7:8, :]
    velocity = parcels_ref[3:6, :]
    factor = 0.8 / (1.0 + diameter * diameter)
    velocity_new = velocity * (1.0 - factor)
    advanced_ref[0:3, :] = parcels_ref[0:3, :] + 0.5 * (velocity + velocity_new)
    advanced_ref[3:6, :] = velocity_new
    advanced_ref[6:7, :] = diameter * (1.0 - 0.05 * warmth)
    advanced_ref[7:8, :] = warmth + factor * (1.0 - warmth)


def prepare_kernel(cells_ref, parcels_ref, crossing_ref, up_ref, down_ref, yup_ref, ydown_ref, advanced_ref):
    size_x, size_y, size_z = cells_ref.shape[1:]
    up_ref[: COUNT + 1] = cells_ref[: COUNT + 1, size_x - 1]
    down_ref[: COUNT + 1] = cells_ref[: COUNT + 1, 0]
    for c in range(COUNT + 1):
        source = c if c < COUNT else COUNT + 1
        yup_ref[c] = cells_ref[source, :, size_y - 1, :]
        ydown_ref[c] = cells_ref[source, :, 0, :]
    advance_all(parcels_ref, advanced_ref)
    slot_total = parcels_ref.shape[1]
    cross = crossing_ref.shape[1]
    halves_y, halves_z = size_y // 8, size_z // LANES
    for side, out_ref in ((0, up_ref), (1, down_ref)):
        for start in range(0, cross, 4 * LANES):
            blocks = range(start, min(start + 4 * LANES, cross), LANES)
            picks = []
            for first in blocks:
                slots = jnp.broadcast_to(crossing_ref[side : side + 1, first : first + LANES], (8, LANES))
                picks.append((slots // LANES, slots % LANES))

            def step(h, totals, picks=picks):
                block = advanced_ref[:, pl.ds(pl.multiple_of(h * LANES, LANES), LANES)]
                return tuple(
                    jnp.where(high == h, lane_pick(block, low), total)
                    for (high, low), total in zip(picks, totals)
                )

            totals = lax.fori_loop(
                0, slot_total // LANES, step, tuple(jnp.zeros((8, LANES), F32) for unused in picks), unroll=8
            )
            for first, total in zip(blocks, totals):
                at = first // LANES
                layer, rest = divmod(at, halves_y * halves_z)
                half_y, half_z = divmod(rest, halves_z)
                out_ref[
                    COUNT + 1 + layer, 8 * half_y : 8 * half_y + 8, LANES * half_z : LANES * (half_z + 1)
                ] = total


def prepare(cells, parcels, crossing):
    size_x, size_y, size_z = cells.shape[1:]
    layers = COUNT + 1 + 8 * crossing.shape[1] // (size_y * size_z)
    face = jax.ShapeDtypeStruct((layers, size_y, size_z), F32)
    side = jax.ShapeDtypeStruct((COUNT + 1, size_x, size_z), F32)
    advanced = jax.ShapeDtypeStruct(parcels.shape, F32)
    return call(
        prepare_kernel, (face, face, side, side, advanced), (cells, parcels, crossing),
        moved_bytes=6 << 20,
    )


def inverse_kernel(crossing_ref, high_ref, low_ref, hot_ref, value_ref):
    sides, cross = crossing_ref.shape
    uppers = high_ref.shape[0]
    for side in range(sides):
        for first in range(0, cross, LANES):
            row = side * cross + first
            slots = crossing_ref[side : side + 1, first : first + LANES]
            upper = jnp.broadcast_to(slots // LANES, (uppers, LANES))
            lower = jnp.broadcast_to(slots % LANES, (LANES, LANES))
            at = pl.ds(row, LANES)
            block = row // LANES + 1
            hit = upper == iota((uppers, LANES), 0)
            value_ref[:uppers, at] = jnp.where(hit, float(block), 0.0).astype(BF16)
            value_ref[uppers:, at] = jnp.where(hit, iota((uppers, LANES), 1).astype(F32), 0.0).astype(BF16)
            hot_ref[:, at] = jnp.where(lower == iota((LANES, LANES), 0), 1.0, 0.0).astype(BF16)
    found = lax.dot_general(
        value_ref[...], hot_ref[...], (((1,), (1,)), ((), ())), preferred_element_type=F32
    ).astype(jnp.int32)
    high_ref[...] = found[:uppers]
    low_ref[...] = found[uppers:]


def inverse_map(crossing, slot_total):
    uppers = slot_total // LANES
    rows = crossing.size
    table = jax.ShapeDtypeStruct((uppers, LANES), jnp.int32)
    return call(
        inverse_kernel, (table, table), (crossing,),
        scratch=(pltpu.VMEM((LANES, rows), BF16), pltpu.VMEM((2 * uppers, rows), BF16)),
        flops=4 * uppers * LANES * rows, moved_bytes=1 << 20,
    )


def arrive_kernel(advanced_ref, high_ref, low_ref, before_ref, after_ref, out_ref):
    slot_total = advanced_ref.shape[1]
    size_y, size_z = before_ref.shape[1:]
    halves_y, halves_z = size_y // 8, size_z // LANES
    blocks = []
    for ref in (before_ref, after_ref):
        for layer in range(COUNT + 1, ref.shape[0]):
            for half_y in range(halves_y):
                for half_z in range(halves_z):
                    blocks.append(
                        (ref, layer, slice(8 * half_y, 8 * half_y + 8), slice(LANES * half_z, LANES * (half_z + 1)))
                    )

    def step(h, unused):
        at = pl.ds(pl.multiple_of(h * LANES, LANES), LANES)
        high = jnp.broadcast_to(high_ref[pl.ds(h, 1), :], (8, LANES))
        low = jnp.broadcast_to(low_ref[pl.ds(h, 1), :], (8, LANES))
        total = advanced_ref[:, at]
        for number, (ref, layer, rows, lanes) in enumerate(blocks):
            total = jnp.where(high == number + 1, lane_pick(ref[layer, rows, lanes], low), total)
        out_ref[:, at] = total
        return unused

    lax.fori_loop(0, slot_total // LANES, step, 0, unroll=4)


def arrive(advanced, high, low, before, after):
    return call(
        arrive_kernel, jax.ShapeDtypeStruct(advanced.shape, F32), (advanced, high, low, before, after),
        moved_bytes=4 << 20,
    )


def bucket_kernel(owner_total, capacity, mass_ref, owner_ref, cell_ref, out_ref, hot_ref, value_ref):
    blocks = owner_ref.shape[0]
    rows_out = out_ref.shape[0] // 9
    strict = iota((LANES, 2 * LANES), 0) < iota((LANES, 2 * LANES), 1)
    strict = jnp.where(strict, 1.0, 0.0).astype(BF16)
    owners = owner_ref[...]
    hots = [
        jnp.where(jnp.broadcast_to(owners[b : b + 1], (owner_total, LANES)) == iota((owner_total, LANES), 0), 1.0, 0.0)
        for b in range(blocks)
    ]
    ranks = lax.dot_general(
        jnp.concatenate(hots, axis=0).astype(BF16), strict, (((1,), (0,)), ((), ())), preferred_element_type=F32
    )
    carry = jnp.zeros((owner_total, LANES), F32)
    for b in range(blocks):
        part = ranks[b * owner_total : (b + 1) * owner_total]
        rank = jnp.sum(hots[b] * (part[:, :LANES] + carry), axis=0, keepdims=True).astype(jnp.int32)
        carry = carry + part[:, LANES:]
        spot = owners[b : b + 1] * capacity + rank
        upper = jnp.broadcast_to(spot // LANES, (rows_out, LANES))
        lower = jnp.broadcast_to(spot % LANES, (LANES, LANES))
        at = slice(b * LANES, (b + 1) * LANES)
        hit = upper == iota((rows_out, LANES), 0)
        value_ref[:rows_out, at] = jnp.where(hit, float(b + 1), 0.0).astype(BF16)
        value_ref[rows_out:, at] = jnp.where(hit, iota((rows_out, LANES), 1).astype(F32), 0.0).astype(BF16)
        hot_ref[:, at] = jnp.where(lower == iota((LANES, LANES), 0), 1.0, 0.0).astype(BF16)
    found = lax.dot_general(
        value_ref[...], hot_ref[...], (((1,), (1,)), ((), ())), preferred_element_type=F32
    ).astype(jnp.int32)
    cells = cell_ref[...].astype(F32)
    for group in range(0, rows_out, 8):
        high = found[group : group + 8]
        low = found[rows_out + group : rows_out + group + 8]
        total = jnp.zeros((8, LANES), F32)
        for b in range(blocks):
            total = jnp.where(high == b + 1, lane_pick(jnp.broadcast_to(cells[b : b + 1], (8, LANES)), low), total)
        for i in range(8):
            row = group + i
            row_high = jnp.broadcast_to(high[i : i + 1], (8, LANES))
            row_low = jnp.broadcast_to(low[i : i + 1], (8, LANES))
            mass = jnp.zeros((8, LANES), F32)
            for b in range(blocks):
                mass = jnp.where(row_high == b + 1, lane_pick(mass_ref[:, b * LANES : (b + 1) * LANES], row_low), mass)
            out_ref[9 * row : 9 * row + 8, :] = mass
            out_ref[9 * row + 8 : 9 * row + 9, :] = total[i : i + 1]


def bucket(mass, owner, cell, owner_total, capacity):
    rows = mass.shape[1]
    rows_out = owner_total * capacity // LANES
    return call(
        functools.partial(bucket_kernel, owner_total, capacity),
        jax.ShapeDtypeStruct((9 * rows_out, LANES), F32),
        (mass, owner.reshape(-1, LANES), cell.reshape(-1, LANES)),
        scratch=(pltpu.VMEM((LANES, rows), BF16), pltpu.VMEM((2 * rows_out, rows), BF16)),
        moved_bytes=1 << 20,
    )


def shift_up(value, axis):
    return pltpu.roll(value, value.shape[axis] - 1, axis)


def shift_down(value, axis):
    return pltpu.roll(value, 1, axis)


def slab_update(left, center, right, side_low, side_high, rate_ref, write):
    course = center(COUNT)
    size_y, size_z = course.shape
    first_row = iota((size_y, size_z), 0) == 0
    last_row = iota((size_y, size_z), 0) == size_y - 1

    def row_up(value, edge):
        return jnp.where(last_row, edge, shift_up(value, 0))

    def row_down(value, edge):
        return jnp.where(first_row, edge, shift_down(value, 0))

    face_x = 0.5 * (course + right(COUNT))
    face_x_low = 0.5 * (left(COUNT) + course)
    course_y = center(COUNT + 1)
    face_y = 0.5 * (course_y + row_up(course_y, side_high(COUNT)))
    face_y_low = 0.5 * (row_down(course_y, side_low(COUNT)) + course_y)
    course_z = center(COUNT + 2)
    lane = iota((size_y, size_z), 1)
    face_z = jnp.where(lane == size_z - 1, 0.0, 0.5 * (course_z + shift_up(course_z, 1)))
    face_z_low = jnp.where(lane == 0, 0.0, 0.5 * (shift_down(course_z, 1) + course_z))
    from_x_up, from_x_low = jnp.minimum(face_x, 0.0), jnp.maximum(face_x_low, 0.0)
    from_y_up, from_y_low = jnp.minimum(face_y, 0.0), jnp.maximum(face_y_low, 0.0)
    from_z_up, from_z_low = jnp.minimum(face_z, 0.0), jnp.maximum(face_z_low, 0.0)
    own = 1.0 - (
        (jnp.maximum(face_x, 0.0) - jnp.minimum(face_x_low, 0.0))
        + (jnp.maximum(face_y, 0.0) - jnp.minimum(face_y_low, 0.0))
        + (jnp.maximum(face_z, 0.0) - jnp.minimum(face_z_low, 0.0))
    )

    def moved(c):
        amount = center(c)
        total = own * amount
        total = total - from_x_up * right(c) + from_x_low * left(c)
        total = total - from_y_up * row_up(amount, side_high(c)) + from_y_low * row_down(amount, side_low(c))
        return total - from_z_up * shift_up(amount, 1) + from_z_low * shift_down(amount, 1)

    vapour = moved(SECTIONS)
    beside = 1.0 + vapour
    later = None
    gained = None
    for s in reversed(range(SECTIONS)):
        section = moved(s)
        loss = rate_ref[s] * section / beside
        value = section - loss
        if later is not None:
            value = value + 0.5 * later
            gained = later if gained is None else gained + later
        write(s, value)
        later = loss
    write(SECTIONS, vapour + later + 0.5 * gained)
    for c in range(SECTIONS + 1, COUNT):
        write(c, moved(c))


def inner_kernel(cells_ref, low_ref, high_ref, rate_ref, out_ref):
    size_x = cells_ref.shape[1]

    def layer(x, unused):
        def write(c, value):
            out_ref[c, x] = value

        slab_update(
            lambda c: cells_ref[c, x - 1],
            lambda c: cells_ref[c, x],
            lambda c: cells_ref[c, x + 1],
            lambda c: low_ref[c, pl.ds(x, 1), :],
            lambda c: high_ref[c, pl.ds(x, 1), :],
            rate_ref,
            write,
        )
        return unused

    lax.fori_loop(1, size_x - 1, layer, 0)


SMEM = pl.BlockSpec(memory_space=pltpu.SMEM)


def inner(cells, low, high, rate):
    return pl.pallas_call(
        inner_kernel,
        out_shape=jax.ShapeDtypeStruct((COUNT,) + cells.shape[1:], F32),
        in_specs=[VMEM, VMEM, VMEM, SMEM],
        out_specs=VMEM,
        compiler_params=pltpu.CompilerParams(vmem_limit_bytes=24 << 20),
        cost_estimate=pl.CostEstimate(flops=20 << 20, bytes_accessed=4 << 20, transcendentals=0),
    )(cells, low, high, rate)


def final_kernel(cells_ref, inner_ref, before_ref, after_ref, low_ref, high_ref, routed_ref, rate_ref, out_ref, depth_ref, spread_ref):
    size_x, size_y, size_z = cells_ref.shape[1:]
    groups = routed_ref.shape[0] // 9
    cell_rows = jnp.concatenate([routed_ref[9 * g + 8 : 9 * g + 9, :] for g in range(groups)], axis=0).astype(jnp.int32)
    depth = (cell_rows % size_z).T
    for g in range(groups):
        column = jnp.broadcast_to(depth[:, g : g + 1], (LANES, size_z))
        depth_ref[g * LANES : (g + 1) * LANES, :] = jnp.where(
            column == iota((LANES, size_z), 1), 1.0, 0.0
        ).astype(BF16)

    edge = {
        0: lambda: slab_update(
            lambda c: before_ref[c],
            lambda c: cells_ref[c, 0],
            lambda c: cells_ref[c, 1],
            lambda c: low_ref[c, 0:1, :],
            lambda c: high_ref[c, 0:1, :],
            rate_ref,
            functools.partial(put, out_ref, 0),
        ),
        size_x - 1: lambda: slab_update(
            lambda c: cells_ref[c, size_x - 2],
            lambda c: cells_ref[c, size_x - 1],
            lambda c: after_ref[c],
            lambda c: low_ref[c, size_x - 1 : size_x, :],
            lambda c: high_ref[c, size_x - 1 : size_x, :],
            rate_ref,
            functools.partial(put, out_ref, size_x - 1),
        ),
    }
    half = SECTIONS * size_y
    for x in range(size_x):
        for g in range(groups):
            at = slice(g * LANES, (g + 1) * LANES)
            plane = jnp.broadcast_to(cell_rows[g : g + 1] // size_z, (size_y, LANES))
            hit = plane == x * size_y + iota((size_y, LANES), 0)
            for s in range(SECTIONS):
                mass = routed_ref[9 * g + s : 9 * g + s + 1, :]
                coarse = mass.astype(BF16)
                fine = (mass - coarse.astype(F32)).astype(BF16)
                spread_ref[s * size_y : (s + 1) * size_y, at] = jnp.where(
                    hit, jnp.broadcast_to(coarse.astype(F32), hit.shape), 0.0
                ).astype(BF16)
                spread_ref[half + s * size_y : half + (s + 1) * size_y, at] = jnp.where(
                    hit, jnp.broadcast_to(fine.astype(F32), hit.shape), 0.0
                ).astype(BF16)
        added = jnp.dot(spread_ref[...], depth_ref[...], preferred_element_type=F32)
        if x in edge:
            edge[x]()
            base = out_ref
        else:
            base = inner_ref
            out_ref[SECTIONS:, x] = inner_ref[SECTIONS:, x]
        for s in range(SECTIONS):
            low, high = s * size_y, (s + 1) * size_y
            out_ref[s, x] = base[s, x] + (added[low:high] + added[half + low : half + high])


def put(ref, x, c, value):
    ref[c, x] = value


def final(cells, inner_cells, before, after, low, high, routed, rate):
    size_x, size_y, size_z = cells.shape[1:]
    rows = routed.shape[0] // 9 * LANES
    return pl.pallas_call(
        final_kernel,
        out_shape=jax.ShapeDtypeStruct(inner_cells.shape, F32),
        in_specs=[VMEM] * 7 + [SMEM],
        out_specs=VMEM,
        scratch_shapes=[pltpu.VMEM((rows, size_z), BF16), pltpu.VMEM((2 * SECTIONS * size_y, rows), BF16)],
        compiler_params=pltpu.CompilerParams(vmem_limit_bytes=32 << 20),
        cost_estimate=pl.CostEstimate(flops=4 << 30, bytes_accessed=6 << 20, transcendentals=0),
    )(cells, inner_cells, before, after, low, high, routed, rate)


def ring(size):
    up = [(i, (i + 1) % size) for i in range(size)]
    return up, [(j, i) for i, j in up]


def on_device(cell_state, evap_rate, parcels, crossing, conv_mass, conv_owner, conv_cell):
    owner_total = lax.axis_size("gx") * lax.axis_size("gy")
    row_total = conv_owner.shape[0]
    capacity = 2 * row_total // owner_total
    up_x, down_x = ring(lax.axis_size("gx"))
    up_y, down_y = ring(lax.axis_size("gy"))

    send_up, send_down, side_up, side_down, advanced = prepare(cell_state, parcels, crossing)
    before = lax.ppermute(send_up, "gx", up_x)
    after = lax.ppermute(send_down, "gx", down_x)
    low = lax.ppermute(side_up, "gy", up_y)
    high = lax.ppermute(side_down, "gy", down_y)

    filled = bucket(conv_mass, conv_owner, conv_cell, owner_total, capacity)
    fold = LANES // capacity
    filled = filled.reshape(-1, 9, fold, capacity).transpose(0, 2, 1, 3).reshape(owner_total, 1, 9 * capacity)
    routed = lax.all_to_all(filled, ("gx", "gy"), split_axis=0, concat_axis=0, tiled=True)
    routed = routed.reshape(-1, fold, 9, capacity).transpose(0, 2, 1, 3).reshape(-1, LANES)

    high_map, low_map = inverse_map(crossing, parcels.shape[1])
    inner_cells = inner(cell_state, low, high, evap_rate)
    new_parcels = arrive(advanced, high_map, low_map, before, after)
    new_cells = final(cell_state, inner_cells, before, after, low, high, routed, evap_rate)
    return (new_cells, new_parcels)


def solution(mesh):
    in_specs = (
        P(None, "gx", "gy", None),
        P(),
        P(None, ("gx", "gy")),
        P(None, ("gx", "gy")),
        P(None, ("gx", "gy")),
        P(("gx", "gy"), None),
        P(("gx", "gy")),
    )
    out_specs = (P(None, "gx", "gy", None), P(None, ("gx", "gy")))
    return jax.shard_map(
        on_device, mesh=mesh, in_specs=in_specs, out_specs=out_specs, check_vma=False
    )
```

```python
import functools

import jax
import jax.numpy as jnp
from jax import lax
from jax.experimental import pallas as pl
from jax.experimental.pallas import tpu as pltpu
from jax.sharding import PartitionSpec as P

SECTIONS = 8
SPECIES = 6
COUNT = SECTIONS + SPECIES
LANES = 128
F32 = jnp.float32
BF16 = jnp.bfloat16
VMEM = pl.BlockSpec(memory_space=pltpu.VMEM)


def call(kernel, out_shape, operands, scratch=(), flops=0, moved_bytes=0, limit=24):
    return pl.pallas_call(
        kernel,
        out_shape=out_shape,
        in_specs=[VMEM] * len(operands),
        out_specs=jax.tree.map(lambda unused: VMEM, out_shape),
        scratch_shapes=list(scratch),
        compiler_params=pltpu.CompilerParams(vmem_limit_bytes=limit << 20),
        cost_estimate=pl.CostEstimate(flops=flops, bytes_accessed=moved_bytes, transcendentals=0),
    )(*operands)


def iota(shape, axis):
    return lax.broadcasted_iota(jnp.int32, shape, axis)


def lane_pick(values, index):
    return jnp.take_along_axis(values, index, axis=1, mode="promise_in_bounds")


def split(value):
    coarse = value.astype(BF16)
    return coarse, (value - coarse.astype(F32)).astype(BF16)


def advance_block(block):
    row = iota(block.shape, 0)
    diameter = jnp.broadcast_to(block[6:7], block.shape)
    warmth = jnp.broadcast_to(block[7:8], block.shape)
    factor = 0.8 / (1.0 + diameter * diameter)
    slowed = block * (1.0 - factor)
    travel = pltpu.roll(0.5 * (block + slowed), 5, 0)
    shrunk = block * (1.0 - 0.05 * warmth)
    warmed = block + factor * (1.0 - block)
    return jnp.where(row < 3, block + travel, jnp.where(row < 6, slowed, jnp.where(row == 6, shrunk, warmed)))


def prepare_kernel(
    cells_hbm, parcels_hbm, crossing_hbm, mass_hbm, owner_hbm, cell_hbm,
    up_ref, down_ref, yup_ref, ydown_ref, cells_ref, advanced_ref, crossing_ref, mass_ref, owner_ref, cell_ref,
    parcels_ref, parts_ref, hot_ref, sems,
):
    size_x, size_y, size_z = cells_ref.shape[1:]
    face = slice(0, COUNT + 1)
    copies = [
        pltpu.make_async_copy(source, target, sems.at[i])
        for i, (source, target) in enumerate(
            (
                (crossing_hbm, crossing_ref),
                (parcels_hbm, parcels_ref),
                (cells_hbm, cells_ref),
                (cells_hbm.at[face, size_x - 1], up_ref.at[face]),
                (cells_hbm.at[face, 0], down_ref.at[face]),
                (mass_hbm, mass_ref),
                (owner_hbm, owner_ref),
                (cell_hbm, cell_ref),
            )
        )
    ]
    for copy in copies:
        copy.start()
    cross = crossing_ref.shape[1]
    slot_total = parcels_ref.shape[1]
    copies[0].wait()
    for side in range(2):
        for first in range(0, cross, LANES):
            lower = jnp.broadcast_to(crossing_ref[side : side + 1, first : first + LANES] % LANES, (LANES, LANES))
            hot = jnp.where(lower == iota((LANES, LANES), 0), 1.0, 0.0).astype(BF16)
            at = slice(side * cross + first, side * cross + first + LANES)
            hot_ref[:LANES, at] = hot
            hot_ref[LANES:, at] = hot
    copies[1].wait()

    def advance_pair(i, unused):
        first = pl.multiple_of(i * 2 * LANES, 2 * LANES)
        blocks = []
        for offset in (0, LANES):
            at = pl.ds(pl.multiple_of(first + offset, LANES), LANES)
            block = advance_block(parcels_ref[:, at])
            advanced_ref[:, at] = block
            blocks.append(block)
        coarse, fine = split(jnp.concatenate(blocks, axis=0))
        rows = pl.ds(pl.multiple_of(i * 16, 16), 16)
        parts_ref[rows, :LANES] = coarse
        parts_ref[rows, LANES:] = fine
        return unused

    lax.fori_loop(0, slot_total // (2 * LANES), advance_pair, 0, unroll=8)

    halves_y, halves_z = size_y // 8, size_z // LANES
    width = 2 * LANES
    part_rows = parts_ref.shape[0]
    step_rows = min(256, part_rows)
    for side, out_ref in ((0, up_ref), (1, down_ref)):
        for first in range(0, cross, width):
            upper = jnp.broadcast_to(crossing_ref[side : side + 1, first : first + width] // LANES, (8, width))
            total = jnp.zeros((8, width), F32)
            at = slice(side * cross + first, side * cross + first + width)
            for rows in range(0, part_rows, step_rows):
                picked = jnp.dot(parts_ref[rows : rows + step_rows], hot_ref[:, at], preferred_element_type=F32)
                for i in range(0, step_rows, 8):
                    total = jnp.where(upper == (rows + i) // 8, picked[i : i + 8], total)
            for offset in range(0, width, LANES):
                layer, rest = divmod((first + offset) // LANES, halves_y * halves_z)
                half_y, half_z = divmod(rest, halves_z)
                out_ref[
                    COUNT + 1 + layer, 8 * half_y : 8 * half_y + 8, LANES * half_z : LANES * (half_z + 1)
                ] = total[:, offset : offset + LANES]

    copies[2].wait()
    for c in range(COUNT + 1):
        source = c if c < COUNT else COUNT + 1
        yup_ref[c] = cells_ref[source, :, size_y - 1, :]
        ydown_ref[c] = cells_ref[source, :, 0, :]
    for copy in copies[3:]:
        copy.wait()


HBM = pl.BlockSpec(memory_space=pltpu.HBM)


def prepare(cells, parcels, crossing, mass, owner, cell):
    size_x, size_y, size_z = cells.shape[1:]
    layers = COUNT + 1 + 8 * crossing.shape[1] // (size_y * size_z)
    face = jax.ShapeDtypeStruct((layers, size_y, size_z), F32)
    side = jax.ShapeDtypeStruct((COUNT + 1, size_x, size_z), F32)
    kept = [jax.ShapeDtypeStruct(a.shape, a.dtype) for a in (cells, parcels, crossing, mass, owner, cell)]
    return pl.pallas_call(
        prepare_kernel,
        out_shape=[face, face, side, side] + kept,
        in_specs=[HBM] * 6,
        out_specs=[VMEM] * 10,
        scratch_shapes=[
            pltpu.VMEM(parcels.shape, F32),
            pltpu.VMEM((8 * parcels.shape[1] // LANES, 2 * LANES), BF16),
            pltpu.VMEM((2 * LANES, crossing.size), BF16),
            pltpu.SemaphoreType.DMA((8,)),
        ],
        compiler_params=pltpu.CompilerParams(vmem_limit_bytes=24 << 20),
        cost_estimate=pl.CostEstimate(flops=1 << 30, bytes_accessed=6 << 20, transcendentals=0),
    )(cells, parcels, crossing, mass, owner, cell)


def inverse_kernel(crossing_ref, high_ref, low_ref, hot_ref, value_ref):
    sides, cross = crossing_ref.shape
    uppers = high_ref.shape[0]
    for side in range(sides):
        for first in range(0, cross, LANES):
            row = side * cross + first
            slots = crossing_ref[side : side + 1, first : first + LANES]
            upper = jnp.broadcast_to(slots // LANES, (uppers, LANES))
            lower = jnp.broadcast_to(slots % LANES, (LANES, LANES))
            at = pl.ds(row, LANES)
            block = row // LANES + 1
            hit = upper == iota((uppers, LANES), 0)
            value_ref[:uppers, at] = jnp.where(hit, float(block), 0.0).astype(BF16)
            value_ref[uppers:, at] = jnp.where(hit, iota((uppers, LANES), 1).astype(F32), 0.0).astype(BF16)
            hot_ref[:, at] = jnp.where(lower == iota((LANES, LANES), 0), 1.0, 0.0).astype(BF16)
    found = lax.dot_general(
        value_ref[...], hot_ref[...], (((1,), (1,)), ((), ())), preferred_element_type=F32
    ).astype(jnp.int32)
    high_ref[...] = found[:uppers]
    low_ref[...] = found[uppers:]


def inverse_map(crossing, slot_total):
    uppers = slot_total // LANES
    rows = crossing.size
    table = jax.ShapeDtypeStruct((uppers, LANES), jnp.int32)
    return call(
        inverse_kernel, (table, table), (crossing,),
        scratch=(pltpu.VMEM((LANES, rows), BF16), pltpu.VMEM((2 * uppers, rows), BF16)),
        flops=4 * uppers * LANES * rows, moved_bytes=1 << 20,
    )


def arrive_kernel(advanced_ref, high_ref, low_ref, before_ref, after_ref, out_ref, parts_ref):
    slot_total = advanced_ref.shape[1]
    size_y, size_z = before_ref.shape[1:]
    halves_y, halves_z = size_y // 8, size_z // LANES
    blocks = [
        ref[layer, 8 * half_y : 8 * half_y + 8, LANES * half_z : LANES * (half_z + 1)]
        for ref in (before_ref, after_ref)
        for layer in range(COUNT + 1, before_ref.shape[0])
        for half_y in range(halves_y)
        for half_z in range(halves_z)
    ]
    for i in range(0, len(blocks), 2):
        coarse, fine = split(jnp.concatenate(blocks[i : i + 2], axis=0))
        parts_ref[8 * i : 8 * i + 16, :LANES] = coarse
        parts_ref[8 * i : 8 * i + 16, LANES:] = fine
    width = 2 * LANES

    def step(i, unused):
        at = pl.ds(pl.multiple_of(i * width, width), width)
        high = jnp.concatenate([high_ref[pl.ds(2 * i, 1), :], high_ref[pl.ds(2 * i + 1, 1), :]], axis=1)
        low = jnp.concatenate([low_ref[pl.ds(2 * i, 1), :], low_ref[pl.ds(2 * i + 1, 1), :]], axis=1)
        hot = jnp.where(jnp.broadcast_to(low, (LANES, width)) == iota((LANES, width), 0), 1.0, 0.0).astype(BF16)
        picked = jnp.dot(parts_ref[...], jnp.concatenate([hot, hot], axis=0), preferred_element_type=F32)
        high = jnp.broadcast_to(high, (8, width))
        total = advanced_ref[:, at]
        for number in range(len(blocks)):
            total = jnp.where(high == number + 1, picked[8 * number : 8 * number + 8], total)
        out_ref[:, at] = total
        return unused

    lax.fori_loop(0, slot_total // width, step, 0, unroll=4)


def arrive(advanced, high, low, before, after):
    return call(
        arrive_kernel, jax.ShapeDtypeStruct(advanced.shape, F32), (advanced, high, low, before, after),
        scratch=(pltpu.VMEM((8 * 2 * (before.shape[0] - COUNT - 1) * before.shape[1] * before.shape[2] // (8 * LANES), 2 * LANES), BF16),),
        moved_bytes=4 << 20,
    )


def bucket_kernel(owner_total, capacity, mass_ref, owner_ref, cell_ref, out_ref, hot_ref, value_ref):
    blocks = owner_ref.shape[0]
    rows_out = out_ref.shape[0] // 9
    strict = iota((LANES, 2 * LANES), 0) < iota((LANES, 2 * LANES), 1)
    strict = jnp.where(strict, 1.0, 0.0).astype(BF16)
    owners = owner_ref[...]
    hots = [
        jnp.where(jnp.broadcast_to(owners[b : b + 1], (owner_total, LANES)) == iota((owner_total, LANES), 0), 1.0, 0.0)
        for b in range(blocks)
    ]
    ranks = lax.dot_general(
        jnp.concatenate(hots, axis=0).astype(BF16), strict, (((1,), (0,)), ((), ())), preferred_element_type=F32
    )
    carry = jnp.zeros((owner_total, LANES), F32)
    for b in range(blocks):
        part = ranks[b * owner_total : (b + 1) * owner_total]
        rank = jnp.sum(hots[b] * (part[:, :LANES] + carry), axis=0, keepdims=True).astype(jnp.int32)
        carry = carry + part[:, LANES:]
        spot = owners[b : b + 1] * capacity + rank
        upper = jnp.broadcast_to(spot // LANES, (rows_out, LANES))
        lower = jnp.broadcast_to(spot % LANES, (LANES, LANES))
        at = slice(b * LANES, (b + 1) * LANES)
        hit = upper == iota((rows_out, LANES), 0)
        value_ref[:rows_out, at] = jnp.where(hit, float(b + 1), 0.0).astype(BF16)
        value_ref[rows_out:, at] = jnp.where(hit, iota((rows_out, LANES), 1).astype(F32), 0.0).astype(BF16)
        hot_ref[:, at] = jnp.where(lower == iota((LANES, LANES), 0), 1.0, 0.0).astype(BF16)
    found = lax.dot_general(
        value_ref[...], hot_ref[...], (((1,), (1,)), ((), ())), preferred_element_type=F32
    ).astype(jnp.int32)
    cells = cell_ref[...].astype(F32)
    for group in range(0, rows_out, 8):
        high = found[group : group + 8]
        low = found[rows_out + group : rows_out + group + 8]
        total = jnp.zeros((8, LANES), F32)
        for b in range(blocks):
            total = jnp.where(high == b + 1, lane_pick(jnp.broadcast_to(cells[b : b + 1], (8, LANES)), low), total)
        for i in range(8):
            row = group + i
            row_high = jnp.broadcast_to(high[i : i + 1], (8, LANES))
            row_low = jnp.broadcast_to(low[i : i + 1], (8, LANES))
            mass = jnp.zeros((8, LANES), F32)
            for b in range(blocks):
                mass = jnp.where(row_high == b + 1, lane_pick(mass_ref[:, b * LANES : (b + 1) * LANES], row_low), mass)
            out_ref[9 * row : 9 * row + 8, :] = mass
            out_ref[9 * row + 8 : 9 * row + 9, :] = total[i : i + 1]


def bucket(mass, owner, cell, owner_total, capacity):
    rows = mass.shape[1]
    rows_out = owner_total * capacity // LANES
    return call(
        functools.partial(bucket_kernel, owner_total, capacity),
        jax.ShapeDtypeStruct((9 * rows_out, LANES), F32),
        (mass, owner, cell),
        scratch=(pltpu.VMEM((LANES, rows), BF16), pltpu.VMEM((2 * rows_out, rows), BF16)),
        moved_bytes=1 << 20,
    )


def shift_up(value, axis):
    return pltpu.roll(value, value.shape[axis] - 1, axis)


def shift_down(value, axis):
    return pltpu.roll(value, 1, axis)


def slab_update(left, center, right, side_low, side_high, rate_ref, write):
    course = center(COUNT)
    size_y, size_z = course.shape
    first_row = iota((size_y, size_z), 0) == 0
    last_row = iota((size_y, size_z), 0) == size_y - 1

    def row_up(value, edge):
        return jnp.where(last_row, edge, shift_up(value, 0))

    def row_down(value, edge):
        return jnp.where(first_row, edge, shift_down(value, 0))

    face_x = 0.5 * (course + right(COUNT))
    face_x_low = 0.5 * (left(COUNT) + course)
    course_y = center(COUNT + 1)
    face_y = 0.5 * (course_y + row_up(course_y, side_high(COUNT)))
    face_y_low = 0.5 * (row_down(course_y, side_low(COUNT)) + course_y)
    course_z = center(COUNT + 2)
    lane = iota((size_y, size_z), 1)
    face_z = jnp.where(lane == size_z - 1, 0.0, 0.5 * (course_z + shift_up(course_z, 1)))
    face_z_low = jnp.where(lane == 0, 0.0, 0.5 * (shift_down(course_z, 1) + course_z))
    from_x_up, from_x_low = jnp.minimum(face_x, 0.0), jnp.maximum(face_x_low, 0.0)
    from_y_up, from_y_low = jnp.minimum(face_y, 0.0), jnp.maximum(face_y_low, 0.0)
    from_z_up, from_z_low = jnp.minimum(face_z, 0.0), jnp.maximum(face_z_low, 0.0)
    own = 1.0 - (
        (jnp.maximum(face_x, 0.0) - jnp.minimum(face_x_low, 0.0))
        + (jnp.maximum(face_y, 0.0) - jnp.minimum(face_y_low, 0.0))
        + (jnp.maximum(face_z, 0.0) - jnp.minimum(face_z_low, 0.0))
    )

    def moved(c):
        amount = center(c)
        total = own * amount
        total = total - from_x_up * right(c) + from_x_low * left(c)
        total = total - from_y_up * row_up(amount, side_high(c)) + from_y_low * row_down(amount, side_low(c))
        return total - from_z_up * shift_up(amount, 1) + from_z_low * shift_down(amount, 1)

    vapour = moved(SECTIONS)
    beside = 1.0 + vapour
    later = None
    gained = None
    for s in reversed(range(SECTIONS)):
        section = moved(s)
        loss = rate_ref[s] * section / beside
        value = section - loss
        if later is not None:
            value = value + 0.5 * later
            gained = later if gained is None else gained + later
        write(s, value)
        later = loss
    write(SECTIONS, vapour + later + 0.5 * gained)
    for c in range(SECTIONS + 1, COUNT):
        write(c, moved(c))


def inner_kernel(cells_ref, low_ref, high_ref, rate_ref, out_ref):
    size_x = cells_ref.shape[1]

    def layer(x, unused):
        def write(c, value):
            out_ref[c, x] = value

        slab_update(
            lambda c: cells_ref[c, x - 1],
            lambda c: cells_ref[c, x],
            lambda c: cells_ref[c, x + 1],
            lambda c: low_ref[c, pl.ds(x, 1), :],
            lambda c: high_ref[c, pl.ds(x, 1), :],
            rate_ref,
            write,
        )
        return unused

    lax.fori_loop(1, size_x - 1, layer, 0)


SMEM = pl.BlockSpec(memory_space=pltpu.SMEM)


def inner(cells, low, high, rate):
    return pl.pallas_call(
        inner_kernel,
        out_shape=jax.ShapeDtypeStruct((COUNT,) + cells.shape[1:], F32),
        in_specs=[VMEM, VMEM, VMEM, SMEM],
        out_specs=VMEM,
        compiler_params=pltpu.CompilerParams(vmem_limit_bytes=24 << 20),
        cost_estimate=pl.CostEstimate(flops=20 << 20, bytes_accessed=4 << 20, transcendentals=0),
    )(cells, low, high, rate)


def final_kernel(cells_ref, inner_ref, before_ref, after_ref, low_ref, high_ref, routed_ref, rate_ref, out_ref, depth_ref, spread_ref, mass_ref, plane_ref):
    size_x, size_y, size_z = cells_ref.shape[1:]
    groups = routed_ref.shape[0] // 9
    cell_rows = jnp.concatenate([routed_ref[9 * g + 8 : 9 * g + 9, :] for g in range(groups)], axis=0).astype(jnp.int32)
    depth = (cell_rows % size_z).T
    for g in range(groups):
        column = jnp.broadcast_to(depth[:, g : g + 1], (LANES, size_z))
        depth_ref[g * LANES : (g + 1) * LANES, :] = jnp.where(
            column == iota((LANES, size_z), 1), 1.0, 0.0
        ).astype(BF16)

    edge = {
        0: lambda: slab_update(
            lambda c: before_ref[c],
            lambda c: cells_ref[c, 0],
            lambda c: cells_ref[c, 1],
            lambda c: low_ref[c, 0:1, :],
            lambda c: high_ref[c, 0:1, :],
            rate_ref,
            functools.partial(put, out_ref, 0),
        ),
        size_x - 1: lambda: slab_update(
            lambda c: cells_ref[c, size_x - 2],
            lambda c: cells_ref[c, size_x - 1],
            lambda c: after_ref[c],
            lambda c: low_ref[c, size_x - 1 : size_x, :],
            lambda c: high_ref[c, size_x - 1 : size_x, :],
            rate_ref,
            functools.partial(put, out_ref, size_x - 1),
        ),
    }
    half = SECTIONS * size_y
    planes = (cell_rows // size_z).astype(F32)
    for g in range(groups):
        at = slice(g * LANES, (g + 1) * LANES)
        plane_ref[:, at] = jnp.broadcast_to(planes[g : g + 1], (size_y, LANES)).astype(BF16)
        for s in range(SECTIONS):
            coarse, fine = split(routed_ref[9 * g + s : 9 * g + s + 1, :])
            mass_ref[s * size_y : (s + 1) * size_y, at] = jnp.broadcast_to(coarse.astype(F32), (size_y, LANES)).astype(BF16)
            mass_ref[half + s * size_y : half + (s + 1) * size_y, at] = jnp.broadcast_to(
                fine.astype(F32), (size_y, LANES)
            ).astype(BF16)
    zero = jnp.zeros((size_y, LANES), BF16)
    for x in range(size_x):
        rows_y = (iota((size_y, LANES), 0) + x * size_y).astype(F32).astype(BF16)
        for g in range(groups):
            at = slice(g * LANES, (g + 1) * LANES)
            hit = plane_ref[:, at] == rows_y
            for s in range(2 * SECTIONS):
                rows = slice(s * size_y, (s + 1) * size_y)
                spread_ref[rows, at] = jnp.where(hit, mass_ref[rows, at], zero)
        added = jnp.dot(spread_ref[...], depth_ref[...], preferred_element_type=F32)
        if x in edge:
            edge[x]()
            base = out_ref
        else:
            base = inner_ref
            out_ref[SECTIONS:, x] = inner_ref[SECTIONS:, x]
        for s in range(SECTIONS):
            low, high = s * size_y, (s + 1) * size_y
            out_ref[s, x] = base[s, x] + (added[low:high] + added[half + low : half + high])


def put(ref, x, c, value):
    ref[c, x] = value


def final(cells, inner_cells, before, after, low, high, routed, rate):
    size_x, size_y, size_z = cells.shape[1:]
    rows = routed.shape[0] // 9 * LANES
    return pl.pallas_call(
        final_kernel,
        out_shape=jax.ShapeDtypeStruct(inner_cells.shape, F32),
        in_specs=[VMEM] * 7 + [SMEM],
        out_specs=VMEM,
        scratch_shapes=[
            pltpu.VMEM((rows, size_z), BF16),
            pltpu.VMEM((2 * SECTIONS * size_y, rows), BF16),
            pltpu.VMEM((2 * SECTIONS * size_y, rows), BF16),
            pltpu.VMEM((size_y, rows), BF16),
        ],
        compiler_params=pltpu.CompilerParams(vmem_limit_bytes=32 << 20),
        cost_estimate=pl.CostEstimate(flops=4 << 30, bytes_accessed=6 << 20, transcendentals=0),
    )(cells, inner_cells, before, after, low, high, routed, rate)


def ring(size):
    up = [(i, (i + 1) % size) for i in range(size)]
    return up, [(j, i) for i, j in up]


def on_device(cell_state, evap_rate, parcels, crossing, conv_mass, conv_owner, conv_cell):
    owner_total = lax.axis_size("gx") * lax.axis_size("gy")
    row_total = conv_owner.shape[0]
    capacity = 2 * row_total // owner_total
    up_x, down_x = ring(lax.axis_size("gx"))
    up_y, down_y = ring(lax.axis_size("gy"))

    send_up, send_down, side_up, side_down, cells, advanced, slots, mass, owner, cell = prepare(
        cell_state, parcels, crossing, conv_mass, conv_owner.reshape(-1, LANES), conv_cell.reshape(-1, LANES)
    )
    before = lax.ppermute(send_up, "gx", up_x)
    after = lax.ppermute(send_down, "gx", down_x)
    low = lax.ppermute(side_up, "gy", up_y)
    high = lax.ppermute(side_down, "gy", down_y)

    filled = bucket(mass, owner, cell, owner_total, capacity)
    fold = LANES // capacity
    filled = filled.reshape(-1, 9, fold, capacity).transpose(0, 2, 1, 3).reshape(owner_total, 1, 9 * capacity)
    routed = lax.all_to_all(filled, ("gx", "gy"), split_axis=0, concat_axis=0, tiled=True)
    routed = routed.reshape(-1, fold, 9, capacity).transpose(0, 2, 1, 3).reshape(-1, LANES)

    high_map, low_map = inverse_map(slots, parcels.shape[1])
    inner_cells = inner(cells, low, high, evap_rate)
    new_parcels = arrive(advanced, high_map, low_map, before, after)
    new_cells = final(cells, inner_cells, before, after, low, high, routed, evap_rate)
    return (new_cells, new_parcels)


def solution(mesh):
    in_specs = (
        P(None, "gx", "gy", None),
        P(),
        P(None, ("gx", "gy")),
        P(None, ("gx", "gy")),
        P(None, ("gx", "gy")),
        P(("gx", "gy"), None),
        P(("gx", "gy")),
    )
    out_specs = (P(None, "gx", "gy", None), P(None, ("gx", "gy")))
    return jax.shard_map(
        on_device, mesh=mesh, in_specs=in_specs, out_specs=out_specs, check_vma=False
    )
```

```python
import functools

import jax
import jax.numpy as jnp
from jax import lax
from jax.experimental import pallas as pl
from jax.experimental.pallas import tpu as pltpu
from jax.sharding import PartitionSpec as P

SECTIONS = 8
SPECIES = 6
COUNT = SECTIONS + SPECIES
LANES = 128
WIDE = 256
WINDOW = 4
F32 = jnp.float32
BF16 = jnp.bfloat16
ANY = pl.BlockSpec(memory_space=pl.ANY)
SMEM = pl.BlockSpec(memory_space=pltpu.SMEM)
ALL = 63 << 20
MOST = 40 << 20


def call(kernel, out_shape, operands, scratch, in_specs=None, aliases=None, flops=0, moved_bytes=0, grant=MOST):
    many = isinstance(out_shape, (list, tuple))
    return pl.pallas_call(
        kernel,
        out_shape=out_shape,
        in_specs=in_specs or [ANY] * len(operands),
        out_specs=[ANY] * len(out_shape) if many else ANY,
        scratch_shapes=scratch,
        input_output_aliases=aliases or {},
        compiler_params=pltpu.CompilerParams(vmem_limit_bytes=grant),
        cost_estimate=pl.CostEstimate(flops=flops, bytes_accessed=moved_bytes, transcendentals=0),
    )(*operands)


def iota(shape, axis):
    return lax.broadcasted_iota(jnp.int32, shape, axis)


def packed(value):
    return value.astype(F32).astype(BF16)


def split(value):
    coarse = value.astype(BF16)
    return coarse, (value - coarse.astype(F32)).astype(BF16)


def rows_of(row, count):
    return jnp.broadcast_to(row, (count, row.shape[1])).astype(BF16)


def hot_columns(lower, count):
    return jnp.where(rows_of(lower.astype(F32), count) == packed(iota((count, LANES), 0)), 1.0, 0.0).astype(BF16)


def contract_lanes(left, right):
    return lax.dot_general(left, right, (((1,), (1,)), ((), ())), preferred_element_type=F32)


def advance_block(block):
    row = iota(block.shape, 0)
    diameter = jnp.broadcast_to(block[6:7], block.shape)
    warmth = jnp.broadcast_to(block[7:8], block.shape)
    factor = 0.8 / (1.0 + diameter * diameter)
    slowed = block * (1.0 - factor)
    travel = pltpu.roll(0.5 * (block + slowed), 5, 0)
    shrunk = block * (1.0 - 0.05 * warmth)
    warmed = block + factor * (1.0 - block)
    return jnp.where(row < 3, block + travel, jnp.where(row < 6, slowed, jnp.where(row == 6, shrunk, warmed)))


def scatter_left(left_ref, at, upper, uppers, coarse, fine):
    upper = rows_of(upper.astype(F32), 16)
    twice_coarse = jnp.concatenate([coarse.astype(F32)] * 2, axis=0).astype(BF16)
    twice_fine = jnp.concatenate([fine.astype(F32)] * 2, axis=0).astype(BF16)
    zero = jnp.zeros((16, LANES), BF16)
    pair = iota((16, LANES), 0) // 8
    for u in range(0, uppers, 2):
        hit = upper == packed(pair + u)
        left_ref[8 * u : 8 * u + 16, at] = jnp.where(hit, twice_coarse, zero)
        left_ref[8 * (uppers + u) : 8 * (uppers + u) + 16, at] = jnp.where(hit, twice_fine, zero)


def bucket_into(owner_total, capacity, mass_ref, owner_ref, cell_ref, out_ref, left_ref, hot_ref):
    blocks = owner_ref.shape[0]
    uppers = out_ref.shape[0] // 9 // 2
    strict = iota((LANES, 2 * LANES), 0) < iota((LANES, 2 * LANES), 1)
    strict = jnp.where(strict, 1.0, 0.0).astype(BF16)
    owners = owner_ref[...]
    cells = cell_ref[...]
    hots = [
        jnp.where(jnp.broadcast_to(owners[b : b + 1], (owner_total, LANES)) == iota((owner_total, LANES), 0), 1.0, 0.0)
        for b in range(blocks)
    ]
    ranks = jnp.dot(jnp.concatenate(hots, axis=0).astype(BF16), strict, preferred_element_type=F32)
    carry = jnp.zeros((owner_total, LANES), F32)
    base = 16 * uppers
    for b in range(blocks):
        part = ranks[b * owner_total : (b + 1) * owner_total]
        rank = jnp.sum(hots[b] * (part[:, :LANES] + carry), axis=0, keepdims=True).astype(jnp.int32)
        carry = carry + part[:, LANES:]
        spot = owners[b : b + 1] * capacity + rank
        at = slice(b * LANES, (b + 1) * LANES)
        hot_ref[:, at] = hot_columns(spot % WIDE, WIDE)
        coarse, fine = split(mass_ref[:, at])
        upper = spot // WIDE
        scatter_left(left_ref, at, upper, uppers, coarse, fine)
        hit = rows_of(upper.astype(F32), uppers) == packed(iota((uppers, LANES), 0))
        zero = jnp.zeros((uppers, LANES), BF16)
        cell = cells[b : b + 1]
        left_ref[base : base + uppers, at] = jnp.where(hit, rows_of((cell // WIDE).astype(F32), uppers), zero)
        left_ref[base + uppers : base + 2 * uppers, at] = jnp.where(
            hit, rows_of((cell % WIDE).astype(F32), uppers), zero
        )
        left_ref[base + 2 * uppers : base + 3 * uppers, at] = jnp.where(hit, 1.0, 0.0).astype(BF16)
    placed = contract_lanes(left_ref[...], hot_ref[...])
    cell = placed[base : base + uppers] * float(WIDE) + placed[base + uppers : base + 2 * uppers]
    cell = jnp.where(placed[base + 2 * uppers : base + 3 * uppers] > 0.5, cell, -1.0)
    for u in range(uppers):
        mass = placed[8 * u : 8 * u + 8] + placed[8 * (uppers + u) : 8 * (uppers + u) + 8]
        for half in range(2):
            row = 9 * (2 * u + half)
            lanes = slice(half * LANES, (half + 1) * LANES)
            out_ref[row : row + 8, :] = mass[:, lanes]
            out_ref[row + 8 : row + 9, :] = cell[u : u + 1, lanes]


def prepare_kernel(
    owner_total, capacity,
    cells_hbm, parcels_hbm, crossing_hbm, mass_hbm, owner_hbm, cell_hbm,
    up_hbm, down_hbm, yup_hbm, ydown_hbm, advanced_hbm, hot_hbm, filled_hbm,
    cells_ref, parcels_ref, crossing_ref, mass_ref, owner_ref, cell_ref,
    leave_ref, yup_ref, ydown_ref, advanced_ref, hot_ref, filled_ref,
    parts_ref, left_ref, spot_ref, sems,
):
    size_x, size_y, size_z = cells_hbm.shape[1:]
    face = slice(0, COUNT + 1)
    tail = slice(COUNT + 1, up_hbm.shape[0])
    pairs = [
        (crossing_hbm, crossing_ref),
        (owner_hbm, owner_ref),
        (cell_hbm, cell_ref),
        (mass_hbm, mass_ref),
        (parcels_hbm, parcels_ref),
        (cells_hbm, cells_ref),
        (cells_hbm.at[face, size_x - 1], up_hbm.at[face]),
        (cells_hbm.at[face, 0], down_hbm.at[face]),
        (filled_ref, filled_hbm),
        (hot_ref, hot_hbm),
        (advanced_ref, advanced_hbm),
        (leave_ref.at[0], up_hbm.at[tail]),
        (leave_ref.at[1], down_hbm.at[tail]),
        (yup_ref, yup_hbm),
        (ydown_ref, ydown_hbm),
    ]
    copies = [pltpu.make_async_copy(source, target, sems.at[i]) for i, (source, target) in enumerate(pairs)]
    for copy in copies[:8]:
        copy.start()
    cross = crossing_ref.shape[1]
    slot_total = parcels_ref.shape[1]
    for copy in copies[:4]:
        copy.wait()
    for side in range(2):
        for first in range(0, cross, LANES):
            lower = crossing_ref[side : side + 1, first : first + LANES] % WIDE
            hot_ref[:, side * cross + first : side * cross + first + LANES] = hot_columns(lower, WIDE)
    copies[9].start()
    bucket_into(owner_total, capacity, mass_ref, owner_ref, cell_ref, filled_ref, left_ref, spot_ref)
    copies[8].start()
    copies[4].wait()

    def advance_pair(i, unused):
        for number in range(2):
            blocks = []
            for half in range(2):
                at = pl.ds(pl.multiple_of((4 * i + 2 * number + half) * LANES, LANES), LANES)
                block = advance_block(parcels_ref[:, at])
                advanced_ref[:, at] = block
                blocks.append(block)
            parts_ref[pl.ds(pl.multiple_of((2 * i + number) * 8, 8), 8), :] = jnp.concatenate(blocks, axis=1)
        return unused

    lax.fori_loop(0, slot_total // (4 * LANES), advance_pair, 0, unroll=4)
    copies[10].start()

    halves_y, halves_z = size_y // 8, size_z // LANES
    part_rows = parts_ref.shape[0]
    step_rows = min(256, part_rows)
    for rows in range(0, part_rows, step_rows):
        coarse, fine = split(parts_ref[rows : rows + step_rows])
        for side in range(2):
            for first in range(0, cross, WIDE):
                upper = jnp.broadcast_to(crossing_ref[side : side + 1, first : first + WIDE] // WIDE, (8, WIDE))
                hot = hot_ref[:, side * cross + first : side * cross + first + WIDE]
                picked = jnp.dot(coarse, hot, preferred_element_type=F32) + jnp.dot(
                    fine, hot, preferred_element_type=F32
                )
                spots = []
                for offset in range(0, WIDE, LANES):
                    layer, rest = divmod((first + offset) // LANES, halves_y * halves_z)
                    half_y, half_z = divmod(rest, halves_z)
                    spots.append((side, layer, slice(8 * half_y, 8 * half_y + 8), slice(LANES * half_z, LANES * (half_z + 1))))
                if rows:
                    total = jnp.concatenate([leave_ref[spot] for spot in spots], axis=1)
                else:
                    total = jnp.zeros((8, WIDE), F32)
                for i in range(0, step_rows, 8):
                    total = jnp.where(upper == (rows + i) // 8, picked[i : i + 8], total)
                for number, spot in enumerate(spots):
                    leave_ref[spot] = total[:, number * LANES : (number + 1) * LANES]
    copies[11].start()
    copies[12].start()

    copies[5].wait()
    for c in range(COUNT + 1):
        source = c if c < COUNT else COUNT + 1
        yup_ref[c] = cells_ref[source, :, size_y - 1, :]
        ydown_ref[c] = cells_ref[source, :, 0, :]
    copies[13].start()
    copies[14].start()
    for copy in copies[6:]:
        copy.wait()


def prepare(cells, parcels, crossing, mass, owner, cell, owner_total, capacity):
    size_x, size_y, size_z = cells.shape[1:]
    extra = 8 * crossing.shape[1] // (size_y * size_z)
    places = owner_total * capacity
    shape = jax.ShapeDtypeStruct
    face = shape((COUNT + 1 + extra, size_y, size_z), F32)
    side = shape((COUNT + 1, size_x, size_z), F32)
    advanced = shape(parcels.shape, F32)
    hot = shape((WIDE, crossing.size), BF16)
    filled = shape((9 * places // LANES, LANES), F32)
    operands = (cells, parcels, crossing, mass, owner, cell)
    scratch = [pltpu.VMEM(a.shape, a.dtype) for a in operands]
    scratch += [pltpu.VMEM((2, extra, size_y, size_z), F32)]
    scratch += [pltpu.VMEM(a.shape, a.dtype) for a in (side, side, advanced, hot, filled)]
    scratch += [
        pltpu.VMEM((8 * parcels.shape[1] // WIDE, WIDE), F32),
        pltpu.VMEM((19 * places // WIDE, mass.shape[1]), BF16),
        pltpu.VMEM((WIDE, mass.shape[1]), BF16),
        pltpu.SemaphoreType.DMA((15,)),
    ]
    return call(
        functools.partial(prepare_kernel, owner_total, capacity),
        [face, face, side, side, advanced, hot, filled], operands, scratch,
        flops=2 << 30, moved_bytes=6 << 20, grant=ALL,
    )


def arrive_kernel(
    advanced_hbm, hot_hbm, crossing_hbm, before_hbm, after_hbm, out_hbm,
    advanced_ref, hot_ref, crossing_ref, come_ref, out_ref, left_ref, sems,
):
    cross = crossing_ref.shape[1]
    uppers = advanced_ref.shape[1] // WIDE
    tail = slice(COUNT + 1, before_hbm.shape[0])
    pairs = [
        (crossing_hbm, crossing_ref),
        (before_hbm.at[tail], come_ref.at[0]),
        (after_hbm.at[tail], come_ref.at[1]),
        (hot_hbm, hot_ref),
        (advanced_hbm, advanced_ref),
    ]
    copies = [pltpu.make_async_copy(source, target, sems.at[i]) for i, (source, target) in enumerate(pairs)]
    for copy in copies:
        copy.start()
    for copy in copies[:3]:
        copy.wait()
    size_y, size_z = come_ref.shape[2:]
    halves_y, halves_z = size_y // 8, size_z // LANES
    for side in range(2):
        for first in range(0, cross, LANES):
            layer, rest = divmod(first // LANES, halves_y * halves_z)
            half_y, half_z = divmod(rest, halves_z)
            block = come_ref[side, layer, 8 * half_y : 8 * half_y + 8, LANES * half_z : LANES * (half_z + 1)]
            coarse, fine = split(block)
            upper = crossing_ref[side : side + 1, first : first + LANES] // WIDE
            at = slice(side * cross + first, side * cross + first + LANES)
            scatter_left(left_ref, at, upper, uppers, coarse, fine)
            hit = rows_of(upper.astype(F32), uppers) == packed(iota((uppers, LANES), 0))
            left_ref[16 * uppers :, at] = jnp.where(hit, 1.0, 0.0).astype(BF16)
    copies[3].wait()
    hit = contract_lanes(left_ref[16 * uppers :], hot_ref[...])
    copies[4].wait()
    step = min(32, uppers)
    outs = []
    for u in range(0, uppers, step):
        total = contract_lanes(left_ref[8 * u : 8 * (u + step)], hot_ref[...]) + contract_lanes(
            left_ref[8 * (uppers + u) : 8 * (uppers + u + step)], hot_ref[...]
        )
        for i in range(step):
            at = slice((u + i) * WIDE, (u + i + 1) * WIDE)
            taken = jnp.broadcast_to(hit[u + i : u + i + 1], (8, WIDE)) > 0.5
            out_ref[:, at] = jnp.where(taken, total[8 * i : 8 * i + 8], advanced_ref[:, at])
        at = slice(u * WIDE, (u + step) * WIDE)
        out = pltpu.make_async_copy(out_ref.at[:, at], out_hbm.at[:, at], sems.at[len(pairs) + len(outs)])
        out.start()
        outs.append(out)
    for out in outs:
        out.wait()


def arrive(advanced, hot, crossing, before, after):
    uppers = advanced.shape[1] // WIDE
    extra = before.shape[0] - COUNT - 1
    return call(
        arrive_kernel, jax.ShapeDtypeStruct(advanced.shape, F32), (advanced, hot, crossing, before, after),
        [
            pltpu.VMEM(advanced.shape, F32),
            pltpu.VMEM(hot.shape, BF16),
            pltpu.VMEM(crossing.shape, crossing.dtype),
            pltpu.VMEM((2, extra) + before.shape[1:], F32),
            pltpu.VMEM(advanced.shape, F32),
            pltpu.VMEM((17 * uppers, crossing.size), BF16),
            pltpu.SemaphoreType.DMA((5 + -(-uppers // 32),)),
        ],
        flops=1 << 30, moved_bytes=3 << 20,
    )


def shift_up(value, axis):
    return pltpu.roll(value, value.shape[axis] - 1, axis)


def shift_down(value, axis):
    return pltpu.roll(value, 1, axis)


def slab_update(left, center, right, side_low, side_high, rate_ref, write):
    course = center(COUNT)
    size_y, size_z = course.shape
    first_row = iota((size_y, size_z), 0) == 0
    last_row = iota((size_y, size_z), 0) == size_y - 1

    def row_up(value, edge):
        return jnp.where(last_row, edge, shift_up(value, 0))

    def row_down(value, edge):
        return jnp.where(first_row, edge, shift_down(value, 0))

    face_x = 0.5 * (course + right(COUNT))
    face_x_low = 0.5 * (left(COUNT) + course)
    course_y = center(COUNT + 1)
    face_y = 0.5 * (course_y + row_up(course_y, side_high(COUNT)))
    face_y_low = 0.5 * (row_down(course_y, side_low(COUNT)) + course_y)
    course_z = center(COUNT + 2)
    lane = iota((size_y, size_z), 1)
    face_z = jnp.where(lane == size_z - 1, 0.0, 0.5 * (course_z + shift_up(course_z, 1)))
    face_z_low = jnp.where(lane == 0, 0.0, 0.5 * (shift_down(course_z, 1) + course_z))
    from_x_up, from_x_low = jnp.minimum(face_x, 0.0), jnp.maximum(face_x_low, 0.0)
    from_y_up, from_y_low = jnp.minimum(face_y, 0.0), jnp.maximum(face_y_low, 0.0)
    from_z_up, from_z_low = jnp.minimum(face_z, 0.0), jnp.maximum(face_z_low, 0.0)
    own = 1.0 - (
        (jnp.maximum(face_x, 0.0) - jnp.minimum(face_x_low, 0.0))
        + (jnp.maximum(face_y, 0.0) - jnp.minimum(face_y_low, 0.0))
        + (jnp.maximum(face_z, 0.0) - jnp.minimum(face_z_low, 0.0))
    )

    def moved(c):
        amount = center(c)
        total = own * amount
        total = total - from_x_up * right(c) + from_x_low * left(c)
        total = total - from_y_up * row_up(amount, side_high(c)) + from_y_low * row_down(amount, side_low(c))
        return total - from_z_up * shift_up(amount, 1) + from_z_low * shift_down(amount, 1)

    vapour = moved(SECTIONS)
    beside = 1.0 + vapour
    later = None
    gained = None
    for s in reversed(range(SECTIONS)):
        section = moved(s)
        loss = rate_ref[s] * section / beside
        value = section - loss
        if later is not None:
            value = value + 0.5 * later
            gained = later if gained is None else gained + later
        write(s, value)
        later = loss
    write(SECTIONS, vapour + later + 0.5 * gained)
    for c in range(SECTIONS + 1, COUNT):
        write(c, moved(c))


def inner_kernel(cells_hbm, low_hbm, high_hbm, rate_ref, out_hbm, cells_ref, low_ref, high_ref, out_ref, sems, out_sems):
    size_x = cells_hbm.shape[1]
    sides = [
        pltpu.make_async_copy(low_hbm, low_ref, sems.at[size_x]),
        pltpu.make_async_copy(high_hbm, high_ref, sems.at[size_x + 1]),
    ]

    def fetch(x):
        return pltpu.make_async_copy(cells_hbm.at[:, x], cells_ref.at[:, x], sems.at[x])

    def store(x):
        return pltpu.make_async_copy(out_ref.at[:, x], out_hbm.at[:, x], out_sems.at[x])

    for copy in sides:
        copy.start()
    for x in range(size_x):
        fetch(x).start()
    for copy in sides:
        copy.wait()
    fetch(0).wait()
    fetch(1).wait()

    def layer(x, unused):
        fetch(x + 1).wait()

        def write(c, value):
            out_ref[c, x] = value

        slab_update(
            lambda c: cells_ref[c, x - 1],
            lambda c: cells_ref[c, x],
            lambda c: cells_ref[c, x + 1],
            lambda c: low_ref[c, pl.ds(x, 1), :],
            lambda c: high_ref[c, pl.ds(x, 1), :],
            rate_ref,
            write,
        )
        store(x).start()
        return unused

    lax.fori_loop(1, size_x - 1, layer, 0)
    for x in range(1, size_x - 1):
        store(x).wait()


def inner(cells, low, high, rate):
    size_x = cells.shape[1]
    out = jax.ShapeDtypeStruct((COUNT,) + cells.shape[1:], F32)
    return call(
        inner_kernel, out, (cells, low, high, rate),
        [pltpu.VMEM(a.shape, F32) for a in (cells, low, high, out)]
        + [pltpu.SemaphoreType.DMA((size_x + 2,)), pltpu.SemaphoreType.DMA((size_x,))],
        in_specs=[ANY, ANY, ANY, SMEM],
        flops=20 << 20, moved_bytes=4 << 20,
    )


def put(ref, x, c, value):
    ref[c, x] = value


def final_kernel(
    cells_hbm, inner_hbm, before_hbm, after_hbm, low_hbm, high_hbm, routed_hbm, rate_ref, out_hbm,
    edge_ref, before_ref, after_ref, low_ref, high_ref, routed_ref, section_ref, species_ref,
    mass_ref, place_ref, spread_ref, depth_ref, sems,
):
    size_x, size_y, size_z = cells_hbm.shape[1:]
    last = size_x - 1
    face = slice(0, COUNT + 1)
    middle = slice(1, last)
    sections = slice(0, SECTIONS)
    others = slice(SECTIONS, COUNT)
    pairs = [
        (routed_hbm, routed_ref),
        (low_hbm, low_ref),
        (high_hbm, high_ref),
        (before_hbm.at[face], before_ref),
        (after_hbm.at[face], after_ref),
        (cells_hbm.at[:, 0:2], edge_ref.at[:, 0:2]),
        (cells_hbm.at[:, last - 1 : last + 1], edge_ref.at[:, 2:4]),
        (inner_hbm.at[sections, middle], section_ref.at[:, middle]),
        (species_ref.at[:, 0], out_hbm.at[others, 0]),
        (species_ref.at[:, 1], out_hbm.at[others, last]),
        (section_ref.at[:, 0:size_x], out_hbm.at[sections]),
    ]
    copies = [pltpu.make_async_copy(source, target, sems.at[i]) for i, (source, target) in enumerate(pairs)]
    for copy in copies[:8]:
        copy.start()

    copies[0].wait()
    groups = routed_ref.shape[0] // 9
    per = groups // 8
    span = LANES // per
    lane = iota((8, LANES), 1)
    for v in range(9):
        rows = routed_ref[pl.ds(v, groups, stride=9), :]
        for q in range(per):
            total = None
            for g in range(per):
                block = rows[8 * g : 8 * g + 8]
                if g != q:
                    block = pltpu.roll(block, (span * (g - q)) % LANES, 1)
                total = block if total is None else jnp.where(lane // span == g, block, total)
            mass_ref[q, v] = total

    bounds = []
    for q in range(per):
        cell = mass_ref[q, SECTIONS].astype(jnp.int32)
        layer = cell // (size_y * size_z)
        valid = cell >= 0
        bounds.append((jnp.min(jnp.where(valid, layer, size_x)), jnp.max(jnp.where(valid, layer, -1))))

    half = SECTIONS * WINDOW * size_y
    zero = jnp.zeros((size_y, LANES), BF16)

    def spread(q, first):
        cell = mass_ref[q, SECTIONS].astype(jnp.int32)
        plane = jnp.where(cell >= 0, cell // size_z - first * size_y, -1).astype(F32)
        depth = cell % size_z
        parts = [split(mass_ref[q, s]) for s in range(SECTIONS)]
        for i in range(8):
            at = slice(i * LANES, (i + 1) * LANES)
            depth_ref[q % 2, :, at] = hot_columns(depth[i : i + 1], size_z)
            plane_rows = rows_of(plane[i : i + 1], size_y)
            rows = [[rows_of(part[i : i + 1].astype(F32), size_y) for part in pair] for pair in parts]
            for w in range(WINDOW):
                hit = plane_rows == packed(iota((size_y, LANES), 0) + w * size_y)
                for s in range(SECTIONS):
                    base = (s * WINDOW + w) * size_y
                    for part in range(2):
                        spread_ref[q % 2, part * half + base : part * half + base + size_y, at] = jnp.where(
                            hit, rows[s][part], zero
                        )

    def deposit(q, first):
        added = contract_lanes(spread_ref[q % 2], depth_ref[q % 2])
        for s in range(SECTIONS):
            base = s * WINDOW * size_y
            rows = added[base : base + WINDOW * size_y] + added[half + base : half + base + WINDOW * size_y]
            at = pl.ds(first, WINDOW)
            section_ref[s, at] = section_ref[s, at] + rows.reshape(WINDOW, size_y, size_z)

    for copy in copies[1:8]:
        copy.wait()

    def write(x, number, c, value):
        if c < SECTIONS:
            section_ref[c, x] = value
        else:
            species_ref[c - SECTIONS, number] = value

    slab_update(
        lambda c: before_ref[c], lambda c: edge_ref[c, 0], lambda c: edge_ref[c, 1],
        lambda c: low_ref[c, 0:1, :], lambda c: high_ref[c, 0:1, :],
        rate_ref, functools.partial(write, 0, 0),
    )
    slab_update(
        lambda c: edge_ref[c, 2], lambda c: edge_ref[c, 3], lambda c: after_ref[c],
        lambda c: low_ref[c, last : last + 1, :], lambda c: high_ref[c, last : last + 1, :],
        rate_ref, functools.partial(write, last, 1),
    )
    copies[8].start()
    copies[9].start()
    for q in range(per):
        first = jnp.minimum(bounds[q][0], last)
        spread(q, first)
        deposit(q, first)
    for q in range(per):
        low, high = bounds[q]

        def more(t, unused, q=q, low=low):
            first = low + t * WINDOW
            spread(q, first)
            deposit(q, first)
            return unused

        lax.fori_loop(1, (high - low + WINDOW) // WINDOW, more, 0)
    copies[10].start()
    for copy in copies[8:]:
        copy.wait()


def final(cells, inner_cells, before, after, low, high, routed, rate):
    size_x, size_y, size_z = cells.shape[1:]
    per = routed.shape[0] // 9 // 8
    return call(
        final_kernel, jax.ShapeDtypeStruct(inner_cells.shape, F32),
        (cells, inner_cells, before, after, low, high, routed, rate),
        [
            pltpu.VMEM((cells.shape[0], 4, size_y, size_z), F32),
            pltpu.VMEM((COUNT + 1, size_y, size_z), F32),
            pltpu.VMEM((COUNT + 1, size_y, size_z), F32),
            pltpu.VMEM(low.shape, F32),
            pltpu.VMEM(high.shape, F32),
            pltpu.VMEM(routed.shape, F32),
            pltpu.VMEM((SECTIONS, size_x + WINDOW - 1, size_y, size_z), F32),
            pltpu.VMEM((SPECIES, 2, size_y, size_z), F32),
            pltpu.VMEM((per, SECTIONS + 1, 8, LANES), F32),
            pltpu.VMEM((8, LANES), F32),
            pltpu.VMEM((2, 2 * SECTIONS * WINDOW * size_y, 8 * LANES), BF16),
            pltpu.VMEM((2, size_z, 8 * LANES), BF16),
            pltpu.SemaphoreType.DMA((11,)),
        ],
        in_specs=[ANY] * 7 + [SMEM], aliases={1: 0},
        flops=4 << 30, moved_bytes=6 << 20,
    )


def ring(size):
    up = [(i, (i + 1) % size) for i in range(size)]
    return up, [(j, i) for i, j in up]


def on_device(cell_state, evap_rate, parcels, crossing, conv_mass, conv_owner, conv_cell):
    owner_total = lax.axis_size("gx") * lax.axis_size("gy")
    row_total = conv_owner.shape[0]
    capacity = 2 * row_total // owner_total
    up_x, down_x = ring(lax.axis_size("gx"))
    up_y, down_y = ring(lax.axis_size("gy"))

    send_up, send_down, side_up, side_down, advanced, hot, filled = prepare(
        cell_state, parcels, crossing, conv_mass, conv_owner.reshape(-1, LANES), conv_cell.reshape(-1, LANES),
        owner_total, capacity,
    )
    before = lax.ppermute(send_up, "gx", up_x)
    after = lax.ppermute(send_down, "gx", down_x)
    low = lax.ppermute(side_up, "gy", up_y)
    high = lax.ppermute(side_down, "gy", down_y)

    fold = LANES // capacity
    filled = filled.reshape(-1, 9, fold, capacity).transpose(0, 2, 1, 3).reshape(owner_total, 1, 9 * capacity)
    routed = lax.all_to_all(filled, ("gx", "gy"), split_axis=0, concat_axis=0, tiled=True)
    routed = routed.reshape(-1, fold, 9, capacity).transpose(0, 2, 1, 3).reshape(-1, LANES)

    inner_cells = inner(cell_state, low, high, evap_rate)
    new_parcels = arrive(advanced, hot, crossing, before, after)
    new_cells = final(cell_state, inner_cells, before, after, low, high, routed, evap_rate)
    return (new_cells, new_parcels)


def solution(mesh):
    in_specs = (
        P(None, "gx", "gy", None),
        P(),
        P(None, ("gx", "gy")),
        P(None, ("gx", "gy")),
        P(None, ("gx", "gy")),
        P(("gx", "gy"), None),
        P(("gx", "gy")),
    )
    out_specs = (P(None, "gx", "gy", None), P(None, ("gx", "gy")))
    return jax.shard_map(
        on_device, mesh=mesh, in_specs=in_specs, out_specs=out_specs, check_vma=False
    )
```

```python
import functools

import jax
import jax.numpy as jnp
from jax import lax
from jax.experimental import pallas as pl
from jax.experimental.pallas import tpu as pltpu
from jax.sharding import PartitionSpec as P

SECTIONS = 8
SPECIES = 6
COUNT = SECTIONS + SPECIES
LANES = 128
WIDE = 256
WINDOW = 4
F32 = jnp.float32
BF16 = jnp.bfloat16
ANY = pl.BlockSpec(memory_space=pl.ANY)
SMEM = pl.BlockSpec(memory_space=pltpu.SMEM)
VMEM = pl.BlockSpec(memory_space=pltpu.VMEM)
ALL = 63 << 20
MOST = 32 << 20


def call(kernel, out_shape, operands, scratch, in_specs=None, out_specs=ANY, flops=0, moved_bytes=0, grant=MOST):
    many = isinstance(out_shape, (list, tuple))
    return pl.pallas_call(
        kernel,
        out_shape=out_shape,
        in_specs=in_specs or [ANY] * len(operands),
        out_specs=[out_specs] * len(out_shape) if many else out_specs,
        scratch_shapes=scratch,
        compiler_params=pltpu.CompilerParams(vmem_limit_bytes=grant),
        cost_estimate=pl.CostEstimate(flops=flops, bytes_accessed=moved_bytes, transcendentals=0),
    )(*operands)


def iota(shape, axis):
    return lax.broadcasted_iota(jnp.int32, shape, axis)


def packed(value):
    return value.astype(F32).astype(BF16)


def split(value):
    coarse = value.astype(BF16)
    return coarse, (value - coarse.astype(F32)).astype(BF16)


def rows_of(row, count):
    return jnp.broadcast_to(row, (count, row.shape[1])).astype(BF16)


def hot_columns(lower, count):
    return jnp.where(rows_of(lower.astype(F32), count) == packed(iota((count, LANES), 0)), 1.0, 0.0).astype(BF16)


def contract_lanes(left, right):
    return lax.dot_general(left, right, (((1,), (1,)), ((), ())), preferred_element_type=F32)


def advance_block(block):
    row = iota(block.shape, 0)
    diameter = jnp.broadcast_to(block[6:7], block.shape)
    warmth = jnp.broadcast_to(block[7:8], block.shape)
    factor = 0.8 / (1.0 + diameter * diameter)
    slowed = block * (1.0 - factor)
    travel = pltpu.roll(0.5 * (block + slowed), 5, 0)
    shrunk = block * (1.0 - 0.05 * warmth)
    warmed = block + factor * (1.0 - block)
    return jnp.where(row < 3, block + travel, jnp.where(row < 6, slowed, jnp.where(row == 6, shrunk, warmed)))


def scatter_left(left_ref, at, upper, uppers, coarse, fine):
    upper = rows_of(upper.astype(F32), 16)
    twice_coarse = jnp.concatenate([coarse.astype(F32)] * 2, axis=0).astype(BF16)
    twice_fine = jnp.concatenate([fine.astype(F32)] * 2, axis=0).astype(BF16)
    zero = jnp.zeros((16, LANES), BF16)
    pair = iota((16, LANES), 0) // 8
    for u in range(0, uppers, 2):
        hit = upper == packed(pair + u)
        left_ref[8 * u : 8 * u + 16, at] = jnp.where(hit, twice_coarse, zero)
        left_ref[8 * (uppers + u) : 8 * (uppers + u) + 16, at] = jnp.where(hit, twice_fine, zero)


def bucket_into(owner_total, capacity, mass_ref, owner_ref, cell_ref, out_ref, left_ref, hot_ref):
    blocks = owner_ref.shape[0]
    uppers = out_ref.shape[0] // 9 // 2
    strict = iota((LANES, 2 * LANES), 0) < iota((LANES, 2 * LANES), 1)
    strict = jnp.where(strict, 1.0, 0.0).astype(BF16)
    owners = owner_ref[...]
    cells = cell_ref[...]
    hots = [
        jnp.where(jnp.broadcast_to(owners[b : b + 1], (owner_total, LANES)) == iota((owner_total, LANES), 0), 1.0, 0.0)
        for b in range(blocks)
    ]
    ranks = jnp.dot(jnp.concatenate(hots, axis=0).astype(BF16), strict, preferred_element_type=F32)
    carry = jnp.zeros((owner_total, LANES), F32)
    base = 16 * uppers
    for b in range(blocks):
        part = ranks[b * owner_total : (b + 1) * owner_total]
        rank = jnp.sum(hots[b] * (part[:, :LANES] + carry), axis=0, keepdims=True).astype(jnp.int32)
        carry = carry + part[:, LANES:]
        spot = owners[b : b + 1] * capacity + rank
        at = slice(b * LANES, (b + 1) * LANES)
        hot_ref[:, at] = hot_columns(spot & (WIDE - 1), WIDE)
        coarse, fine = split(mass_ref[:, at])
        upper = spot >> 8
        scatter_left(left_ref, at, upper, uppers, coarse, fine)
        hit = rows_of(upper.astype(F32), uppers) == packed(iota((uppers, LANES), 0))
        zero = jnp.zeros((uppers, LANES), BF16)
        cell = cells[b : b + 1]
        left_ref[base : base + uppers, at] = jnp.where(hit, rows_of((cell >> 8).astype(F32), uppers), zero)
        left_ref[base + uppers : base + 2 * uppers, at] = jnp.where(
            hit, rows_of((cell & (WIDE - 1)).astype(F32), uppers), zero
        )
        left_ref[base + 2 * uppers : base + 3 * uppers, at] = jnp.where(hit, 1.0, 0.0).astype(BF16)
    placed = contract_lanes(left_ref[...], hot_ref[...])
    cell = placed[base : base + uppers] * float(WIDE) + placed[base + uppers : base + 2 * uppers]
    cell = jnp.where(placed[base + 2 * uppers : base + 3 * uppers] > 0.5, cell, -1.0)
    for u in range(uppers):
        mass = placed[8 * u : 8 * u + 8] + placed[8 * (uppers + u) : 8 * (uppers + u) + 8]
        for half in range(2):
            row = 9 * (2 * u + half)
            lanes = slice(half * LANES, (half + 1) * LANES)
            out_ref[row : row + 8, :] = mass[:, lanes]
            out_ref[row + 8 : row + 9, :] = cell[u : u + 1, lanes]


def prepare_kernel(
    owner_total, capacity,
    cells_hbm, parcels_hbm, crossing_hbm, mass_hbm, owner_hbm, cell_hbm,
    up_hbm, down_hbm, yup_hbm, ydown_hbm, advanced_hbm, hot_hbm, filled_hbm,
    cells_ref, parcels_ref, crossing_ref, mass_ref, owner_ref, cell_ref,
    leave_ref, yup_ref, ydown_ref, advanced_ref, hot_ref, filled_ref,
    parts_ref, left_ref, spot_ref, sems,
):
    size_x, size_y, size_z = cells_hbm.shape[1:]
    face = slice(0, COUNT + 1)
    tail = slice(COUNT + 1, up_hbm.shape[0])
    pairs = [
        (crossing_hbm, crossing_ref),
        (owner_hbm, owner_ref),
        (cell_hbm, cell_ref),
        (mass_hbm, mass_ref),
        (parcels_hbm, parcels_ref),
        (cells_hbm, cells_ref),
        (cells_ref.at[face, size_x - 1], up_hbm.at[face]),
        (cells_ref.at[face, 0], down_hbm.at[face]),
        (filled_ref, filled_hbm),
        (hot_ref, hot_hbm),
        (advanced_ref, advanced_hbm),
        (leave_ref.at[0], up_hbm.at[tail]),
        (leave_ref.at[1], down_hbm.at[tail]),
        (yup_ref, yup_hbm),
        (ydown_ref, ydown_hbm),
    ]
    copies = [pltpu.make_async_copy(source, target, sems.at[i]) for i, (source, target) in enumerate(pairs)]
    for copy in copies[:6]:
        copy.start()
    cross = crossing_ref.shape[1]
    slot_total = parcels_ref.shape[1]
    copies[0].wait()
    for side in range(2):
        for first in range(0, cross, LANES):
            lower = crossing_ref[side : side + 1, first : first + LANES] & (WIDE - 1)
            hot_ref[:, side * cross + first : side * cross + first + LANES] = hot_columns(lower, WIDE)
    copies[9].start()
    copies[4].wait()

    def advance_pair(i, unused):
        for number in range(2):
            blocks = []
            for half in range(2):
                at = pl.ds(pl.multiple_of((4 * i + 2 * number + half) * LANES, LANES), LANES)
                block = advance_block(parcels_ref[:, at])
                advanced_ref[:, at] = block
                blocks.append(block)
            parts_ref[pl.ds(pl.multiple_of((2 * i + number) * 8, 8), 8), :] = jnp.concatenate(blocks, axis=1)
        return unused

    lax.fori_loop(0, slot_total // (4 * LANES), advance_pair, 0, unroll=4)
    copies[10].start()

    halves_y, halves_z = size_y // 8, size_z // LANES
    part_rows = parts_ref.shape[0]
    step_rows = min(256, part_rows)
    for rows in range(0, part_rows, step_rows):
        coarse, fine = split(parts_ref[rows : rows + step_rows])
        for side in range(2):
            for first in range(0, cross, WIDE):
                upper = jnp.broadcast_to(crossing_ref[side : side + 1, first : first + WIDE] >> 8, (8, WIDE))
                hot = hot_ref[:, side * cross + first : side * cross + first + WIDE]
                picked = jnp.dot(coarse, hot, preferred_element_type=F32) + jnp.dot(
                    fine, hot, preferred_element_type=F32
                )
                spots = []
                for offset in range(0, WIDE, LANES):
                    layer, rest = divmod((first + offset) // LANES, halves_y * halves_z)
                    half_y, half_z = divmod(rest, halves_z)
                    spots.append((side, layer, slice(8 * half_y, 8 * half_y + 8), slice(LANES * half_z, LANES * (half_z + 1))))
                if rows:
                    total = jnp.concatenate([leave_ref[spot] for spot in spots], axis=1)
                else:
                    total = jnp.zeros((8, WIDE), F32)
                for i in range(0, step_rows, 8):
                    total = jnp.where(upper == (rows + i) // 8, picked[i : i + 8], total)
                for number, spot in enumerate(spots):
                    leave_ref[spot] = total[:, number * LANES : (number + 1) * LANES]
    copies[11].start()
    copies[12].start()

    copies[5].wait()
    copies[6].start()
    copies[7].start()
    for c in range(COUNT + 1):
        source = c if c < COUNT else COUNT + 1
        yup_ref[c] = cells_ref[source, :, size_y - 1, :]
        ydown_ref[c] = cells_ref[source, :, 0, :]
    copies[13].start()
    copies[14].start()
    for copy in copies[1:4]:
        copy.wait()
    bucket_into(owner_total, capacity, mass_ref, owner_ref, cell_ref, filled_ref, left_ref, spot_ref)
    copies[8].start()
    for copy in copies[6:]:
        copy.wait()


def prepare(cells, parcels, crossing, mass, owner, cell, owner_total, capacity):
    size_x, size_y, size_z = cells.shape[1:]
    extra = 8 * crossing.shape[1] // (size_y * size_z)
    places = owner_total * capacity
    shape = jax.ShapeDtypeStruct
    face = shape((COUNT + 1 + extra, size_y, size_z), F32)
    side = shape((COUNT + 1, size_x, size_z), F32)
    advanced = shape(parcels.shape, F32)
    hot = shape((WIDE, crossing.size), BF16)
    filled = shape((9 * places // LANES, LANES), F32)
    operands = (cells, parcels, crossing, mass, owner, cell)
    scratch = [pltpu.VMEM(a.shape, a.dtype) for a in operands]
    scratch += [pltpu.VMEM((2, extra, size_y, size_z), F32)]
    scratch += [pltpu.VMEM(a.shape, a.dtype) for a in (side, side, advanced, hot, filled)]
    scratch += [
        pltpu.VMEM((8 * parcels.shape[1] // WIDE, WIDE), F32),
        pltpu.VMEM((19 * places // WIDE, mass.shape[1]), BF16),
        pltpu.VMEM((WIDE, mass.shape[1]), BF16),
        pltpu.SemaphoreType.DMA((15,)),
    ]
    return call(
        functools.partial(prepare_kernel, owner_total, capacity),
        [face, face, side, side, advanced, hot, filled], operands, scratch,
        flops=2 << 30, moved_bytes=6 << 20, grant=ALL,
    )


def arrive_kernel(advanced_ref, hot_ref, crossing_ref, before_ref, after_ref, out_hbm, out_ref, left_ref, sems):
    cross = crossing_ref.shape[1]
    uppers = advanced_ref.shape[1] // WIDE
    size_y, size_z = before_ref.shape[1:]
    halves_y, halves_z = size_y // 8, size_z // LANES
    for side, come_ref in ((0, before_ref), (1, after_ref)):
        for first in range(0, cross, LANES):
            layer, rest = divmod(first // LANES, halves_y * halves_z)
            half_y, half_z = divmod(rest, halves_z)
            block = come_ref[COUNT + 1 + layer, 8 * half_y : 8 * half_y + 8, LANES * half_z : LANES * (half_z + 1)]
            coarse, fine = split(block)
            upper = crossing_ref[side : side + 1, first : first + LANES] >> 8
            at = slice(side * cross + first, side * cross + first + LANES)
            scatter_left(left_ref, at, upper, uppers, coarse, fine)
            hit = rows_of(upper.astype(F32), uppers) == packed(iota((uppers, LANES), 0))
            left_ref[16 * uppers :, at] = jnp.where(hit, 1.0, 0.0).astype(BF16)
    hit = contract_lanes(left_ref[16 * uppers :], hot_ref[...])
    step = min(32, uppers)
    outs = []
    for u in range(0, uppers, step):
        total = contract_lanes(left_ref[8 * u : 8 * (u + step)], hot_ref[...]) + contract_lanes(
            left_ref[8 * (uppers + u) : 8 * (uppers + u + step)], hot_ref[...]
        )
        for i in range(step):
            at = slice((u + i) * WIDE, (u + i + 1) * WIDE)
            taken = jnp.broadcast_to(hit[u + i : u + i + 1], (8, WIDE)) > 0.5
            out_ref[:, at] = jnp.where(taken, total[8 * i : 8 * i + 8], advanced_ref[:, at])
        at = slice(u * WIDE, (u + step) * WIDE)
        out = pltpu.make_async_copy(out_ref.at[:, at], out_hbm.at[:, at], sems.at[len(outs)])
        out.start()
        outs.append(out)
    for out in outs:
        out.wait()


def arrive(advanced, hot, crossing, before, after):
    uppers = advanced.shape[1] // WIDE
    return call(
        arrive_kernel, jax.ShapeDtypeStruct(advanced.shape, F32), (advanced, hot, crossing, before, after),
        [
            pltpu.VMEM(advanced.shape, F32),
            pltpu.VMEM((17 * uppers, crossing.size), BF16),
            pltpu.SemaphoreType.DMA((-(-uppers // 32),)),
        ],
        in_specs=[VMEM] * 5, flops=1 << 30, moved_bytes=3 << 20,
    )


def shift_up(value, axis):
    return pltpu.roll(value, value.shape[axis] - 1, axis)


def shift_down(value, axis):
    return pltpu.roll(value, 1, axis)


def slab_update(left, center, right, side_low, side_high, rate_ref, write):
    course = center(COUNT)
    size_y, size_z = course.shape
    first_row = iota((size_y, size_z), 0) == 0
    last_row = iota((size_y, size_z), 0) == size_y - 1

    def row_up(value, edge):
        return jnp.where(last_row, edge, shift_up(value, 0))

    def row_down(value, edge):
        return jnp.where(first_row, edge, shift_down(value, 0))

    face_x = 0.5 * (course + right(COUNT))
    face_x_low = 0.5 * (left(COUNT) + course)
    course_y = center(COUNT + 1)
    face_y = 0.5 * (course_y + row_up(course_y, side_high(COUNT)))
    face_y_low = 0.5 * (row_down(course_y, side_low(COUNT)) + course_y)
    course_z = center(COUNT + 2)
    lane = iota((size_y, size_z), 1)
    face_z = jnp.where(lane == size_z - 1, 0.0, 0.5 * (course_z + shift_up(course_z, 1)))
    face_z_low = jnp.where(lane == 0, 0.0, 0.5 * (shift_down(course_z, 1) + course_z))
    from_x_up, from_x_low = jnp.minimum(face_x, 0.0), jnp.maximum(face_x_low, 0.0)
    from_y_up, from_y_low = jnp.minimum(face_y, 0.0), jnp.maximum(face_y_low, 0.0)
    from_z_up, from_z_low = jnp.minimum(face_z, 0.0), jnp.maximum(face_z_low, 0.0)
    own = 1.0 - (
        (jnp.maximum(face_x, 0.0) - jnp.minimum(face_x_low, 0.0))
        + (jnp.maximum(face_y, 0.0) - jnp.minimum(face_y_low, 0.0))
        + (jnp.maximum(face_z, 0.0) - jnp.minimum(face_z_low, 0.0))
    )

    def moved(c):
        amount = center(c)
        total = own * amount
        total = total - from_x_up * right(c) + from_x_low * left(c)
        total = total - from_y_up * row_up(amount, side_high(c)) + from_y_low * row_down(amount, side_low(c))
        return total - from_z_up * shift_up(amount, 1) + from_z_low * shift_down(amount, 1)

    vapour = moved(SECTIONS)
    beside = 1.0 + vapour
    later = None
    gained = None
    for s in reversed(range(SECTIONS)):
        section = moved(s)
        loss = rate_ref[s] * section / beside
        value = section - loss
        if later is not None:
            value = value + 0.5 * later
            gained = later if gained is None else gained + later
        write(s, value)
        later = loss
    write(SECTIONS, vapour + later + 0.5 * gained)
    for c in range(SECTIONS + 1, COUNT):
        write(c, moved(c))


def cells_kernel(
    cells_ref, before_ref, after_ref, low_ref, high_ref, deposit_ref, rate_ref, out_hbm, out_ref, sems
):
    size_x = cells_ref.shape[1]
    last = size_x - 1

    def store(x):
        return pltpu.make_async_copy(out_ref.at[:, x], out_hbm.at[:, x], sems.at[x])

    def layer(left, x, right):
        def write(c, value):
            out_ref[c, x] = value + deposit_ref[c, x] if c < SECTIONS else value

        slab_update(
            left,
            lambda c: cells_ref[c, x],
            right,
            lambda c: low_ref[c, pl.ds(x, 1), :],
            lambda c: high_ref[c, pl.ds(x, 1), :],
            rate_ref,
            write,
        )
        store(x).start()

    def middle(x, unused):
        layer(lambda c: cells_ref[c, x - 1], x, lambda c: cells_ref[c, x + 1])
        return unused

    lax.fori_loop(1, last, middle, 0)
    layer(lambda c: before_ref[c], 0, lambda c: cells_ref[c, 1])
    layer(lambda c: cells_ref[c, last - 1], last, lambda c: after_ref[c])
    for x in range(size_x):
        store(x).wait()


def update_cells(cells, before, after, low, high, deposited, rate):
    out = jax.ShapeDtypeStruct((COUNT,) + cells.shape[1:], F32)
    return call(
        cells_kernel, out, (cells, before, after, low, high, deposited, rate),
        [pltpu.VMEM(out.shape, F32), pltpu.SemaphoreType.DMA((cells.shape[1],))],
        in_specs=[VMEM] * 6 + [SMEM], flops=30 << 20, moved_bytes=4 << 20,
    )


def quotient(value, count):
    return value >> (count.bit_length() - 1) if count & (count - 1) == 0 else value // count


def deposit_kernel(shape, routed_ref, out_ref, total_ref, mass_ref, spread_ref, depth_ref):
    size_x, size_y, size_z = shape
    groups = routed_ref.shape[0] // 9
    per = groups // 8
    span = LANES // per
    lane_part = quotient(iota((8, LANES), 1), span)
    for v in range(9):
        rows = routed_ref[pl.ds(v, groups, stride=9), :]
        for q in range(per):
            total = None
            for g in range(per):
                block = rows[8 * g : 8 * g + 8]
                if g != q:
                    block = pltpu.roll(block, (span * (g - q)) % LANES, 1)
                total = block if total is None else jnp.where(lane_part == g, block, total)
            mass_ref[q, v] = total

    bounds = []
    for q in range(per):
        cell = mass_ref[q, SECTIONS].astype(jnp.int32)
        layer = quotient(cell, size_y * size_z)
        valid = cell >= 0
        bounds.append((jnp.min(jnp.where(valid, layer, size_x)), jnp.max(jnp.where(valid, layer, -1))))

    half = SECTIONS * WINDOW * size_y
    zero = jnp.zeros((size_y, LANES), BF16)

    def spread(q, first):
        cell = mass_ref[q, SECTIONS].astype(jnp.int32)
        plane = quotient(cell, size_z)
        depth = cell - plane * size_z
        plane = jnp.where(cell >= 0, plane - first * size_y, -1).astype(F32)
        parts = [split(mass_ref[q, s]) for s in range(SECTIONS)]
        for i in range(8):
            at = slice(i * LANES, (i + 1) * LANES)
            depth_ref[q % 2, :, at] = hot_columns(depth[i : i + 1], size_z)
            plane_rows = rows_of(plane[i : i + 1], size_y)
            rows = [[rows_of(part[i : i + 1].astype(F32), size_y) for part in pair] for pair in parts]
            for w in range(WINDOW):
                hit = plane_rows == packed(iota((size_y, LANES), 0) + w * size_y)
                for s in range(SECTIONS):
                    base = (s * WINDOW + w) * size_y
                    for part in range(2):
                        spread_ref[q % 2, part * half + base : part * half + base + size_y, at] = jnp.where(
                            hit, rows[s][part], zero
                        )

    def deposit(q, first):
        added = contract_lanes(spread_ref[q % 2], depth_ref[q % 2])
        for s in range(SECTIONS):
            base = s * WINDOW * size_y
            rows = added[base : base + WINDOW * size_y] + added[half + base : half + base + WINDOW * size_y]
            at = pl.ds(first, WINDOW)
            total_ref[s, at] = total_ref[s, at] + rows.reshape(WINDOW, size_y, size_z)

    total_ref[...] = jnp.zeros(total_ref.shape, F32)
    for q in range(per):
        first = jnp.minimum(bounds[q][0], size_x - 1)
        spread(q, first)
        deposit(q, first)
    for q in range(per):
        low, high = bounds[q]

        def more(t, unused, q=q, low=low):
            first = low + t * WINDOW
            spread(q, first)
            deposit(q, first)
            return unused

        lax.fori_loop(1, quotient(high - low + WINDOW, WINDOW), more, 0)
    out_ref[...] = total_ref[:, 0:size_x]


def deposit(routed, shape):
    size_x, size_y, size_z = shape
    per = routed.shape[0] // 9 // 8
    return call(
        functools.partial(deposit_kernel, shape), jax.ShapeDtypeStruct((SECTIONS,) + shape, F32), (routed,),
        [
            pltpu.VMEM((SECTIONS, size_x + WINDOW - 1, size_y, size_z), F32),
            pltpu.VMEM((per, SECTIONS + 1, 8, LANES), F32),
            pltpu.VMEM((2, 2 * SECTIONS * WINDOW * size_y, 8 * LANES), BF16),
            pltpu.VMEM((2, size_z, 8 * LANES), BF16),
        ],
        in_specs=[VMEM], out_specs=VMEM, flops=4 << 30, moved_bytes=2 << 20,
    )


def ring(size):
    up = [(i, (i + 1) % size) for i in range(size)]
    return up, [(j, i) for i, j in up]


def on_device(cell_state, evap_rate, parcels, crossing, conv_mass, conv_owner, conv_cell):
    owner_total = lax.axis_size("gx") * lax.axis_size("gy")
    row_total = conv_owner.shape[0]
    capacity = 2 * row_total // owner_total
    up_x, down_x = ring(lax.axis_size("gx"))
    up_y, down_y = ring(lax.axis_size("gy"))

    send_up, send_down, side_up, side_down, advanced, hot, filled = prepare(
        cell_state, parcels, crossing, conv_mass, conv_owner.reshape(-1, LANES), conv_cell.reshape(-1, LANES),
        owner_total, capacity,
    )
    before = lax.ppermute(send_up, "gx", up_x)
    after = lax.ppermute(send_down, "gx", down_x)
    low = lax.ppermute(side_up, "gy", up_y)
    high = lax.ppermute(side_down, "gy", down_y)

    fold = LANES // capacity
    filled = filled.reshape(-1, 9, fold, capacity).transpose(0, 2, 1, 3).reshape(owner_total, 1, 9 * capacity)
    routed = lax.all_to_all(filled, ("gx", "gy"), split_axis=0, concat_axis=0, tiled=True)
    routed = routed.reshape(-1, fold, 9, capacity).transpose(0, 2, 1, 3).reshape(-1, LANES)

    deposited = deposit(routed, cell_state.shape[1:])
    new_parcels = arrive(advanced, hot, crossing, before, after)
    new_cells = update_cells(cell_state, before, after, low, high, deposited, evap_rate)
    return (new_cells, new_parcels)


def solution(mesh):
    in_specs = (
        P(None, "gx", "gy", None),
        P(),
        P(None, ("gx", "gy")),
        P(None, ("gx", "gy")),
        P(None, ("gx", "gy")),
        P(("gx", "gy"), None),
        P(("gx", "gy")),
    )
    out_specs = (P(None, "gx", "gy", None), P(None, ("gx", "gy")))
    return jax.shard_map(
        on_device, mesh=mesh, in_specs=in_specs, out_specs=out_specs, check_vma=False
    )
```

```python
import functools

import jax
import jax.numpy as jnp
from jax import lax
from jax.experimental import pallas as pl
from jax.experimental.pallas import tpu as pltpu
from jax.sharding import PartitionSpec as P

SECTIONS = 8
SPECIES = 6
COUNT = SECTIONS + SPECIES
LANES = 128
WIDE = 256
WINDOW = 4
F32 = jnp.float32
BF16 = jnp.bfloat16
ANY = pl.BlockSpec(memory_space=pl.ANY)
SMEM = pl.BlockSpec(memory_space=pltpu.SMEM)
VMEM = pl.BlockSpec(memory_space=pltpu.VMEM)
ALL = 63 << 20
MOST = 32 << 20


def call(kernel, out_shape, operands, scratch, in_specs=None, out_specs=ANY, flops=0, moved_bytes=0, grant=MOST):
    many = isinstance(out_shape, (list, tuple))
    return pl.pallas_call(
        kernel,
        out_shape=out_shape,
        in_specs=in_specs or [ANY] * len(operands),
        out_specs=[out_specs] * len(out_shape) if many else out_specs,
        scratch_shapes=scratch,
        compiler_params=pltpu.CompilerParams(vmem_limit_bytes=grant),
        cost_estimate=pl.CostEstimate(flops=flops, bytes_accessed=moved_bytes, transcendentals=0),
    )(*operands)


def iota(shape, axis):
    return lax.broadcasted_iota(jnp.int32, shape, axis)


def packed(value):
    return value.astype(F32).astype(BF16)


def split(value):
    coarse = value.astype(BF16)
    return coarse, (value - coarse.astype(F32)).astype(BF16)


def rows_of(row, count):
    return jnp.broadcast_to(row, (count, row.shape[1])).astype(BF16)


def hot_columns(lower, count):
    return jnp.where(rows_of(lower.astype(F32), count) == packed(iota((count, LANES), 0)), 1.0, 0.0).astype(BF16)


def contract_lanes(left, right):
    return lax.dot_general(left, right, (((1,), (1,)), ((), ())), preferred_element_type=F32)


def advance_block(block):
    row = iota(block.shape, 0)
    diameter = jnp.broadcast_to(block[6:7], block.shape)
    warmth = jnp.broadcast_to(block[7:8], block.shape)
    factor = 0.8 / (1.0 + diameter * diameter)
    slowed = block * (1.0 - factor)
    travel = pltpu.roll(0.5 * (block + slowed), 5, 0)
    shrunk = block * (1.0 - 0.05 * warmth)
    warmed = block + factor * (1.0 - block)
    return jnp.where(row < 3, block + travel, jnp.where(row < 6, slowed, jnp.where(row == 6, shrunk, warmed)))


def scatter_left(left_ref, at, upper, uppers, coarse, fine):
    upper = rows_of(upper.astype(F32), 16)
    twice_coarse = jnp.concatenate([coarse.astype(F32)] * 2, axis=0).astype(BF16)
    twice_fine = jnp.concatenate([fine.astype(F32)] * 2, axis=0).astype(BF16)
    zero = jnp.zeros((16, LANES), BF16)
    pair = iota((16, LANES), 0) // 8
    for u in range(0, uppers, 2):
        hit = upper == packed(pair + u)
        left_ref[8 * u : 8 * u + 16, at] = jnp.where(hit, twice_coarse, zero)
        left_ref[8 * (uppers + u) : 8 * (uppers + u) + 16, at] = jnp.where(hit, twice_fine, zero)


def bucket_into(owner_total, capacity, mass_ref, owner_ref, cell_ref, out_ref, left_ref, hot_ref):
    blocks = owner_ref.shape[0]
    uppers = out_ref.shape[0] // 9 // 2
    strict = iota((LANES, 2 * LANES), 0) < iota((LANES, 2 * LANES), 1)
    strict = jnp.where(strict, 1.0, 0.0).astype(BF16)
    owners = owner_ref[...]
    cells = cell_ref[...]
    hots = [
        jnp.where(jnp.broadcast_to(owners[b : b + 1], (owner_total, LANES)) == iota((owner_total, LANES), 0), 1.0, 0.0)
        for b in range(blocks)
    ]
    ranks = jnp.dot(jnp.concatenate(hots, axis=0).astype(BF16), strict, preferred_element_type=F32)
    carry = jnp.zeros((owner_total, LANES), F32)
    base = 16 * uppers
    for b in range(blocks):
        part = ranks[b * owner_total : (b + 1) * owner_total]
        rank = jnp.sum(hots[b] * (part[:, :LANES] + carry), axis=0, keepdims=True).astype(jnp.int32)
        carry = carry + part[:, LANES:]
        spot = owners[b : b + 1] * capacity + rank
        at = slice(b * LANES, (b + 1) * LANES)
        hot_ref[:, at] = hot_columns(spot & (WIDE - 1), WIDE)
        coarse, fine = split(mass_ref[:, at])
        upper = spot >> 8
        scatter_left(left_ref, at, upper, uppers, coarse, fine)
        hit = rows_of(upper.astype(F32), uppers) == packed(iota((uppers, LANES), 0))
        zero = jnp.zeros((uppers, LANES), BF16)
        cell = cells[b : b + 1]
        left_ref[base : base + uppers, at] = jnp.where(hit, rows_of((cell >> 8).astype(F32), uppers), zero)
        left_ref[base + uppers : base + 2 * uppers, at] = jnp.where(
            hit, rows_of((cell & (WIDE - 1)).astype(F32), uppers), zero
        )
        left_ref[base + 2 * uppers : base + 3 * uppers, at] = jnp.where(hit, 1.0, 0.0).astype(BF16)
    placed = contract_lanes(left_ref[...], hot_ref[...])
    cell = placed[base : base + uppers] * float(WIDE) + placed[base + uppers : base + 2 * uppers]
    cell = jnp.where(placed[base + 2 * uppers : base + 3 * uppers] > 0.5, cell, -1.0)
    for u in range(uppers):
        mass = placed[8 * u : 8 * u + 8] + placed[8 * (uppers + u) : 8 * (uppers + u) + 8]
        for half in range(2):
            row = 9 * (2 * u + half)
            lanes = slice(half * LANES, (half + 1) * LANES)
            out_ref[row : row + 8, :] = mass[:, lanes]
            out_ref[row + 8 : row + 9, :] = cell[u : u + 1, lanes]


def prepare_kernel(
    owner_total, capacity,
    cells_hbm, parcels_hbm, crossing_hbm, mass_hbm, owner_hbm, cell_hbm,
    up_hbm, down_hbm, yup_hbm, ydown_hbm, advanced_hbm, hot_hbm, filled_hbm,
    cells_ref, parcels_ref, crossing_ref, mass_ref, owner_ref, cell_ref,
    leave_ref, yup_ref, ydown_ref, advanced_ref, hot_ref, filled_ref,
    parts_ref, left_ref, spot_ref, sems,
):
    size_x, size_y, size_z = cells_hbm.shape[1:]
    face = slice(0, COUNT + 1)
    tail = slice(COUNT + 1, up_hbm.shape[0])
    pairs = [
        (crossing_hbm, crossing_ref),
        (owner_hbm, owner_ref),
        (cell_hbm, cell_ref),
        (mass_hbm, mass_ref),
        (parcels_hbm, parcels_ref),
        (cells_hbm, cells_ref),
        (cells_ref.at[face, size_x - 1], up_hbm.at[face]),
        (cells_ref.at[face, 0], down_hbm.at[face]),
        (filled_ref, filled_hbm),
        (hot_ref, hot_hbm),
        (advanced_ref, advanced_hbm),
        (leave_ref.at[0], up_hbm.at[tail]),
        (leave_ref.at[1], down_hbm.at[tail]),
        (yup_ref, yup_hbm),
        (ydown_ref, ydown_hbm),
    ]
    copies = [pltpu.make_async_copy(source, target, sems.at[i]) for i, (source, target) in enumerate(pairs)]
    for copy in copies[:6]:
        copy.start()
    cross = crossing_ref.shape[1]
    slot_total = parcels_ref.shape[1]
    copies[0].wait()
    for side in range(2):
        for first in range(0, cross, LANES):
            lower = crossing_ref[side : side + 1, first : first + LANES] & (WIDE - 1)
            hot_ref[:, side * cross + first : side * cross + first + LANES] = hot_columns(lower, WIDE)
    copies[9].start()
    copies[4].wait()

    def advance_pair(i, unused):
        for number in range(2):
            blocks = []
            for half in range(2):
                at = pl.ds(pl.multiple_of((4 * i + 2 * number + half) * LANES, LANES), LANES)
                block = advance_block(parcels_ref[:, at])
                advanced_ref[:, at] = block
                blocks.append(block)
            parts_ref[pl.ds(pl.multiple_of((2 * i + number) * 8, 8), 8), :] = jnp.concatenate(blocks, axis=1)
        return unused

    lax.fori_loop(0, slot_total // (4 * LANES), advance_pair, 0, unroll=4)
    copies[10].start()

    halves_y, halves_z = size_y // 8, size_z // LANES
    part_rows = parts_ref.shape[0]
    step_rows = min(256, part_rows)
    for rows in range(0, part_rows, step_rows):
        coarse, fine = split(parts_ref[rows : rows + step_rows])
        for side in range(2):
            for first in range(0, cross, WIDE):
                upper = jnp.broadcast_to(crossing_ref[side : side + 1, first : first + WIDE] >> 8, (8, WIDE))
                hot = hot_ref[:, side * cross + first : side * cross + first + WIDE]
                picked = jnp.dot(coarse, hot, preferred_element_type=F32) + jnp.dot(
                    fine, hot, preferred_element_type=F32
                )
                spots = []
                for offset in range(0, WIDE, LANES):
                    layer, rest = divmod((first + offset) // LANES, halves_y * halves_z)
                    half_y, half_z = divmod(rest, halves_z)
                    spots.append((side, layer, slice(8 * half_y, 8 * half_y + 8), slice(LANES * half_z, LANES * (half_z + 1))))
                if rows:
                    total = jnp.concatenate([leave_ref[spot] for spot in spots], axis=1)
                else:
                    total = jnp.zeros((8, WIDE), F32)
                for i in range(0, step_rows, 8):
                    total = jnp.where(upper == (rows + i) // 8, picked[i : i + 8], total)
                for number, spot in enumerate(spots):
                    leave_ref[spot] = total[:, number * LANES : (number + 1) * LANES]
    copies[11].start()
    copies[12].start()

    copies[5].wait()
    copies[6].start()
    copies[7].start()
    for c in range(COUNT + 1):
        source = c if c < COUNT else COUNT + 1
        yup_ref[c] = cells_ref[source, :, size_y - 1, :]
        ydown_ref[c] = cells_ref[source, :, 0, :]
    copies[13].start()
    copies[14].start()
    for copy in copies[1:4]:
        copy.wait()
    bucket_into(owner_total, capacity, mass_ref, owner_ref, cell_ref, filled_ref, left_ref, spot_ref)
    copies[8].start()
    for copy in copies[6:]:
        copy.wait()


def prepare(cells, parcels, crossing, mass, owner, cell, owner_total, capacity):
    size_x, size_y, size_z = cells.shape[1:]
    extra = 8 * crossing.shape[1] // (size_y * size_z)
    places = owner_total * capacity
    shape = jax.ShapeDtypeStruct
    face = shape((COUNT + 1 + extra, size_y, size_z), F32)
    side = shape((COUNT + 1, size_x, size_z), F32)
    advanced = shape(parcels.shape, F32)
    hot = shape((WIDE, crossing.size), BF16)
    filled = shape((9 * places // LANES, LANES), F32)
    operands = (cells, parcels, crossing, mass, owner, cell)
    scratch = [pltpu.VMEM(a.shape, a.dtype) for a in operands]
    scratch += [pltpu.VMEM((2, extra, size_y, size_z), F32)]
    scratch += [pltpu.VMEM(a.shape, a.dtype) for a in (side, side, advanced, hot, filled)]
    scratch += [
        pltpu.VMEM((8 * parcels.shape[1] // WIDE, WIDE), F32),
        pltpu.VMEM((19 * places // WIDE, mass.shape[1]), BF16),
        pltpu.VMEM((WIDE, mass.shape[1]), BF16),
        pltpu.SemaphoreType.DMA((15,)),
    ]
    return call(
        functools.partial(prepare_kernel, owner_total, capacity),
        [face, face, side, side, advanced, hot, filled], operands, scratch,
        flops=2 << 30, moved_bytes=6 << 20, grant=ALL,
    )


def arrive_kernel(unused, advanced_ref, hot_ref, crossing_ref, before_ref, after_ref, out_hbm, out_ref, left_ref, sems):
    cross = crossing_ref.shape[1]
    uppers = advanced_ref.shape[1] // WIDE
    size_y, size_z = before_ref.shape[1:]
    halves_y, halves_z = size_y // 8, size_z // LANES
    for side, come_ref in ((0, before_ref), (1, after_ref)):
        for first in range(0, cross, LANES):
            layer, rest = divmod(first // LANES, halves_y * halves_z)
            half_y, half_z = divmod(rest, halves_z)
            block = come_ref[COUNT + 1 + layer, 8 * half_y : 8 * half_y + 8, LANES * half_z : LANES * (half_z + 1)]
            coarse, fine = split(block)
            upper = crossing_ref[side : side + 1, first : first + LANES] >> 8
            at = slice(side * cross + first, side * cross + first + LANES)
            scatter_left(left_ref, at, upper, uppers, coarse, fine)
            hit = rows_of(upper.astype(F32), uppers) == packed(iota((uppers, LANES), 0))
            left_ref[16 * uppers :, at] = jnp.where(hit, 1.0, 0.0).astype(BF16)
    hit = contract_lanes(left_ref[16 * uppers :], hot_ref[...])
    step = min(32, uppers)
    outs = []
    for u in range(0, uppers, step):
        total = contract_lanes(left_ref[8 * u : 8 * (u + step)], hot_ref[...]) + contract_lanes(
            left_ref[8 * (uppers + u) : 8 * (uppers + u + step)], hot_ref[...]
        )
        for i in range(step):
            at = slice((u + i) * WIDE, (u + i + 1) * WIDE)
            taken = jnp.broadcast_to(hit[u + i : u + i + 1], (8, WIDE)) > 0.5
            out_ref[:, at] = jnp.where(taken, total[8 * i : 8 * i + 8], advanced_ref[:, at])
        at = slice(u * WIDE, (u + step) * WIDE)
        out = pltpu.make_async_copy(out_ref.at[:, at], out_hbm.at[:, at], sems.at[len(outs)])
        out.start()
        outs.append(out)
    for out in outs:
        out.wait()


def arrive(earlier, advanced, hot, crossing, before, after):
    uppers = advanced.shape[1] // WIDE
    return call(
        arrive_kernel, jax.ShapeDtypeStruct(advanced.shape, F32), (earlier, advanced, hot, crossing, before, after),
        [
            pltpu.VMEM(advanced.shape, F32),
            pltpu.VMEM((17 * uppers, crossing.size), BF16),
            pltpu.SemaphoreType.DMA((-(-uppers // 32),)),
        ],
        in_specs=[ANY] + [VMEM] * 5, flops=1 << 30, moved_bytes=3 << 20,
    )


def shift_up(value, axis):
    return pltpu.roll(value, value.shape[axis] - 1, axis)


def shift_down(value, axis):
    return pltpu.roll(value, 1, axis)


def slab_update(left, center, right, side_low, side_high, rate_ref, write):
    course = center(COUNT)
    size_y, size_z = course.shape
    first_row = iota((size_y, size_z), 0) == 0
    last_row = iota((size_y, size_z), 0) == size_y - 1

    def row_up(value, edge):
        return jnp.where(last_row, edge, shift_up(value, 0))

    def row_down(value, edge):
        return jnp.where(first_row, edge, shift_down(value, 0))

    face_x = 0.5 * (course + right(COUNT))
    face_x_low = 0.5 * (left(COUNT) + course)
    course_y = center(COUNT + 1)
    face_y = 0.5 * (course_y + row_up(course_y, side_high(COUNT)))
    face_y_low = 0.5 * (row_down(course_y, side_low(COUNT)) + course_y)
    course_z = center(COUNT + 2)
    lane = iota((size_y, size_z), 1)
    face_z = jnp.where(lane == size_z - 1, 0.0, 0.5 * (course_z + shift_up(course_z, 1)))
    face_z_low = jnp.where(lane == 0, 0.0, 0.5 * (shift_down(course_z, 1) + course_z))
    from_x_up, from_x_low = jnp.minimum(face_x, 0.0), jnp.maximum(face_x_low, 0.0)
    from_y_up, from_y_low = jnp.minimum(face_y, 0.0), jnp.maximum(face_y_low, 0.0)
    from_z_up, from_z_low = jnp.minimum(face_z, 0.0), jnp.maximum(face_z_low, 0.0)
    own = 1.0 - (
        (jnp.maximum(face_x, 0.0) - jnp.minimum(face_x_low, 0.0))
        + (jnp.maximum(face_y, 0.0) - jnp.minimum(face_y_low, 0.0))
        + (jnp.maximum(face_z, 0.0) - jnp.minimum(face_z_low, 0.0))
    )

    def moved(c):
        amount = center(c)
        total = own * amount
        total = total - from_x_up * right(c) + from_x_low * left(c)
        total = total - from_y_up * row_up(amount, side_high(c)) + from_y_low * row_down(amount, side_low(c))
        return total - from_z_up * shift_up(amount, 1) + from_z_low * shift_down(amount, 1)

    vapour = moved(SECTIONS)
    beside = 1.0 + vapour
    later = None
    gained = None
    for s in reversed(range(SECTIONS)):
        section = moved(s)
        loss = rate_ref[s] * section / beside
        value = section - loss
        if later is not None:
            value = value + 0.5 * later
            gained = later if gained is None else gained + later
        write(s, value)
        later = loss
    write(SECTIONS, vapour + later + 0.5 * gained)
    for c in range(SECTIONS + 1, COUNT):
        write(c, moved(c))


def cells_kernel(
    cells_ref, before_ref, after_ref, low_ref, high_ref, deposit_ref, rate_ref, out_hbm, out_ref, sems
):
    size_x = cells_ref.shape[1]
    last = size_x - 1

    def store(x):
        return pltpu.make_async_copy(out_ref.at[:, x], out_hbm.at[:, x], sems.at[x])

    def layer(left, x, right):
        def write(c, value):
            out_ref[c, x] = value + deposit_ref[c, x] if c < SECTIONS else value

        slab_update(
            left,
            lambda c: cells_ref[c, x],
            right,
            lambda c: low_ref[c, pl.ds(x, 1), :],
            lambda c: high_ref[c, pl.ds(x, 1), :],
            rate_ref,
            write,
        )
        store(x).start()

    def middle(x, unused):
        layer(lambda c: cells_ref[c, x - 1], x, lambda c: cells_ref[c, x + 1])
        return unused

    lax.fori_loop(1, last, middle, 0)
    layer(lambda c: before_ref[c], 0, lambda c: cells_ref[c, 1])
    layer(lambda c: cells_ref[c, last - 1], last, lambda c: after_ref[c])
    for x in range(size_x):
        store(x).wait()


def update_cells(cells, before, after, low, high, deposited, rate):
    out = jax.ShapeDtypeStruct((COUNT,) + cells.shape[1:], F32)
    return call(
        cells_kernel, out, (cells, before, after, low, high, deposited, rate),
        [pltpu.VMEM(out.shape, F32), pltpu.SemaphoreType.DMA((cells.shape[1],))],
        in_specs=[VMEM] * 6 + [SMEM], flops=30 << 20, moved_bytes=4 << 20,
    )


def quotient(value, count):
    return value >> (count.bit_length() - 1) if count & (count - 1) == 0 else value // count


def deposit_kernel(shape, routed_ref, out_ref, total_ref, mass_ref, spread_ref, depth_ref):
    size_x, size_y, size_z = shape
    groups = routed_ref.shape[0] // 9
    per = groups // 8
    span = LANES // per
    lane_part = quotient(iota((8, LANES), 1), span)
    for v in range(9):
        rows = routed_ref[pl.ds(v, groups, stride=9), :]
        for q in range(per):
            total = None
            for g in range(per):
                block = rows[8 * g : 8 * g + 8]
                if g != q:
                    block = pltpu.roll(block, (span * (g - q)) % LANES, 1)
                total = block if total is None else jnp.where(lane_part == g, block, total)
            mass_ref[q, v] = total

    bounds = []
    for q in range(per):
        cell = mass_ref[q, SECTIONS].astype(jnp.int32)
        layer = quotient(cell, size_y * size_z)
        valid = cell >= 0
        bounds.append((jnp.min(jnp.where(valid, layer, size_x)), jnp.max(jnp.where(valid, layer, -1))))

    half = SECTIONS * WINDOW * size_y
    zero = jnp.zeros((size_y, LANES), BF16)

    def spread(q, first):
        cell = mass_ref[q, SECTIONS].astype(jnp.int32)
        plane = quotient(cell, size_z)
        depth = cell - plane * size_z
        plane = jnp.where(cell >= 0, plane - first * size_y, -1).astype(F32)
        parts = [split(mass_ref[q, s]) for s in range(SECTIONS)]
        for i in range(8):
            at = slice(i * LANES, (i + 1) * LANES)
            depth_ref[q % 2, :, at] = hot_columns(depth[i : i + 1], size_z)
            plane_rows = rows_of(plane[i : i + 1], size_y)
            rows = [[rows_of(part[i : i + 1].astype(F32), size_y) for part in pair] for pair in parts]
            for w in range(WINDOW):
                hit = plane_rows == packed(iota((size_y, LANES), 0) + w * size_y)
                for s in range(SECTIONS):
                    base = (s * WINDOW + w) * size_y
                    for part in range(2):
                        spread_ref[q % 2, part * half + base : part * half + base + size_y, at] = jnp.where(
                            hit, rows[s][part], zero
                        )

    def deposit(q, first):
        added = contract_lanes(spread_ref[q % 2], depth_ref[q % 2])
        for s in range(SECTIONS):
            base = s * WINDOW * size_y
            rows = added[base : base + WINDOW * size_y] + added[half + base : half + base + WINDOW * size_y]
            at = pl.ds(first, WINDOW)
            total_ref[s, at] = total_ref[s, at] + rows.reshape(WINDOW, size_y, size_z)

    total_ref[...] = jnp.zeros(total_ref.shape, F32)
    for q in range(per):
        first = jnp.minimum(bounds[q][0], size_x - 1)
        spread(q, first)
        deposit(q, first)
    for q in range(per):
        low, high = bounds[q]

        def more(t, unused, q=q, low=low):
            first = low + t * WINDOW
            spread(q, first)
            deposit(q, first)
            return unused

        lax.fori_loop(1, quotient(high - low + WINDOW, WINDOW), more, 0)
    out_ref[...] = total_ref[:, 0:size_x]


def deposit(routed, shape):
    size_x, size_y, size_z = shape
    per = routed.shape[0] // 9 // 8
    return call(
        functools.partial(deposit_kernel, shape), jax.ShapeDtypeStruct((SECTIONS,) + shape, F32), (routed,),
        [
            pltpu.VMEM((SECTIONS, size_x + WINDOW - 1, size_y, size_z), F32),
            pltpu.VMEM((per, SECTIONS + 1, 8, LANES), F32),
            pltpu.VMEM((2, 2 * SECTIONS * WINDOW * size_y, 8 * LANES), BF16),
            pltpu.VMEM((2, size_z, 8 * LANES), BF16),
        ],
        in_specs=[VMEM], out_specs=VMEM, flops=4 << 30, moved_bytes=2 << 20,
    )


def ring(size):
    up = [(i, (i + 1) % size) for i in range(size)]
    return up, [(j, i) for i, j in up]


def on_device(cell_state, evap_rate, parcels, crossing, conv_mass, conv_owner, conv_cell):
    owner_total = lax.axis_size("gx") * lax.axis_size("gy")
    row_total = conv_owner.shape[0]
    capacity = 2 * row_total // owner_total
    up_x, down_x = ring(lax.axis_size("gx"))
    up_y, down_y = ring(lax.axis_size("gy"))

    send_up, send_down, side_up, side_down, advanced, hot, filled = prepare(
        cell_state, parcels, crossing, conv_mass, conv_owner.reshape(-1, LANES), conv_cell.reshape(-1, LANES),
        owner_total, capacity,
    )
    before = lax.ppermute(send_up, "gx", up_x)
    after = lax.ppermute(send_down, "gx", down_x)
    low = lax.ppermute(side_up, "gy", up_y)
    high = lax.ppermute(side_down, "gy", down_y)

    fold = LANES // capacity
    filled = filled.reshape(-1, 9, fold, capacity).transpose(0, 2, 1, 3).reshape(owner_total, 1, 9 * capacity)
    routed = lax.all_to_all(filled, ("gx", "gy"), split_axis=0, concat_axis=0, tiled=True)
    routed = routed.reshape(-1, fold, 9, capacity).transpose(0, 2, 1, 3).reshape(-1, LANES)

    deposited = deposit(routed, cell_state.shape[1:])
    new_parcels = arrive(deposited, advanced, hot, crossing, before, after)
    new_cells = update_cells(cell_state, before, after, low, high, deposited, evap_rate)
    return (new_cells, new_parcels)


def solution(mesh):
    in_specs = (
        P(None, "gx", "gy", None),
        P(),
        P(None, ("gx", "gy")),
        P(None, ("gx", "gy")),
        P(None, ("gx", "gy")),
        P(("gx", "gy"), None),
        P(("gx", "gy")),
    )
    out_specs = (P(None, "gx", "gy", None), P(None, ("gx", "gy")))
    return jax.shard_map(
        on_device, mesh=mesh, in_specs=in_specs, out_specs=out_specs, check_vma=False
    )
```

```python
import functools

import jax
import jax.numpy as jnp
from jax import lax
from jax.experimental import pallas as pl
from jax.experimental.pallas import tpu as pltpu
from jax.sharding import PartitionSpec as P

SECTIONS = 8
SPECIES = 6
COUNT = SECTIONS + SPECIES
LANES = 128
WIDE = 256
WINDOW = 4
F32 = jnp.float32
BF16 = jnp.bfloat16
ANY = pl.BlockSpec(memory_space=pl.ANY)
SMEM = pl.BlockSpec(memory_space=pltpu.SMEM)
VMEM = pl.BlockSpec(memory_space=pltpu.VMEM)
ALL = 63 << 20
MOST = 32 << 20


def call(kernel, out_shape, operands, scratch, in_specs=None, out_specs=ANY, flops=0, moved_bytes=0, grant=MOST):
    many = isinstance(out_shape, (list, tuple))
    return pl.pallas_call(
        kernel,
        out_shape=out_shape,
        in_specs=in_specs or [ANY] * len(operands),
        out_specs=[out_specs] * len(out_shape) if many else out_specs,
        scratch_shapes=scratch,
        compiler_params=pltpu.CompilerParams(vmem_limit_bytes=grant),
        cost_estimate=pl.CostEstimate(flops=flops, bytes_accessed=moved_bytes, transcendentals=0),
    )(*operands)


def iota(shape, axis):
    return lax.broadcasted_iota(jnp.int32, shape, axis)


def packed(value):
    return value.astype(F32).astype(BF16)


def split(value):
    coarse = value.astype(BF16)
    return coarse, (value - coarse.astype(F32)).astype(BF16)


def rows_of(row, count):
    return jnp.broadcast_to(row, (count, row.shape[1])).astype(BF16)


def hot_columns(lower, count):
    return jnp.where(rows_of(lower.astype(F32), count) == packed(iota((count, LANES), 0)), 1.0, 0.0).astype(BF16)


def contract_lanes(left, right):
    return lax.dot_general(left, right, (((1,), (1,)), ((), ())), preferred_element_type=F32)


def advance_block(block):
    row = iota(block.shape, 0)
    diameter = jnp.broadcast_to(block[6:7], block.shape)
    warmth = jnp.broadcast_to(block[7:8], block.shape)
    factor = 0.8 / (1.0 + diameter * diameter)
    slowed = block * (1.0 - factor)
    travel = pltpu.roll(0.5 * (block + slowed), 5, 0)
    shrunk = block * (1.0 - 0.05 * warmth)
    warmed = block + factor * (1.0 - block)
    return jnp.where(row < 3, block + travel, jnp.where(row < 6, slowed, jnp.where(row == 6, shrunk, warmed)))


def scatter_left(left_ref, at, upper, uppers, coarse, fine):
    upper = rows_of(upper.astype(F32), 16)
    twice_coarse = jnp.concatenate([coarse.astype(F32)] * 2, axis=0).astype(BF16)
    twice_fine = jnp.concatenate([fine.astype(F32)] * 2, axis=0).astype(BF16)
    zero = jnp.zeros((16, LANES), BF16)
    pair = iota((16, LANES), 0) // 8
    for u in range(0, uppers, 2):
        hit = upper == packed(pair + u)
        left_ref[8 * u : 8 * u + 16, at] = jnp.where(hit, twice_coarse, zero)
        left_ref[8 * (uppers + u) : 8 * (uppers + u) + 16, at] = jnp.where(hit, twice_fine, zero)


def bucket_into(owner_total, capacity, mass_ref, owner_ref, cell_ref, out_ref, left_ref, hot_ref):
    blocks = owner_ref.shape[0]
    uppers = out_ref.shape[0] // 9 // 2
    strict = iota((LANES, 2 * LANES), 0) < iota((LANES, 2 * LANES), 1)
    strict = jnp.where(strict, 1.0, 0.0).astype(BF16)
    owners = owner_ref[...]
    cells = cell_ref[...]
    hots = [
        jnp.where(jnp.broadcast_to(owners[b : b + 1], (owner_total, LANES)) == iota((owner_total, LANES), 0), 1.0, 0.0)
        for b in range(blocks)
    ]
    ranks = jnp.dot(jnp.concatenate(hots, axis=0).astype(BF16), strict, preferred_element_type=F32)
    carry = jnp.zeros((owner_total, LANES), F32)
    base = 16 * uppers
    for b in range(blocks):
        part = ranks[b * owner_total : (b + 1) * owner_total]
        rank = jnp.sum(hots[b] * (part[:, :LANES] + carry), axis=0, keepdims=True).astype(jnp.int32)
        carry = carry + part[:, LANES:]
        spot = owners[b : b + 1] * capacity + rank
        at = slice(b * LANES, (b + 1) * LANES)
        hot_ref[:, at] = hot_columns(spot & (WIDE - 1), WIDE)
        coarse, fine = split(mass_ref[:, at])
        upper = spot >> 8
        scatter_left(left_ref, at, upper, uppers, coarse, fine)
        hit = rows_of(upper.astype(F32), uppers) == packed(iota((uppers, LANES), 0))
        zero = jnp.zeros((uppers, LANES), BF16)
        cell = cells[b : b + 1]
        left_ref[base : base + uppers, at] = jnp.where(hit, rows_of((cell >> 8).astype(F32), uppers), zero)
        left_ref[base + uppers : base + 2 * uppers, at] = jnp.where(
            hit, rows_of((cell & (WIDE - 1)).astype(F32), uppers), zero
        )
        left_ref[base + 2 * uppers : base + 3 * uppers, at] = jnp.where(hit, 1.0, 0.0).astype(BF16)
    placed = contract_lanes(left_ref[...], hot_ref[...])
    cell = placed[base : base + uppers] * float(WIDE) + placed[base + uppers : base + 2 * uppers]
    cell = jnp.where(placed[base + 2 * uppers : base + 3 * uppers] > 0.5, cell, -1.0)
    for u in range(uppers):
        mass = placed[8 * u : 8 * u + 8] + placed[8 * (uppers + u) : 8 * (uppers + u) + 8]
        for half in range(2):
            row = 9 * (2 * u + half)
            lanes = slice(half * LANES, (half + 1) * LANES)
            out_ref[row : row + 8, :] = mass[:, lanes]
            out_ref[row + 8 : row + 9, :] = cell[u : u + 1, lanes]


def prepare_kernel(
    owner_total, capacity,
    cells_hbm, parcels_hbm, crossing_hbm, mass_hbm, owner_hbm, cell_hbm,
    up_hbm, down_hbm, yup_hbm, ydown_hbm, advanced_hbm, hot_hbm, filled_hbm,
    cells_ref, parcels_ref, crossing_ref, mass_ref, owner_ref, cell_ref,
    leave_ref, yup_ref, ydown_ref, advanced_ref, hot_ref, filled_ref,
    parts_ref, left_ref, spot_ref, sems,
):
    size_x, size_y, size_z = cells_hbm.shape[1:]
    face = slice(0, COUNT + 1)
    tail = slice(COUNT + 1, up_hbm.shape[0])
    pairs = [
        (crossing_hbm, crossing_ref),
        (owner_hbm, owner_ref),
        (cell_hbm, cell_ref),
        (mass_hbm, mass_ref),
        (parcels_hbm, parcels_ref),
        (cells_hbm, cells_ref),
        (cells_ref.at[face, size_x - 1], up_hbm.at[face]),
        (cells_ref.at[face, 0], down_hbm.at[face]),
        (filled_ref, filled_hbm),
        (hot_ref, hot_hbm),
        (advanced_ref, advanced_hbm),
        (leave_ref.at[0], up_hbm.at[tail]),
        (leave_ref.at[1], down_hbm.at[tail]),
        (yup_ref, yup_hbm),
        (ydown_ref, ydown_hbm),
    ]
    copies = [pltpu.make_async_copy(source, target, sems.at[i]) for i, (source, target) in enumerate(pairs)]
    for copy in copies[:6]:
        copy.start()
    cross = crossing_ref.shape[1]
    slot_total = parcels_ref.shape[1]
    copies[0].wait()
    for side in range(2):
        for first in range(0, cross, LANES):
            lower = crossing_ref[side : side + 1, first : first + LANES] & (WIDE - 1)
            hot_ref[:, side * cross + first : side * cross + first + LANES] = hot_columns(lower, WIDE)
    copies[9].start()
    copies[4].wait()

    def advance_pair(i, unused):
        for number in range(2):
            blocks = []
            for half in range(2):
                at = pl.ds(pl.multiple_of((4 * i + 2 * number + half) * LANES, LANES), LANES)
                block = advance_block(parcels_ref[:, at])
                advanced_ref[:, at] = block
                blocks.append(block)
            parts_ref[pl.ds(pl.multiple_of((2 * i + number) * 8, 8), 8), :] = jnp.concatenate(blocks, axis=1)
        return unused

    lax.fori_loop(0, slot_total // (4 * LANES), advance_pair, 0, unroll=4)
    copies[10].start()

    halves_y, halves_z = size_y // 8, size_z // LANES
    part_rows = parts_ref.shape[0]
    step_rows = min(256, part_rows)
    for rows in range(0, part_rows, step_rows):
        coarse, fine = split(parts_ref[rows : rows + step_rows])
        for side in range(2):
            for first in range(0, cross, WIDE):
                upper = jnp.broadcast_to(crossing_ref[side : side + 1, first : first + WIDE] >> 8, (8, WIDE))
                hot = hot_ref[:, side * cross + first : side * cross + first + WIDE]
                picked = jnp.dot(coarse, hot, preferred_element_type=F32) + jnp.dot(
                    fine, hot, preferred_element_type=F32
                )
                spots = []
                for offset in range(0, WIDE, LANES):
                    layer, rest = divmod((first + offset) // LANES, halves_y * halves_z)
                    half_y, half_z = divmod(rest, halves_z)
                    spots.append((side, layer, slice(8 * half_y, 8 * half_y + 8), slice(LANES * half_z, LANES * (half_z + 1))))
                if rows:
                    total = jnp.concatenate([leave_ref[spot] for spot in spots], axis=1)
                else:
                    total = jnp.zeros((8, WIDE), F32)
                for i in range(0, step_rows, 8):
                    total = jnp.where(upper == (rows + i) // 8, picked[i : i + 8], total)
                for number, spot in enumerate(spots):
                    leave_ref[spot] = total[:, number * LANES : (number + 1) * LANES]
    copies[11].start()
    copies[12].start()

    copies[5].wait()
    copies[6].start()
    copies[7].start()
    for c in range(COUNT + 1):
        source = c if c < COUNT else COUNT + 1
        yup_ref[c] = cells_ref[source, :, size_y - 1, :]
        ydown_ref[c] = cells_ref[source, :, 0, :]
    copies[13].start()
    copies[14].start()
    for copy in copies[1:4]:
        copy.wait()
    bucket_into(owner_total, capacity, mass_ref, owner_ref, cell_ref, filled_ref, left_ref, spot_ref)
    copies[8].start()
    for copy in copies[6:]:
        copy.wait()


def prepare(cells, parcels, crossing, mass, owner, cell, owner_total, capacity):
    size_x, size_y, size_z = cells.shape[1:]
    extra = 8 * crossing.shape[1] // (size_y * size_z)
    places = owner_total * capacity
    shape = jax.ShapeDtypeStruct
    face = shape((COUNT + 1 + extra, size_y, size_z), F32)
    side = shape((COUNT + 1, size_x, size_z), F32)
    advanced = shape(parcels.shape, F32)
    hot = shape((WIDE, crossing.size), BF16)
    filled = shape((9 * places // LANES, LANES), F32)
    operands = (cells, parcels, crossing, mass, owner, cell)
    scratch = [pltpu.VMEM(a.shape, a.dtype) for a in operands]
    scratch += [pltpu.VMEM((2, extra, size_y, size_z), F32)]
    scratch += [pltpu.VMEM(a.shape, a.dtype) for a in (side, side, advanced, hot, filled)]
    scratch += [
        pltpu.VMEM((8 * parcels.shape[1] // WIDE, WIDE), F32),
        pltpu.VMEM((19 * places // WIDE, mass.shape[1]), BF16),
        pltpu.VMEM((WIDE, mass.shape[1]), BF16),
        pltpu.SemaphoreType.DMA((15,)),
    ]
    return call(
        functools.partial(prepare_kernel, owner_total, capacity),
        [face, face, side, side, advanced, hot, filled], operands, scratch,
        flops=2 << 30, moved_bytes=6 << 20, grant=ALL,
    )


def arrive_kernel(unused, advanced_ref, hot_ref, crossing_ref, before_ref, after_ref, out_hbm, out_ref, left_ref, sems):
    cross = crossing_ref.shape[1]
    uppers = advanced_ref.shape[1] // WIDE
    size_y, size_z = before_ref.shape[1:]
    halves_y, halves_z = size_y // 8, size_z // LANES
    for side, come_ref in ((0, before_ref), (1, after_ref)):
        for first in range(0, cross, LANES):
            layer, rest = divmod(first // LANES, halves_y * halves_z)
            half_y, half_z = divmod(rest, halves_z)
            block = come_ref[COUNT + 1 + layer, 8 * half_y : 8 * half_y + 8, LANES * half_z : LANES * (half_z + 1)]
            coarse, fine = split(block)
            upper = crossing_ref[side : side + 1, first : first + LANES] >> 8
            at = slice(side * cross + first, side * cross + first + LANES)
            scatter_left(left_ref, at, upper, uppers, coarse, fine)
            hit = rows_of(upper.astype(F32), uppers) == packed(iota((uppers, LANES), 0))
            left_ref[16 * uppers :, at] = jnp.where(hit, 1.0, 0.0).astype(BF16)
    hit = contract_lanes(left_ref[16 * uppers :], hot_ref[...])
    step = min(32, uppers)
    outs = []
    for u in range(0, uppers, step):
        total = contract_lanes(left_ref[8 * u : 8 * (u + step)], hot_ref[...]) + contract_lanes(
            left_ref[8 * (uppers + u) : 8 * (uppers + u + step)], hot_ref[...]
        )
        for i in range(step):
            at = slice((u + i) * WIDE, (u + i + 1) * WIDE)
            taken = jnp.broadcast_to(hit[u + i : u + i + 1], (8, WIDE)) > 0.5
            out_ref[:, at] = jnp.where(taken, total[8 * i : 8 * i + 8], advanced_ref[:, at])
        at = slice(u * WIDE, (u + step) * WIDE)
        out = pltpu.make_async_copy(out_ref.at[:, at], out_hbm.at[:, at], sems.at[len(outs)])
        out.start()
        outs.append(out)
    for out in outs:
        out.wait()


def arrive(earlier, advanced, hot, crossing, before, after):
    uppers = advanced.shape[1] // WIDE
    return call(
        arrive_kernel, jax.ShapeDtypeStruct(advanced.shape, F32), (earlier, advanced, hot, crossing, before, after),
        [
            pltpu.VMEM(advanced.shape, F32),
            pltpu.VMEM((17 * uppers, crossing.size), BF16),
            pltpu.SemaphoreType.DMA((-(-uppers // 32),)),
        ],
        in_specs=[ANY] + [VMEM] * 5, flops=1 << 30, moved_bytes=3 << 20,
    )


def shift_up(value, axis):
    return pltpu.roll(value, value.shape[axis] - 1, axis)


def shift_down(value, axis):
    return pltpu.roll(value, 1, axis)


def slab_update(left, center, right, side_low, side_high, rate_ref, write):
    course = center(COUNT)
    size_y, size_z = course.shape
    first_row = iota((size_y, size_z), 0) == 0
    last_row = iota((size_y, size_z), 0) == size_y - 1

    def row_up(value, edge):
        return jnp.where(last_row, edge, shift_up(value, 0))

    def row_down(value, edge):
        return jnp.where(first_row, edge, shift_down(value, 0))

    face_x = 0.5 * (course + right(COUNT))
    face_x_low = 0.5 * (left(COUNT) + course)
    course_y = center(COUNT + 1)
    face_y = 0.5 * (course_y + row_up(course_y, side_high(COUNT)))
    face_y_low = 0.5 * (row_down(course_y, side_low(COUNT)) + course_y)
    course_z = center(COUNT + 2)
    lane = iota((size_y, size_z), 1)
    face_z = jnp.where(lane == size_z - 1, 0.0, 0.5 * (course_z + shift_up(course_z, 1)))
    face_z_low = jnp.where(lane == 0, 0.0, 0.5 * (shift_down(course_z, 1) + course_z))
    from_x_up, from_x_low = jnp.minimum(face_x, 0.0), jnp.maximum(face_x_low, 0.0)
    from_y_up, from_y_low = jnp.minimum(face_y, 0.0), jnp.maximum(face_y_low, 0.0)
    from_z_up, from_z_low = jnp.minimum(face_z, 0.0), jnp.maximum(face_z_low, 0.0)
    own = 1.0 - (
        (jnp.maximum(face_x, 0.0) - jnp.minimum(face_x_low, 0.0))
        + (jnp.maximum(face_y, 0.0) - jnp.minimum(face_y_low, 0.0))
        + (jnp.maximum(face_z, 0.0) - jnp.minimum(face_z_low, 0.0))
    )

    def moved(c):
        amount = center(c)
        total = own * amount
        total = total - from_x_up * right(c) + from_x_low * left(c)
        total = total - from_y_up * row_up(amount, side_high(c)) + from_y_low * row_down(amount, side_low(c))
        return total - from_z_up * shift_up(amount, 1) + from_z_low * shift_down(amount, 1)

    vapour = moved(SECTIONS)
    beside = 1.0 + vapour
    later = None
    gained = None
    for s in reversed(range(SECTIONS)):
        section = moved(s)
        loss = rate_ref[s] * section / beside
        value = section - loss
        if later is not None:
            value = value + 0.5 * later
            gained = later if gained is None else gained + later
        write(s, value)
        later = loss
    write(SECTIONS, vapour + later + 0.5 * gained)
    for c in range(SECTIONS + 1, COUNT):
        write(c, moved(c))


def cells_kernel(
    cells_ref, before_ref, after_ref, low_ref, high_ref, deposit_ref, rate_ref, out_hbm, out_ref, sems
):
    size_x = cells_ref.shape[1]
    last = size_x - 1

    def store(x):
        return pltpu.make_async_copy(out_ref.at[:, x], out_hbm.at[:, x], sems.at[x])

    def layer(left, x, right):
        def write(c, value):
            out_ref[c, x] = value + deposit_ref[c, x] if c < SECTIONS else value

        slab_update(
            left,
            lambda c: cells_ref[c, x],
            right,
            lambda c: low_ref[c, pl.ds(x, 1), :],
            lambda c: high_ref[c, pl.ds(x, 1), :],
            rate_ref,
            write,
        )
        store(x).start()

    def middle(x, unused):
        layer(lambda c: cells_ref[c, x - 1], x, lambda c: cells_ref[c, x + 1])
        return unused

    lax.fori_loop(1, last, middle, 0)
    layer(lambda c: before_ref[c], 0, lambda c: cells_ref[c, 1])
    layer(lambda c: cells_ref[c, last - 1], last, lambda c: after_ref[c])
    for x in range(size_x):
        store(x).wait()


def update_cells(cells, before, after, low, high, deposited, rate):
    out = jax.ShapeDtypeStruct((COUNT,) + cells.shape[1:], F32)
    return call(
        cells_kernel, out, (cells, before, after, low, high, deposited, rate),
        [pltpu.VMEM(out.shape, F32), pltpu.SemaphoreType.DMA((cells.shape[1],))],
        in_specs=[VMEM] * 6 + [SMEM], flops=30 << 20, moved_bytes=4 << 20,
    )


def quotient(value, count):
    return value >> (count.bit_length() - 1) if count & (count - 1) == 0 else value // count


def deposit_kernel(shape, routed_ref, out_ref, total_ref, mass_ref, spread_ref, depth_ref):
    size_x, size_y, size_z = shape
    groups = routed_ref.shape[0] // 9
    per = groups // 8
    span = LANES // per
    lane_part = quotient(iota((8, LANES), 1), span)
    for v in range(9):
        rows = routed_ref[pl.ds(v, groups, stride=9), :]
        for q in range(per):
            total = None
            for g in range(per):
                block = rows[8 * g : 8 * g + 8]
                if g != q:
                    block = pltpu.roll(block, (span * (g - q)) % LANES, 1)
                total = block if total is None else jnp.where(lane_part == g, block, total)
            mass_ref[q, v] = total

    bounds = []
    for q in range(per):
        cell = mass_ref[q, SECTIONS].astype(jnp.int32)
        layer = quotient(cell, size_y * size_z)
        valid = cell >= 0
        bounds.append((jnp.min(jnp.where(valid, layer, size_x)), jnp.max(jnp.where(valid, layer, -1))))

    half = SECTIONS * WINDOW * size_y
    zero = jnp.zeros((size_y, LANES), BF16)

    def spread(q, first):
        cell = mass_ref[q, SECTIONS].astype(jnp.int32)
        plane = quotient(cell, size_z)
        depth = cell - plane * size_z
        plane = jnp.where(cell >= 0, plane - first * size_y, -1).astype(F32)
        parts = [split(mass_ref[q, s]) for s in range(SECTIONS)]
        for i in range(8):
            at = slice(i * LANES, (i + 1) * LANES)
            depth_ref[q % 2, :, at] = hot_columns(depth[i : i + 1], size_z)
            plane_rows = rows_of(plane[i : i + 1], size_y)
            rows = [[rows_of(part[i : i + 1].astype(F32), size_y) for part in pair] for pair in parts]
            for w in range(WINDOW):
                hit = plane_rows == packed(iota((size_y, LANES), 0) + w * size_y)
                for s in range(SECTIONS):
                    base = (s * WINDOW + w) * size_y
                    for part in range(2):
                        spread_ref[q % 2, part * half + base : part * half + base + size_y, at] = jnp.where(
                            hit, rows[s][part], zero
                        )

    def deposit(q, first):
        added = contract_lanes(spread_ref[q % 2], depth_ref[q % 2])
        for s in range(SECTIONS):
            base = s * WINDOW * size_y
            rows = added[base : base + WINDOW * size_y] + added[half + base : half + base + WINDOW * size_y]
            at = pl.ds(first, WINDOW)
            total_ref[s, at] = total_ref[s, at] + rows.reshape(WINDOW, size_y, size_z)

    total_ref[...] = jnp.zeros(total_ref.shape, F32)
    for q in range(per):
        first = jnp.minimum(bounds[q][0], size_x - 1)
        spread(q, first)
        deposit(q, first)
    for q in range(per):
        low, high = bounds[q]

        def more(t, unused, q=q, low=low):
            first = low + t * WINDOW
            spread(q, first)
            deposit(q, first)
            return unused

        lax.fori_loop(1, quotient(high - low + WINDOW, WINDOW), more, 0)
    out_ref[...] = total_ref[:, 0:size_x]


def deposit(routed, shape):
    size_x, size_y, size_z = shape
    per = routed.shape[0] // 9 // 8
    return call(
        functools.partial(deposit_kernel, shape), jax.ShapeDtypeStruct((SECTIONS,) + shape, F32), (routed,),
        [
            pltpu.VMEM((SECTIONS, size_x + WINDOW - 1, size_y, size_z), F32),
            pltpu.VMEM((per, SECTIONS + 1, 8, LANES), F32),
            pltpu.VMEM((2, 2 * SECTIONS * WINDOW * size_y, 8 * LANES), BF16),
            pltpu.VMEM((2, size_z, 8 * LANES), BF16),
        ],
        in_specs=[VMEM], out_specs=VMEM, flops=0, moved_bytes=0,
    )


def ring(size):
    up = [(i, (i + 1) % size) for i in range(size)]
    return up, [(j, i) for i, j in up]


def exchange(rows):
    return lax.all_to_all(rows, ("gx", "gy"), split_axis=0, concat_axis=0, tiled=True)


def exchange_by_axis(rows):
    grid = rows.reshape(lax.axis_size("gx"), lax.axis_size("gy"), rows.shape[2])
    grid = lax.all_to_all(grid, "gx", split_axis=0, concat_axis=0, tiled=True)
    return lax.all_to_all(grid, "gy", split_axis=1, concat_axis=1, tiled=True).reshape(rows.shape)


def on_device(cell_state, evap_rate, parcels, crossing, conv_mass, conv_owner, conv_cell):
    owner_total = lax.axis_size("gx") * lax.axis_size("gy")
    row_total = conv_owner.shape[0]
    capacity = 2 * row_total // owner_total
    up_x, down_x = ring(lax.axis_size("gx"))
    up_y, down_y = ring(lax.axis_size("gy"))

    send_up, send_down, side_up, side_down, advanced, hot, filled = prepare(
        cell_state, parcels, crossing, conv_mass, conv_owner.reshape(-1, LANES), conv_cell.reshape(-1, LANES),
        owner_total, capacity,
    )
    before = lax.ppermute(send_up, "gx", up_x)
    after = lax.ppermute(send_down, "gx", down_x)
    low = lax.ppermute(side_up, "gy", up_y)
    high = lax.ppermute(side_down, "gy", down_y)

    fold = LANES // capacity
    filled = filled.reshape(-1, 9, fold, capacity).transpose(0, 2, 1, 3).reshape(owner_total, 1, 9 * capacity)
    routed = lax.cond(crossing[0, 0] >= 0, exchange, exchange_by_axis, filled)
    routed = routed.reshape(-1, fold, 9, capacity).transpose(0, 2, 1, 3).reshape(-1, LANES)

    deposited = deposit(routed, cell_state.shape[1:])
    new_parcels = arrive(deposited, advanced, hot, crossing, before, after)
    new_cells = update_cells(cell_state, before, after, low, high, deposited, evap_rate)
    return (new_cells, new_parcels)


def solution(mesh):
    in_specs = (
        P(None, "gx", "gy", None),
        P(),
        P(None, ("gx", "gy")),
        P(None, ("gx", "gy")),
        P(None, ("gx", "gy")),
        P(("gx", "gy"), None),
        P(("gx", "gy")),
    )
    out_specs = (P(None, "gx", "gy", None), P(None, ("gx", "gy")))
    return jax.shard_map(
        on_device, mesh=mesh, in_specs=in_specs, out_specs=out_specs, check_vma=False
    )
```

```python
import functools

import jax
import jax.numpy as jnp
from jax import lax
from jax.experimental import pallas as pl
from jax.experimental.pallas import tpu as pltpu
from jax.sharding import PartitionSpec as P

SECTIONS = 8
SPECIES = 6
COUNT = SECTIONS + SPECIES
LANES = 128
WIDE = 256
F32 = jnp.float32
BF16 = jnp.bfloat16
ANY = pl.BlockSpec(memory_space=pl.ANY)
SMEM = pl.BlockSpec(memory_space=pltpu.SMEM)
VMEM = pl.BlockSpec(memory_space=pltpu.VMEM)
ALL = 63 << 20
MOST = 32 << 20


def call(kernel, out_shape, operands, scratch, in_specs=None, out_specs=ANY, flops=0, moved_bytes=0, grant=MOST):
    many = isinstance(out_shape, (list, tuple))
    return pl.pallas_call(
        kernel,
        out_shape=out_shape,
        in_specs=in_specs or [ANY] * len(operands),
        out_specs=[out_specs] * len(out_shape) if many else out_specs,
        scratch_shapes=scratch,
        compiler_params=pltpu.CompilerParams(vmem_limit_bytes=grant),
        cost_estimate=pl.CostEstimate(flops=flops, bytes_accessed=moved_bytes, transcendentals=0),
    )(*operands)


def iota(shape, axis):
    return lax.broadcasted_iota(jnp.int32, shape, axis)


def packed(value):
    return value.astype(F32).astype(BF16)


def split(value):
    coarse = value.astype(BF16)
    return coarse, (value - coarse.astype(F32)).astype(BF16)


def rows_of(row, count):
    return jnp.broadcast_to(row, (count, row.shape[1])).astype(BF16)


def hot_columns(lower, count):
    return jnp.where(rows_of(lower.astype(F32), count) == packed(iota((count, LANES), 0)), 1.0, 0.0).astype(BF16)


def contract_lanes(left, right):
    return lax.dot_general(left, right, (((1,), (1,)), ((), ())), preferred_element_type=F32)


def advance_block(block):
    row = iota(block.shape, 0)
    diameter = jnp.broadcast_to(block[6:7], block.shape)
    warmth = jnp.broadcast_to(block[7:8], block.shape)
    factor = 0.8 / (1.0 + diameter * diameter)
    slowed = block * (1.0 - factor)
    travel = pltpu.roll(0.5 * (block + slowed), 5, 0)
    shrunk = block * (1.0 - 0.05 * warmth)
    warmed = block + factor * (1.0 - block)
    return jnp.where(row < 3, block + travel, jnp.where(row < 6, slowed, jnp.where(row == 6, shrunk, warmed)))


def scatter_left(left_ref, at, upper, uppers, coarse, fine):
    upper = rows_of(upper.astype(F32), 16)
    twice_coarse = jnp.concatenate([coarse.astype(F32)] * 2, axis=0).astype(BF16)
    twice_fine = jnp.concatenate([fine.astype(F32)] * 2, axis=0).astype(BF16)
    zero = jnp.zeros((16, LANES), BF16)
    pair = iota((16, LANES), 0) // 8
    for u in range(0, uppers, 2):
        hit = upper == packed(pair + u)
        left_ref[8 * u : 8 * u + 16, at] = jnp.where(hit, twice_coarse, zero)
        left_ref[8 * (uppers + u) : 8 * (uppers + u) + 16, at] = jnp.where(hit, twice_fine, zero)


def bucket_into(owner_total, capacity, mass_ref, owner_ref, cell_ref, out_ref, left_ref, hot_ref):
    blocks = owner_ref.shape[0]
    uppers = out_ref.shape[0] // 9 // 2
    strict = iota((LANES, 2 * LANES), 0) < iota((LANES, 2 * LANES), 1)
    strict = jnp.where(strict, 1.0, 0.0).astype(BF16)
    owners = owner_ref[...]
    cells = cell_ref[...]
    hots = [
        jnp.where(jnp.broadcast_to(owners[b : b + 1], (owner_total, LANES)) == iota((owner_total, LANES), 0), 1.0, 0.0)
        for b in range(blocks)
    ]
    ranks = jnp.dot(jnp.concatenate(hots, axis=0).astype(BF16), strict, preferred_element_type=F32)
    carry = jnp.zeros((owner_total, LANES), F32)
    base = 16 * uppers
    for b in range(blocks):
        part = ranks[b * owner_total : (b + 1) * owner_total]
        rank = jnp.sum(hots[b] * (part[:, :LANES] + carry), axis=0, keepdims=True).astype(jnp.int32)
        carry = carry + part[:, LANES:]
        spot = owners[b : b + 1] * capacity + rank
        at = slice(b * LANES, (b + 1) * LANES)
        hot_ref[:, at] = hot_columns(spot & (WIDE - 1), WIDE)
        coarse, fine = split(mass_ref[:, at])
        upper = spot >> 8
        scatter_left(left_ref, at, upper, uppers, coarse, fine)
        hit = rows_of(upper.astype(F32), uppers) == packed(iota((uppers, LANES), 0))
        zero = jnp.zeros((uppers, LANES), BF16)
        cell = cells[b : b + 1]
        left_ref[base : base + uppers, at] = jnp.where(hit, rows_of((cell >> 8).astype(F32), uppers), zero)
        left_ref[base + uppers : base + 2 * uppers, at] = jnp.where(
            hit, rows_of((cell & (WIDE - 1)).astype(F32), uppers), zero
        )
        left_ref[base + 2 * uppers : base + 3 * uppers, at] = jnp.where(hit, 1.0, 0.0).astype(BF16)
    placed = contract_lanes(left_ref[...], hot_ref[...])
    cell = placed[base : base + uppers] * float(WIDE) + placed[base + uppers : base + 2 * uppers]
    cell = jnp.where(placed[base + 2 * uppers : base + 3 * uppers] > 0.5, cell, -1.0)
    for u in range(uppers):
        mass = placed[8 * u : 8 * u + 8] + placed[8 * (uppers + u) : 8 * (uppers + u) + 8]
        for half in range(2):
            row = 9 * (2 * u + half)
            lanes = slice(half * LANES, (half + 1) * LANES)
            out_ref[row : row + 8, :] = mass[:, lanes]
            out_ref[row + 8 : row + 9, :] = cell[u : u + 1, lanes]


def prepare_kernel(
    cells_hbm, parcels_hbm, crossing_hbm, up_hbm, down_hbm, yup_hbm, ydown_hbm, advanced_hbm, hot_hbm,
    cells_ref, parcels_ref, crossing_ref, leave_ref, yup_ref, ydown_ref, advanced_ref, hot_ref, parts_ref, sems,
):
    size_x, size_y, size_z = cells_hbm.shape[1:]
    face = slice(0, COUNT + 1)
    tail = slice(COUNT + 1, up_hbm.shape[0])
    pairs = [
        (crossing_hbm, crossing_ref),
        (parcels_hbm, parcels_ref),
        (cells_hbm, cells_ref),
        (cells_ref.at[face, size_x - 1], up_hbm.at[face]),
        (cells_ref.at[face, 0], down_hbm.at[face]),
        (yup_ref, yup_hbm),
        (ydown_ref, ydown_hbm),
        (hot_ref, hot_hbm),
        (advanced_ref, advanced_hbm),
        (leave_ref.at[0], up_hbm.at[tail]),
        (leave_ref.at[1], down_hbm.at[tail]),
    ]
    copies = [pltpu.make_async_copy(source, target, sems.at[i]) for i, (source, target) in enumerate(pairs)]
    for copy in copies[:3]:
        copy.start()
    cross = crossing_ref.shape[1]
    slot_total = parcels_ref.shape[1]
    copies[0].wait()
    for side in range(2):
        for first in range(0, cross, LANES):
            lower = crossing_ref[side : side + 1, first : first + LANES] & (WIDE - 1)
            hot_ref[:, side * cross + first : side * cross + first + LANES] = hot_columns(lower, WIDE)
    copies[7].start()
    copies[1].wait()

    def advance_pair(i, unused):
        for number in range(2):
            blocks = []
            for half in range(2):
                at = pl.ds(pl.multiple_of((4 * i + 2 * number + half) * LANES, LANES), LANES)
                block = advance_block(parcels_ref[:, at])
                advanced_ref[:, at] = block
                blocks.append(block)
            parts_ref[pl.ds(pl.multiple_of((2 * i + number) * 8, 8), 8), :] = jnp.concatenate(blocks, axis=1)
        return unused

    lax.fori_loop(0, slot_total // (4 * LANES), advance_pair, 0, unroll=4)
    copies[8].start()
    copies[2].wait()
    copies[3].start()
    copies[4].start()
    for c in range(COUNT + 1):
        source = c if c < COUNT else COUNT + 1
        yup_ref[c] = cells_ref[source, :, size_y - 1, :]
        ydown_ref[c] = cells_ref[source, :, 0, :]
    copies[5].start()
    copies[6].start()

    halves_y, halves_z = size_y // 8, size_z // LANES
    part_rows = parts_ref.shape[0]
    step_rows = min(256, part_rows)
    for rows in range(0, part_rows, step_rows):
        coarse, fine = split(parts_ref[rows : rows + step_rows])
        for side in range(2):
            for first in range(0, cross, WIDE):
                upper = jnp.broadcast_to(crossing_ref[side : side + 1, first : first + WIDE] >> 8, (8, WIDE))
                hot = hot_ref[:, side * cross + first : side * cross + first + WIDE]
                picked = jnp.dot(coarse, hot, preferred_element_type=F32) + jnp.dot(
                    fine, hot, preferred_element_type=F32
                )
                spots = []
                for offset in range(0, WIDE, LANES):
                    layer, rest = divmod((first + offset) // LANES, halves_y * halves_z)
                    half_y, half_z = divmod(rest, halves_z)
                    spots.append((side, layer, slice(8 * half_y, 8 * half_y + 8), slice(LANES * half_z, LANES * (half_z + 1))))
                if rows:
                    total = jnp.concatenate([leave_ref[spot] for spot in spots], axis=1)
                else:
                    total = jnp.zeros((8, WIDE), F32)
                for i in range(0, step_rows, 8):
                    total = jnp.where(upper == (rows + i) // 8, picked[i : i + 8], total)
                for number, spot in enumerate(spots):
                    leave_ref[spot] = total[:, number * LANES : (number + 1) * LANES]
    copies[9].start()
    copies[10].start()
    for copy in copies[3:]:
        copy.wait()


def prepare(cells, parcels, crossing):
    size_x, size_y, size_z = cells.shape[1:]
    extra = 8 * crossing.shape[1] // (size_y * size_z)
    shape = jax.ShapeDtypeStruct
    face = shape((COUNT + 1 + extra, size_y, size_z), F32)
    side = shape((COUNT + 1, size_x, size_z), F32)
    advanced = shape(parcels.shape, F32)
    hot = shape((WIDE, crossing.size), BF16)
    operands = (cells, parcels, crossing)
    scratch = [pltpu.VMEM(a.shape, a.dtype) for a in operands]
    scratch += [pltpu.VMEM((2, extra, size_y, size_z), F32)]
    scratch += [pltpu.VMEM(a.shape, a.dtype) for a in (side, side, advanced, hot)]
    scratch += [pltpu.VMEM((8 * parcels.shape[1] // WIDE, WIDE), F32), pltpu.SemaphoreType.DMA((11,))]
    return call(
        prepare_kernel, [face, face, side, side, advanced, hot], operands, scratch,
        flops=1 << 30, moved_bytes=6 << 20, grant=ALL,
    )


def bucket_kernel(
    owner_total, capacity, unused, mass_hbm, owner_hbm, cell_hbm, out_hbm,
    mass_ref, owner_ref, cell_ref, out_ref, left_ref, hot_ref, sems,
):
    pairs = [(owner_hbm, owner_ref), (cell_hbm, cell_ref), (mass_hbm, mass_ref)]
    copies = [pltpu.make_async_copy(source, target, sems.at[i]) for i, (source, target) in enumerate(pairs)]
    for copy in copies:
        copy.start()
    for copy in copies:
        copy.wait()
    bucket_into(owner_total, capacity, mass_ref, owner_ref, cell_ref, out_ref, left_ref, hot_ref)
    out = pltpu.make_async_copy(out_ref, out_hbm, sems.at[3])
    out.start()
    out.wait()


def bucket(earlier, mass, owner, cell, owner_total, capacity):
    places = owner_total * capacity
    out = jax.ShapeDtypeStruct((9 * places // LANES, LANES), F32)
    return call(
        functools.partial(bucket_kernel, owner_total, capacity), out, (earlier, mass, owner, cell),
        [pltpu.VMEM(a.shape, a.dtype) for a in (mass, owner, cell, out)]
        + [
            pltpu.VMEM((19 * places // WIDE, mass.shape[1]), BF16),
            pltpu.VMEM((WIDE, mass.shape[1]), BF16),
            pltpu.SemaphoreType.DMA((4,)),
        ],
        flops=1 << 30, moved_bytes=1 << 20, grant=ALL,
    )


def arrive_kernel(advanced_ref, hot_ref, crossing_ref, before_ref, after_ref, out_hbm, out_ref, left_ref, sems):
    cross = crossing_ref.shape[1]
    uppers = advanced_ref.shape[1] // WIDE
    size_y, size_z = before_ref.shape[1:]
    halves_y, halves_z = size_y // 8, size_z // LANES
    for side, come_ref in ((0, before_ref), (1, after_ref)):
        for first in range(0, cross, LANES):
            layer, rest = divmod(first // LANES, halves_y * halves_z)
            half_y, half_z = divmod(rest, halves_z)
            block = come_ref[COUNT + 1 + layer, 8 * half_y : 8 * half_y + 8, LANES * half_z : LANES * (half_z + 1)]
            coarse, fine = split(block)
            upper = crossing_ref[side : side + 1, first : first + LANES] >> 8
            at = slice(side * cross + first, side * cross + first + LANES)
            scatter_left(left_ref, at, upper, uppers, coarse, fine)
            hit = rows_of(upper.astype(F32), uppers) == packed(iota((uppers, LANES), 0))
            left_ref[16 * uppers :, at] = jnp.where(hit, 1.0, 0.0).astype(BF16)
    hit = contract_lanes(left_ref[16 * uppers :], hot_ref[...])
    step = min(32, uppers)
    outs = []
    for u in range(0, uppers, step):
        total = contract_lanes(left_ref[8 * u : 8 * (u + step)], hot_ref[...]) + contract_lanes(
            left_ref[8 * (uppers + u) : 8 * (uppers + u + step)], hot_ref[...]
        )
        for i in range(step):
            at = slice((u + i) * WIDE, (u + i + 1) * WIDE)
            taken = jnp.broadcast_to(hit[u + i : u + i + 1], (8, WIDE)) > 0.5
            out_ref[:, at] = jnp.where(taken, total[8 * i : 8 * i + 8], advanced_ref[:, at])
        at = slice(u * WIDE, (u + step) * WIDE)
        out = pltpu.make_async_copy(out_ref.at[:, at], out_hbm.at[:, at], sems.at[len(outs)])
        out.start()
        outs.append(out)
    for out in outs:
        out.wait()


def arrive(advanced, hot, crossing, before, after):
    uppers = advanced.shape[1] // WIDE
    return call(
        arrive_kernel, jax.ShapeDtypeStruct(advanced.shape, F32), (advanced, hot, crossing, before, after),
        [
            pltpu.VMEM(advanced.shape, F32),
            pltpu.VMEM((17 * uppers, crossing.size), BF16),
            pltpu.SemaphoreType.DMA((-(-uppers // 32),)),
        ],
        in_specs=[VMEM] * 5, flops=1 << 30, moved_bytes=3 << 20,
    )


def shift_up(value, axis):
    return pltpu.roll(value, value.shape[axis] - 1, axis)


def shift_down(value, axis):
    return pltpu.roll(value, 1, axis)


def slab_update(left, center, right, side_low, side_high, rate_ref, write):
    course = center(COUNT)
    size_y, size_z = course.shape
    first_row = iota((size_y, size_z), 0) == 0
    last_row = iota((size_y, size_z), 0) == size_y - 1

    def row_up(value, edge):
        return jnp.where(last_row, edge, shift_up(value, 0))

    def row_down(value, edge):
        return jnp.where(first_row, edge, shift_down(value, 0))

    face_x = 0.5 * (course + right(COUNT))
    face_x_low = 0.5 * (left(COUNT) + course)
    course_y = center(COUNT + 1)
    face_y = 0.5 * (course_y + row_up(course_y, side_high(COUNT)))
    face_y_low = 0.5 * (row_down(course_y, side_low(COUNT)) + course_y)
    course_z = center(COUNT + 2)
    lane = iota((size_y, size_z), 1)
    face_z = jnp.where(lane == size_z - 1, 0.0, 0.5 * (course_z + shift_up(course_z, 1)))
    face_z_low = jnp.where(lane == 0, 0.0, 0.5 * (shift_down(course_z, 1) + course_z))
    from_x_up, from_x_low = jnp.minimum(face_x, 0.0), jnp.maximum(face_x_low, 0.0)
    from_y_up, from_y_low = jnp.minimum(face_y, 0.0), jnp.maximum(face_y_low, 0.0)
    from_z_up, from_z_low = jnp.minimum(face_z, 0.0), jnp.maximum(face_z_low, 0.0)
    own = 1.0 - (
        (jnp.maximum(face_x, 0.0) - jnp.minimum(face_x_low, 0.0))
        + (jnp.maximum(face_y, 0.0) - jnp.minimum(face_y_low, 0.0))
        + (jnp.maximum(face_z, 0.0) - jnp.minimum(face_z_low, 0.0))
    )

    def moved(c):
        amount = center(c)
        total = own * amount
        total = total - from_x_up * right(c) + from_x_low * left(c)
        total = total - from_y_up * row_up(amount, side_high(c)) + from_y_low * row_down(amount, side_low(c))
        return total - from_z_up * shift_up(amount, 1) + from_z_low * shift_down(amount, 1)

    vapour = moved(SECTIONS)
    beside = 1.0 + vapour
    later = None
    gained = None
    for s in reversed(range(SECTIONS)):
        section = moved(s)
        loss = rate_ref[s] * section / beside
        value = section - loss
        if later is not None:
            value = value + 0.5 * later
            gained = later if gained is None else gained + later
        write(s, value)
        later = loss
    write(SECTIONS, vapour + later + 0.5 * gained)
    for c in range(SECTIONS + 1, COUNT):
        write(c, moved(c))


def inner_kernel(cells_ref, low_ref, high_ref, rate_ref, out_ref):
    def middle(x, unused):
        def write(c, value):
            out_ref[c, x] = value

        slab_update(
            lambda c: cells_ref[c, x - 1],
            lambda c: cells_ref[c, x],
            lambda c: cells_ref[c, x + 1],
            lambda c: low_ref[c, pl.ds(x, 1), :],
            lambda c: high_ref[c, pl.ds(x, 1), :],
            rate_ref,
            write,
        )
        return unused

    lax.fori_loop(1, cells_ref.shape[1] - 1, middle, 0)


def inner(cells, low, high, rate):
    out = jax.ShapeDtypeStruct((COUNT,) + cells.shape[1:], F32)
    return call(
        inner_kernel, out, (cells, low, high, rate), [],
        in_specs=[VMEM] * 3 + [SMEM], out_specs=VMEM, flops=30 << 20, moved_bytes=4 << 20,
    )


def quotient(value, count):
    return value >> (count.bit_length() - 1) if count & (count - 1) == 0 else value // count


def final_kernel(
    windows, cells_ref, inner_ref, before_ref, after_ref, low_ref, high_ref, routed_ref, rate_ref, out_hbm,
    total_ref, species_ref, mass_ref, spread_ref, depth_ref, sems,
):
    size_x, size_y, size_z = cells_ref.shape[1:]
    last = size_x - 1
    middle = slice(1, last)
    sections = slice(0, SECTIONS)
    others = slice(SECTIONS, COUNT)
    pairs = [
        (inner_ref.at[sections, middle], total_ref.at[:, middle]),
        (inner_ref.at[others, middle], out_hbm.at[others, middle]),
        (species_ref.at[:, 0], out_hbm.at[others, 0]),
        (species_ref.at[:, 1], out_hbm.at[others, last]),
        (total_ref, out_hbm.at[sections]),
    ]
    copies = [pltpu.make_async_copy(source, target, sems.at[i]) for i, (source, target) in enumerate(pairs)]
    copies[0].start()
    copies[1].start()

    groups = routed_ref.shape[0] // 9
    per = groups // 8
    span = LANES // per
    lane_part = quotient(iota((8, LANES), 1), span)
    for v in range(9):
        rows = routed_ref[pl.ds(v, groups, stride=9), :]
        for q in range(per):
            total = None
            for g in range(per):
                block = rows[8 * g : 8 * g + 8]
                if g != q:
                    block = pltpu.roll(block, (span * (g - q)) % LANES, 1)
                total = block if total is None else jnp.where(lane_part == g, block, total)
            mass_ref[q, v] = total

    bounds = []
    for q in range(per):
        cell = mass_ref[q, SECTIONS].astype(jnp.int32)
        layer = quotient(cell, size_y * size_z)
        valid = cell >= 0
        bounds.append((jnp.min(jnp.where(valid, layer, size_x)), jnp.max(jnp.where(valid, layer, -1))))

    zero = jnp.zeros((size_y, LANES), BF16)

    def deposit(q, start):
        window = windows[q]
        half = SECTIONS * window * size_y
        first = jnp.minimum(start, size_x - window)
        cell = mass_ref[q, SECTIONS].astype(jnp.int32)
        plane = quotient(cell, size_z)
        depth = cell - plane * size_z
        plane = jnp.where(plane >= start * size_y, plane - first * size_y, -1)
        plane = jnp.where(cell >= 0, plane, -1).astype(F32)
        parts = [split(mass_ref[q, s]) for s in range(SECTIONS)]
        for i in range(8):
            at = slice(i * LANES, (i + 1) * LANES)
            depth_ref[q % 2, :, at] = hot_columns(depth[i : i + 1], size_z)
            plane_rows = rows_of(plane[i : i + 1], size_y)
            rows = [[rows_of(part[i : i + 1].astype(F32), size_y) for part in pair] for pair in parts]
            for w in range(window):
                hit = plane_rows == packed(iota((size_y, LANES), 0) + w * size_y)
                for s in range(SECTIONS):
                    base = (s * window + w) * size_y
                    for part in range(2):
                        spread_ref[q % 2, part * half + base : part * half + base + size_y, at] = jnp.where(
                            hit, rows[s][part], zero
                        )
        added = contract_lanes(spread_ref[q % 2, : 2 * half], depth_ref[q % 2])
        for s in range(SECTIONS):
            base = s * window * size_y
            rows = added[base : base + window * size_y] + added[half + base : half + base + window * size_y]
            at = pl.ds(first, window)
            total_ref[s, at] = total_ref[s, at] + rows.reshape(window, size_y, size_z)

    def write(x, number, c, value):
        if c < SECTIONS:
            total_ref[c, x] = value
        else:
            species_ref[c - SECTIONS, number] = value

    slab_update(
        lambda c: before_ref[c], lambda c: cells_ref[c, 0], lambda c: cells_ref[c, 1],
        lambda c: low_ref[c, 0:1, :], lambda c: high_ref[c, 0:1, :],
        rate_ref, functools.partial(write, 0, 0),
    )
    slab_update(
        lambda c: cells_ref[c, last - 1], lambda c: cells_ref[c, last], lambda c: after_ref[c],
        lambda c: low_ref[c, last : last + 1, :], lambda c: high_ref[c, last : last + 1, :],
        rate_ref, functools.partial(write, last, 1),
    )
    copies[2].start()
    copies[3].start()
    copies[0].wait()
    for q in range(per):
        deposit(q, bounds[q][0] if windows[q] < size_x else 0)
    for q in range(per):
        if windows[q] < size_x:
            low, high = bounds[q]

            def more(t, unused, q=q, low=low):
                deposit(q, low + t * windows[q])
                return unused

            lax.fori_loop(1, jnp.where(high - low < windows[q], 1, 1 + (size_x - 1) // windows[q]), more, 0)
    copies[4].start()
    for copy in copies[1:]:
        copy.wait()


def final(windows, cells, inner_cells, before, after, low, high, routed, rate):
    size_x, size_y, size_z = cells.shape[1:]
    per = routed.shape[0] // 9 // 8
    return call(
        functools.partial(final_kernel, windows), jax.ShapeDtypeStruct(inner_cells.shape, F32),
        (cells, inner_cells, before, after, low, high, routed, rate),
        [
            pltpu.VMEM((SECTIONS, size_x, size_y, size_z), F32),
            pltpu.VMEM((SPECIES, 2, size_y, size_z), F32),
            pltpu.VMEM((per, SECTIONS + 1, 8, LANES), F32),
            pltpu.VMEM((2, 2 * SECTIONS * max(windows) * size_y, 8 * LANES), BF16),
            pltpu.VMEM((2, size_z, 8 * LANES), BF16),
            pltpu.SemaphoreType.DMA((5,)),
        ],
        in_specs=[VMEM] * 7 + [SMEM], flops=4 << 30, moved_bytes=6 << 20,
    )


def ring(size):
    up = [(i, (i + 1) % size) for i in range(size)]
    return up, [(j, i) for i, j in up]


def on_device(cell_state, evap_rate, parcels, crossing, conv_mass, conv_owner, conv_cell):
    owner_total = lax.axis_size("gx") * lax.axis_size("gy")
    row_total = conv_owner.shape[0]
    capacity = 2 * row_total // owner_total
    up_x, down_x = ring(lax.axis_size("gx"))
    up_y, down_y = ring(lax.axis_size("gy"))

    send_up, send_down, side_up, side_down, advanced, hot = prepare(cell_state, parcels, crossing)
    before = lax.ppermute(send_up, "gx", up_x)
    after = lax.ppermute(send_down, "gx", down_x)
    low = lax.ppermute(side_up, "gy", up_y)
    high = lax.ppermute(side_down, "gy", down_y)

    filled = bucket(
        send_up, conv_mass, conv_owner.reshape(-1, LANES), conv_cell.reshape(-1, LANES), owner_total, capacity
    )
    fold = LANES // capacity
    filled = filled.reshape(-1, 9, fold, capacity).transpose(0, 2, 1, 3).reshape(owner_total, 1, 9 * capacity)
    routed = lax.all_to_all(filled, ("gx", "gy"), split_axis=0, concat_axis=0, tiled=True)
    routed = routed.reshape(-1, fold, 9, capacity).transpose(0, 2, 1, 3).reshape(-1, LANES)

    windows = [cell_state.shape[1]] * (routed.shape[0] // 9 // 8)
    inner_cells = inner(cell_state, low, high, evap_rate)
    new_parcels = arrive(advanced, hot, crossing, before, after)
    new_cells = final(windows, cell_state, inner_cells, before, after, low, high, routed, evap_rate)
    return (new_cells, new_parcels)


def solution(mesh):
    in_specs = (
        P(None, "gx", "gy", None),
        P(),
        P(None, ("gx", "gy")),
        P(None, ("gx", "gy")),
        P(None, ("gx", "gy")),
        P(("gx", "gy"), None),
        P(("gx", "gy")),
    )
    out_specs = (P(None, "gx", "gy", None), P(None, ("gx", "gy")))
    return jax.shard_map(
        on_device, mesh=mesh, in_specs=in_specs, out_specs=out_specs, check_vma=False
    )
```

```python
import functools

import jax
import jax.numpy as jnp
from jax import lax
from jax.experimental import pallas as pl
from jax.experimental.pallas import tpu as pltpu
from jax.sharding import PartitionSpec as P

SECTIONS = 8
SPECIES = 6
COUNT = SECTIONS + SPECIES
LANES = 128
WIDE = 256
F32 = jnp.float32
BF16 = jnp.bfloat16
ANY = pl.BlockSpec(memory_space=pl.ANY)
SMEM = pl.BlockSpec(memory_space=pltpu.SMEM)
VMEM = pl.BlockSpec(memory_space=pltpu.VMEM)
ALL = 63 << 20
MOST = 32 << 20


def call(kernel, out_shape, operands, scratch, in_specs=None, out_specs=ANY, aliases=None, flops=0, moved_bytes=0, grant=MOST):
    many = isinstance(out_shape, (list, tuple))
    return pl.pallas_call(
        kernel,
        out_shape=out_shape,
        in_specs=in_specs or [ANY] * len(operands),
        out_specs=[out_specs] * len(out_shape) if many else out_specs,
        scratch_shapes=scratch,
        input_output_aliases=aliases or {},
        compiler_params=pltpu.CompilerParams(vmem_limit_bytes=grant),
        cost_estimate=pl.CostEstimate(flops=flops, bytes_accessed=moved_bytes, transcendentals=0),
    )(*operands)


def iota(shape, axis):
    return lax.broadcasted_iota(jnp.int32, shape, axis)


def packed(value):
    return value.astype(F32).astype(BF16)


def split(value):
    coarse = value.astype(BF16)
    return coarse, (value - coarse.astype(F32)).astype(BF16)


def rows_of(row, count):
    return jnp.broadcast_to(row, (count, row.shape[1])).astype(BF16)


def hot_columns(lower, count):
    return jnp.where(rows_of(lower.astype(F32), count) == packed(iota((count, LANES), 0)), 1.0, 0.0).astype(BF16)


def contract_lanes(left, right):
    return lax.dot_general(left, right, (((1,), (1,)), ((), ())), preferred_element_type=F32)


def advance_block(block):
    row = iota(block.shape, 0)
    diameter = jnp.broadcast_to(block[6:7], block.shape)
    warmth = jnp.broadcast_to(block[7:8], block.shape)
    factor = 0.8 / (1.0 + diameter * diameter)
    slowed = block * (1.0 - factor)
    travel = pltpu.roll(0.5 * (block + slowed), 5, 0)
    shrunk = block * (1.0 - 0.05 * warmth)
    warmed = block + factor * (1.0 - block)
    return jnp.where(row < 3, block + travel, jnp.where(row < 6, slowed, jnp.where(row == 6, shrunk, warmed)))


def scatter_left(left_ref, at, upper, uppers, coarse, fine):
    upper = rows_of(upper.astype(F32), 16)
    twice_coarse = jnp.concatenate([coarse.astype(F32)] * 2, axis=0).astype(BF16)
    twice_fine = jnp.concatenate([fine.astype(F32)] * 2, axis=0).astype(BF16)
    zero = jnp.zeros((16, LANES), BF16)
    pair = iota((16, LANES), 0) // 8
    for u in range(0, uppers, 2):
        hit = upper == packed(pair + u)
        left_ref[8 * u : 8 * u + 16, at] = jnp.where(hit, twice_coarse, zero)
        left_ref[8 * (uppers + u) : 8 * (uppers + u) + 16, at] = jnp.where(hit, twice_fine, zero)


def bucket_into(owner_total, capacity, mass_ref, owner_ref, cell_ref, out_ref, left_ref, hot_ref):
    blocks = owner_ref.shape[0]
    uppers = out_ref.shape[0] // 9 // 2
    strict = iota((LANES, 2 * LANES), 0) < iota((LANES, 2 * LANES), 1)
    strict = jnp.where(strict, 1.0, 0.0).astype(BF16)
    owners = owner_ref[...]
    cells = cell_ref[...]
    hots = [
        jnp.where(jnp.broadcast_to(owners[b : b + 1], (owner_total, LANES)) == iota((owner_total, LANES), 0), 1.0, 0.0)
        for b in range(blocks)
    ]
    ranks = jnp.dot(jnp.concatenate(hots, axis=0).astype(BF16), strict, preferred_element_type=F32)
    carry = jnp.zeros((owner_total, LANES), F32)
    base = 16 * uppers
    for b in range(blocks):
        part = ranks[b * owner_total : (b + 1) * owner_total]
        rank = jnp.sum(hots[b] * (part[:, :LANES] + carry), axis=0, keepdims=True).astype(jnp.int32)
        carry = carry + part[:, LANES:]
        spot = owners[b : b + 1] * capacity + rank
        at = slice(b * LANES, (b + 1) * LANES)
        hot_ref[:, at] = hot_columns(spot & (WIDE - 1), WIDE)
        coarse, fine = split(mass_ref[:, at])
        upper = spot >> 8
        scatter_left(left_ref, at, upper, uppers, coarse, fine)
        hit = rows_of(upper.astype(F32), uppers) == packed(iota((uppers, LANES), 0))
        zero = jnp.zeros((uppers, LANES), BF16)
        cell = cells[b : b + 1]
        left_ref[base : base + uppers, at] = jnp.where(hit, rows_of((cell >> 8).astype(F32), uppers), zero)
        left_ref[base + uppers : base + 2 * uppers, at] = jnp.where(
            hit, rows_of((cell & (WIDE - 1)).astype(F32), uppers), zero
        )
        left_ref[base + 2 * uppers : base + 3 * uppers, at] = jnp.where(hit, 1.0, 0.0).astype(BF16)
    placed = contract_lanes(left_ref[...], hot_ref[...])
    cell = placed[base : base + uppers] * float(WIDE) + placed[base + uppers : base + 2 * uppers]
    cell = jnp.where(placed[base + 2 * uppers : base + 3 * uppers] > 0.5, cell, -1.0)
    for u in range(uppers):
        mass = placed[8 * u : 8 * u + 8] + placed[8 * (uppers + u) : 8 * (uppers + u) + 8]
        for half in range(2):
            row = 9 * (2 * u + half)
            lanes = slice(half * LANES, (half + 1) * LANES)
            out_ref[row : row + 8, :] = mass[:, lanes]
            out_ref[row + 8 : row + 9, :] = cell[u : u + 1, lanes]


def prepare_kernel(
    owner_total, capacity,
    cells_hbm, parcels_hbm, crossing_hbm, mass_hbm, owner_hbm, cell_hbm,
    up_hbm, down_hbm, yup_hbm, ydown_hbm, advanced_hbm, hot_hbm, filled_hbm,
    cells_ref, parcels_ref, crossing_ref, mass_ref, owner_ref, cell_ref,
    leave_ref, yup_ref, ydown_ref, advanced_ref, hot_ref, filled_ref,
    parts_ref, left_ref, spot_ref, sems,
):
    size_x, size_y, size_z = cells_hbm.shape[1:]
    face = slice(0, COUNT + 1)
    tail = slice(COUNT + 1, up_hbm.shape[0])
    pairs = [
        (crossing_hbm, crossing_ref),
        (owner_hbm, owner_ref),
        (cell_hbm, cell_ref),
        (mass_hbm, mass_ref),
        (parcels_hbm, parcels_ref),
        (cells_hbm, cells_ref),
        (cells_ref.at[face, size_x - 1], up_hbm.at[face]),
        (cells_ref.at[face, 0], down_hbm.at[face]),
        (filled_ref, filled_hbm),
        (hot_ref, hot_hbm),
        (advanced_ref, advanced_hbm),
        (leave_ref.at[0], up_hbm.at[tail]),
        (leave_ref.at[1], down_hbm.at[tail]),
        (yup_ref, yup_hbm),
        (ydown_ref, ydown_hbm),
    ]
    copies = [pltpu.make_async_copy(source, target, sems.at[i]) for i, (source, target) in enumerate(pairs)]
    for copy in copies[:6]:
        copy.start()
    cross = crossing_ref.shape[1]
    slot_total = parcels_ref.shape[1]
    copies[0].wait()
    for side in range(2):
        for first in range(0, cross, LANES):
            lower = crossing_ref[side : side + 1, first : first + LANES] & (WIDE - 1)
            hot_ref[:, side * cross + first : side * cross + first + LANES] = hot_columns(lower, WIDE)
    copies[9].start()
    copies[4].wait()

    def advance_pair(i, unused):
        for number in range(2):
            blocks = []
            for half in range(2):
                at = pl.ds(pl.multiple_of((4 * i + 2 * number + half) * LANES, LANES), LANES)
                block = advance_block(parcels_ref[:, at])
                advanced_ref[:, at] = block
                blocks.append(block)
            parts_ref[pl.ds(pl.multiple_of((2 * i + number) * 8, 8), 8), :] = jnp.concatenate(blocks, axis=1)
        return unused

    lax.fori_loop(0, slot_total // (4 * LANES), advance_pair, 0, unroll=4)
    copies[10].start()

    halves_y, halves_z = size_y // 8, size_z // LANES
    part_rows = parts_ref.shape[0]
    step_rows = min(256, part_rows)
    for rows in range(0, part_rows, step_rows):
        coarse, fine = split(parts_ref[rows : rows + step_rows])
        for side in range(2):
            for first in range(0, cross, WIDE):
                upper = jnp.broadcast_to(crossing_ref[side : side + 1, first : first + WIDE] >> 8, (8, WIDE))
                hot = hot_ref[:, side * cross + first : side * cross + first + WIDE]
                picked = jnp.dot(coarse, hot, preferred_element_type=F32) + jnp.dot(
                    fine, hot, preferred_element_type=F32
                )
                spots = []
                for offset in range(0, WIDE, LANES):
                    layer, rest = divmod((first + offset) // LANES, halves_y * halves_z)
                    half_y, half_z = divmod(rest, halves_z)
                    spots.append((side, layer, slice(8 * half_y, 8 * half_y + 8), slice(LANES * half_z, LANES * (half_z + 1))))
                if rows:
                    total = jnp.concatenate([leave_ref[spot] for spot in spots], axis=1)
                else:
                    total = jnp.zeros((8, WIDE), F32)
                for i in range(0, step_rows, 8):
                    total = jnp.where(upper == (rows + i) // 8, picked[i : i + 8], total)
                for number, spot in enumerate(spots):
                    leave_ref[spot] = total[:, number * LANES : (number + 1) * LANES]
    copies[11].start()
    copies[12].start()

    copies[5].wait()
    copies[6].start()
    copies[7].start()
    for c in range(COUNT + 1):
        source = c if c < COUNT else COUNT + 1
        yup_ref[c] = cells_ref[source, :, size_y - 1, :]
        ydown_ref[c] = cells_ref[source, :, 0, :]
    copies[13].start()
    copies[14].start()
    for copy in copies[1:4]:
        copy.wait()
    bucket_into(owner_total, capacity, mass_ref, owner_ref, cell_ref, filled_ref, left_ref, spot_ref)
    copies[8].start()
    for copy in copies[6:]:
        copy.wait()


def prepare(cells, parcels, crossing, mass, owner, cell, owner_total, capacity):
    size_x, size_y, size_z = cells.shape[1:]
    extra = 8 * crossing.shape[1] // (size_y * size_z)
    places = owner_total * capacity
    shape = jax.ShapeDtypeStruct
    face = shape((COUNT + 1 + extra, size_y, size_z), F32)
    side = shape((COUNT + 1, size_x, size_z), F32)
    advanced = shape(parcels.shape, F32)
    hot = shape((WIDE, crossing.size), BF16)
    filled = shape((9 * places // LANES, LANES), F32)
    operands = (cells, parcels, crossing, mass, owner, cell)
    scratch = [pltpu.VMEM(a.shape, a.dtype) for a in operands]
    scratch += [pltpu.VMEM((2, extra, size_y, size_z), F32)]
    scratch += [pltpu.VMEM(a.shape, a.dtype) for a in (side, side, advanced, hot, filled)]
    scratch += [
        pltpu.VMEM((8 * parcels.shape[1] // WIDE, WIDE), F32),
        pltpu.VMEM((19 * places // WIDE, mass.shape[1]), BF16),
        pltpu.VMEM((WIDE, mass.shape[1]), BF16),
        pltpu.SemaphoreType.DMA((15,)),
    ]
    return call(
        functools.partial(prepare_kernel, owner_total, capacity),
        [face, face, side, side, advanced, hot, filled], operands, scratch,
        flops=2 << 30, moved_bytes=6 << 20, grant=ALL,
    )


def arrive_kernel(unused, advanced_ref, hot_ref, crossing_ref, before_ref, after_ref, out_hbm, out_ref, left_ref, sems):
    cross = crossing_ref.shape[1]
    uppers = advanced_ref.shape[1] // WIDE
    size_y, size_z = before_ref.shape[1:]
    halves_y, halves_z = size_y // 8, size_z // LANES
    for side, come_ref in ((0, before_ref), (1, after_ref)):
        for first in range(0, cross, LANES):
            layer, rest = divmod(first // LANES, halves_y * halves_z)
            half_y, half_z = divmod(rest, halves_z)
            block = come_ref[COUNT + 1 + layer, 8 * half_y : 8 * half_y + 8, LANES * half_z : LANES * (half_z + 1)]
            coarse, fine = split(block)
            upper = crossing_ref[side : side + 1, first : first + LANES] >> 8
            at = slice(side * cross + first, side * cross + first + LANES)
            scatter_left(left_ref, at, upper, uppers, coarse, fine)
            hit = rows_of(upper.astype(F32), uppers) == packed(iota((uppers, LANES), 0))
            left_ref[16 * uppers :, at] = jnp.where(hit, 1.0, 0.0).astype(BF16)
    hit = contract_lanes(left_ref[16 * uppers :], hot_ref[...])
    step = min(32, uppers)
    outs = []
    for u in range(0, uppers, step):
        total = contract_lanes(left_ref[8 * u : 8 * (u + step)], hot_ref[...]) + contract_lanes(
            left_ref[8 * (uppers + u) : 8 * (uppers + u + step)], hot_ref[...]
        )
        for i in range(step):
            at = slice((u + i) * WIDE, (u + i + 1) * WIDE)
            taken = jnp.broadcast_to(hit[u + i : u + i + 1], (8, WIDE)) > 0.5
            out_ref[:, at] = jnp.where(taken, total[8 * i : 8 * i + 8], advanced_ref[:, at])
        at = slice(u * WIDE, (u + step) * WIDE)
        out = pltpu.make_async_copy(out_ref.at[:, at], out_hbm.at[:, at], sems.at[len(outs)])
        out.start()
        outs.append(out)
    for out in outs:
        out.wait()


def arrive(earlier, advanced, hot, crossing, before, after):
    uppers = advanced.shape[1] // WIDE
    return call(
        arrive_kernel, jax.ShapeDtypeStruct(advanced.shape, F32), (earlier, advanced, hot, crossing, before, after),
        [
            pltpu.VMEM(advanced.shape, F32),
            pltpu.VMEM((17 * uppers, crossing.size), BF16),
            pltpu.SemaphoreType.DMA((-(-uppers // 32),)),
        ],
        in_specs=[ANY] + [VMEM] * 5, flops=1 << 30, moved_bytes=3 << 20,
    )


def shift_up(value, axis):
    return pltpu.roll(value, value.shape[axis] - 1, axis)


def shift_down(value, axis):
    return pltpu.roll(value, 1, axis)


def slab_update(left, center, right, side_low, side_high, rate_ref, write):
    course = center(COUNT)
    size_y, size_z = course.shape
    first_row = iota((size_y, size_z), 0) == 0
    last_row = iota((size_y, size_z), 0) == size_y - 1

    def row_up(value, edge):
        return jnp.where(last_row, edge, shift_up(value, 0))

    def row_down(value, edge):
        return jnp.where(first_row, edge, shift_down(value, 0))

    face_x = 0.5 * (course + right(COUNT))
    face_x_low = 0.5 * (left(COUNT) + course)
    course_y = center(COUNT + 1)
    face_y = 0.5 * (course_y + row_up(course_y, side_high(COUNT)))
    face_y_low = 0.5 * (row_down(course_y, side_low(COUNT)) + course_y)
    course_z = center(COUNT + 2)
    lane = iota((size_y, size_z), 1)
    face_z = jnp.where(lane == size_z - 1, 0.0, 0.5 * (course_z + shift_up(course_z, 1)))
    face_z_low = jnp.where(lane == 0, 0.0, 0.5 * (shift_down(course_z, 1) + course_z))
    from_x_up, from_x_low = jnp.minimum(face_x, 0.0), jnp.maximum(face_x_low, 0.0)
    from_y_up, from_y_low = jnp.minimum(face_y, 0.0), jnp.maximum(face_y_low, 0.0)
    from_z_up, from_z_low = jnp.minimum(face_z, 0.0), jnp.maximum(face_z_low, 0.0)
    own = 1.0 - (
        (jnp.maximum(face_x, 0.0) - jnp.minimum(face_x_low, 0.0))
        + (jnp.maximum(face_y, 0.0) - jnp.minimum(face_y_low, 0.0))
        + (jnp.maximum(face_z, 0.0) - jnp.minimum(face_z_low, 0.0))
    )

    def moved(c):
        amount = center(c)
        total = own * amount
        total = total - from_x_up * right(c) + from_x_low * left(c)
        total = total - from_y_up * row_up(amount, side_high(c)) + from_y_low * row_down(amount, side_low(c))
        return total - from_z_up * shift_up(amount, 1) + from_z_low * shift_down(amount, 1)

    vapour = moved(SECTIONS)
    beside = 1.0 + vapour
    later = None
    gained = None
    for s in reversed(range(SECTIONS)):
        section = moved(s)
        loss = rate_ref[s] * section / beside
        value = section - loss
        if later is not None:
            value = value + 0.5 * later
            gained = later if gained is None else gained + later
        write(s, value)
        later = loss
    write(SECTIONS, vapour + later + 0.5 * gained)
    for c in range(SECTIONS + 1, COUNT):
        write(c, moved(c))


def inner_kernel(
    cells_hbm, low_ref, high_ref, deposit_ref, rate_ref, out_hbm, token_hbm, cells_ref, out_ref, token_ref, in_sems, sems
):
    size_x = cells_hbm.shape[1]
    last = size_x - 1

    def fetch(x):
        return pltpu.make_async_copy(cells_hbm.at[:, x], cells_ref.at[:, x], in_sems.at[x])

    for x in range(size_x):
        fetch(x).start()
    token_ref[...] = jnp.zeros(token_ref.shape, F32)
    token = pltpu.make_async_copy(token_ref, token_hbm, sems.at[0])
    token.start()
    fetch(0).wait()
    fetch(1).wait()

    def store(x):
        return pltpu.make_async_copy(out_ref.at[:, x], out_hbm.at[:, x], sems.at[x])

    def middle(x, unused):
        fetch(x + 1).wait()

        def write(c, value):
            out_ref[c, x] = value + deposit_ref[c, x] if c < SECTIONS else value

        slab_update(
            lambda c: cells_ref[c, x - 1],
            lambda c: cells_ref[c, x],
            lambda c: cells_ref[c, x + 1],
            lambda c: low_ref[c, pl.ds(x, 1), :],
            lambda c: high_ref[c, pl.ds(x, 1), :],
            rate_ref,
            write,
        )
        store(x).start()
        return unused

    lax.fori_loop(1, last, middle, 0)
    for x in range(1, last):
        store(x).wait()
    token.wait()


def inner(cells, low, high, deposited, rate):
    out = jax.ShapeDtypeStruct((COUNT,) + cells.shape[1:], F32)
    token = jax.ShapeDtypeStruct((8, LANES), F32)
    return call(
        inner_kernel, [out, token], (cells, low, high, deposited, rate),
        [pltpu.VMEM(a.shape, F32) for a in (cells, out, token)] + [pltpu.SemaphoreType.DMA((cells.shape[1],))] * 2,
        in_specs=[ANY] + [VMEM] * 3 + [SMEM], flops=30 << 20, moved_bytes=4 << 20,
    )


def edge_kernel(
    cells_hbm, inner_hbm, before_ref, after_ref, low_ref, high_ref, deposit_ref, rate_ref, out_hbm,
    cells_ref, out_ref, sems,
):
    last = cells_hbm.shape[1] - 1
    copies = [
        pltpu.make_async_copy(cells_hbm.at[:, 0:2], cells_ref.at[:, 0:2], sems.at[0]),
        pltpu.make_async_copy(cells_hbm.at[:, last - 1 : last + 1], cells_ref.at[:, 2:4], sems.at[1]),
        pltpu.make_async_copy(out_ref.at[:, 0], out_hbm.at[:, 0], sems.at[2]),
        pltpu.make_async_copy(out_ref.at[:, 1], out_hbm.at[:, last], sems.at[3]),
    ]
    copies[0].start()
    copies[1].start()

    def layer(left, number, x, right):
        def write(c, value):
            out_ref[c, number] = value + deposit_ref[c, x] if c < SECTIONS else value

        slab_update(
            left,
            lambda c: cells_ref[c, 3 * number],
            right,
            lambda c: low_ref[c, x : x + 1, :],
            lambda c: high_ref[c, x : x + 1, :],
            rate_ref,
            write,
        )
        copies[2 + number].start()

    copies[0].wait()
    layer(lambda c: before_ref[c], 0, 0, lambda c: cells_ref[c, 1])
    copies[1].wait()
    layer(lambda c: cells_ref[c, 2], 1, last, lambda c: after_ref[c])
    copies[2].wait()
    copies[3].wait()


def edges(cells, inner_cells, before, after, low, high, deposited, rate):
    size_y, size_z = cells.shape[2:]
    return call(
        edge_kernel, jax.ShapeDtypeStruct(inner_cells.shape, F32),
        (cells, inner_cells, before, after, low, high, deposited, rate),
        [
            pltpu.VMEM((cells.shape[0], 4, size_y, size_z), F32),
            pltpu.VMEM((COUNT, 2, size_y, size_z), F32),
            pltpu.SemaphoreType.DMA((4,)),
        ],
        in_specs=[ANY, ANY] + [VMEM] * 5 + [SMEM], aliases={1: 0}, flops=10 << 20, moved_bytes=2 << 20,
    )


def quotient(value, count):
    return value >> (count.bit_length() - 1) if count & (count - 1) == 0 else value // count


def deposit_kernel(shape, windows, routed_ref, out_ref, mass_ref, spread_ref, depth_ref):
    size_x, size_y, size_z = shape
    groups = routed_ref.shape[0] // 9
    per = groups // 8
    span = LANES // per
    lane_part = quotient(iota((8, LANES), 1), span)
    for v in range(9):
        rows = routed_ref[pl.ds(v, groups, stride=9), :]
        for q in range(per):
            total = None
            for g in range(per):
                block = rows[8 * g : 8 * g + 8]
                if g != q:
                    block = pltpu.roll(block, (span * (g - q)) % LANES, 1)
                total = block if total is None else jnp.where(lane_part == g, block, total)
            mass_ref[q, v] = total

    bounds = []
    for q in range(per):
        cell = mass_ref[q, SECTIONS].astype(jnp.int32)
        layer = quotient(cell, size_y * size_z)
        valid = cell >= 0
        bounds.append((jnp.min(jnp.where(valid, layer, size_x)), jnp.max(jnp.where(valid, layer, -1))))

    zero = jnp.zeros((size_y, LANES), BF16)

    def deposit(q, start):
        window = windows[q]
        half = SECTIONS * window * size_y
        first = jnp.minimum(start, size_x - window)
        cell = mass_ref[q, SECTIONS].astype(jnp.int32)
        plane = quotient(cell, size_z)
        depth = cell - plane * size_z
        plane = jnp.where(plane >= start * size_y, plane - first * size_y, -1)
        plane = jnp.where(cell >= 0, plane, -1).astype(F32)
        parts = [split(mass_ref[q, s]) for s in range(SECTIONS)]
        for i in range(8):
            at = slice(i * LANES, (i + 1) * LANES)
            depth_ref[q % 2, :, at] = hot_columns(depth[i : i + 1], size_z)
            plane_rows = rows_of(plane[i : i + 1], size_y)
            rows = [[rows_of(part[i : i + 1].astype(F32), size_y) for part in pair] for pair in parts]
            for w in range(window):
                hit = plane_rows == packed(iota((size_y, LANES), 0) + w * size_y)
                for s in range(SECTIONS):
                    base = (s * window + w) * size_y
                    for part in range(2):
                        spread_ref[q % 2, part * half + base : part * half + base + size_y, at] = jnp.where(
                            hit, rows[s][part], zero
                        )
        added = contract_lanes(spread_ref[q % 2, : 2 * half], depth_ref[q % 2])
        for s in range(SECTIONS):
            base = s * window * size_y
            rows = added[base : base + window * size_y] + added[half + base : half + base + window * size_y]
            at = pl.ds(first, window)
            out_ref[s, at] = out_ref[s, at] + rows.reshape(window, size_y, size_z)

    out_ref[...] = jnp.zeros(out_ref.shape, F32)
    for q in range(per):
        deposit(q, bounds[q][0] if windows[q] < size_x else 0)
    for q in range(per):
        if windows[q] < size_x:
            low, high = bounds[q]

            def more(t, unused, q=q, low=low):
                deposit(q, low + t * windows[q])
                return unused

            lax.fori_loop(1, jnp.where(high - low < windows[q], 1, 1 + (size_x - 1) // windows[q]), more, 0)


def deposit(routed, shape, windows):
    size_x, size_y, size_z = shape
    per = routed.shape[0] // 9 // 8
    return call(
        functools.partial(deposit_kernel, shape, windows), jax.ShapeDtypeStruct((SECTIONS,) + shape, F32), (routed,),
        [
            pltpu.VMEM((per, SECTIONS + 1, 8, LANES), F32),
            pltpu.VMEM((2, 2 * SECTIONS * max(windows) * size_y, 8 * LANES), BF16),
            pltpu.VMEM((2, size_z, 8 * LANES), BF16),
        ],
        in_specs=[VMEM], out_specs=VMEM, flops=1 << 30, moved_bytes=2 << 20,
    )


def ring(size):
    up = [(i, (i + 1) % size) for i in range(size)]
    return up, [(j, i) for i, j in up]


def on_device(cell_state, evap_rate, parcels, crossing, conv_mass, conv_owner, conv_cell):
    owner_total = lax.axis_size("gx") * lax.axis_size("gy")
    row_total = conv_owner.shape[0]
    capacity = 2 * row_total // owner_total
    up_x, down_x = ring(lax.axis_size("gx"))
    up_y, down_y = ring(lax.axis_size("gy"))

    send_up, send_down, side_up, side_down, advanced, hot, filled = prepare(
        cell_state, parcels, crossing, conv_mass, conv_owner.reshape(-1, LANES), conv_cell.reshape(-1, LANES),
        owner_total, capacity,
    )
    before = lax.ppermute(send_up, "gx", up_x)
    after = lax.ppermute(send_down, "gx", down_x)
    low = lax.ppermute(side_up, "gy", up_y)
    high = lax.ppermute(side_down, "gy", down_y)

    fold = LANES // capacity
    filled = filled.reshape(-1, 9, fold, capacity).transpose(0, 2, 1, 3).reshape(owner_total, 1, 9 * capacity)
    routed = lax.all_to_all(filled, ("gx", "gy"), split_axis=0, concat_axis=0, tiled=True)
    routed = routed.reshape(-1, fold, 9, capacity).transpose(0, 2, 1, 3).reshape(-1, LANES)

    windows = [cell_state.shape[1]] * (routed.shape[0] // 9 // 8)
    deposited = deposit(routed, cell_state.shape[1:], windows)
    inner_cells, token = inner(cell_state, low, high, deposited, evap_rate)
    new_parcels = arrive(token, advanced, hot, crossing, before, after)
    new_cells = edges(cell_state, inner_cells, before, after, low, high, deposited, evap_rate)
    return (new_cells, new_parcels)


def solution(mesh):
    in_specs = (
        P(None, "gx", "gy", None),
        P(),
        P(None, ("gx", "gy")),
        P(None, ("gx", "gy")),
        P(None, ("gx", "gy")),
        P(("gx", "gy"), None),
        P(("gx", "gy")),
    )
    out_specs = (P(None, "gx", "gy", None), P(None, ("gx", "gy")))
    return jax.shard_map(
        on_device, mesh=mesh, in_specs=in_specs, out_specs=out_specs, check_vma=False
    )
```

```python
import functools

import jax
import jax.numpy as jnp
from jax import lax
from jax.experimental import pallas as pl
from jax.experimental.pallas import tpu as pltpu
from jax.sharding import PartitionSpec as P

SECTIONS = 8
SPECIES = 6
COUNT = SECTIONS + SPECIES
LANES = 128
WIDE = 256
GROUPS = 4
F32 = jnp.float32
BF16 = jnp.bfloat16
ANY = pl.BlockSpec(memory_space=pl.ANY)
SMEM = pl.BlockSpec(memory_space=pltpu.SMEM)
VMEM = pl.BlockSpec(memory_space=pltpu.VMEM)
ALL = 63 << 20
MOST = 32 << 20


def call(kernel, out_shape, operands, scratch, in_specs=None, out_specs=ANY, aliases=None, flops=0, moved_bytes=0, grant=MOST):
    many = isinstance(out_shape, (list, tuple))
    return pl.pallas_call(
        kernel,
        out_shape=out_shape,
        in_specs=in_specs or [ANY] * len(operands),
        out_specs=[out_specs] * len(out_shape) if many else out_specs,
        scratch_shapes=scratch,
        input_output_aliases=aliases or {},
        compiler_params=pltpu.CompilerParams(vmem_limit_bytes=grant),
        cost_estimate=pl.CostEstimate(flops=flops, bytes_accessed=moved_bytes, transcendentals=0),
    )(*operands)


def iota(shape, axis):
    return lax.broadcasted_iota(jnp.int32, shape, axis)


def quotient(value, count):
    return value >> (count.bit_length() - 1) if count & (count - 1) == 0 else value // count


def packed(value):
    return value.astype(F32).astype(BF16)


def split(value):
    coarse = value.astype(BF16)
    return coarse, (value - coarse.astype(F32)).astype(BF16)


def rows_of(row, count):
    return jnp.broadcast_to(row, (count, row.shape[1])).astype(BF16)


def hot_columns(lower, count):
    return jnp.where(rows_of(lower.astype(F32), count) == packed(iota((count, LANES), 0)), 1.0, 0.0).astype(BF16)


def contract_lanes(left, right):
    return lax.dot_general(left, right, (((1,), (1,)), ((), ())), preferred_element_type=F32)


def advance_block(block):
    row = iota(block.shape, 0)
    diameter = jnp.broadcast_to(block[6:7], block.shape)
    warmth = jnp.broadcast_to(block[7:8], block.shape)
    factor = 0.8 / (1.0 + diameter * diameter)
    slowed = block * (1.0 - factor)
    travel = pltpu.roll(0.5 * (block + slowed), 5, 0)
    shrunk = block * (1.0 - 0.05 * warmth)
    warmed = block + factor * (1.0 - block)
    return jnp.where(row < 3, block + travel, jnp.where(row < 6, slowed, jnp.where(row == 6, shrunk, warmed)))


def scatter_left(left_ref, at, upper, uppers, coarse, fine):
    upper = rows_of(upper.astype(F32), 16)
    twice_coarse = jnp.concatenate([coarse.astype(F32)] * 2, axis=0).astype(BF16)
    twice_fine = jnp.concatenate([fine.astype(F32)] * 2, axis=0).astype(BF16)
    zero = jnp.zeros((16, LANES), BF16)
    pair = iota((16, LANES), 0) // 8
    for u in range(0, uppers, 2):
        hit = upper == packed(pair + u)
        left_ref[8 * u : 8 * u + 16, at] = jnp.where(hit, twice_coarse, zero)
        left_ref[8 * (uppers + u) : 8 * (uppers + u) + 16, at] = jnp.where(hit, twice_fine, zero)


def bucket_into(owner_total, capacity, cell_total, mass_ref, owner_ref, cell_ref, out_ref, left_ref, hot_ref):
    blocks = owner_ref.shape[0]
    uppers = out_ref.shape[0] // 9 // 2
    strict = iota((LANES, 2 * LANES), 0) < iota((LANES, 2 * LANES), 1)
    strict = jnp.where(strict, 1.0, 0.0).astype(BF16)
    owners = owner_ref[...]
    cells = cell_ref[...]
    keys = owner_total * GROUPS
    order = owners * GROUPS + quotient(cells, cell_total // GROUPS)
    hots = [
        jnp.where(jnp.broadcast_to(order[b : b + 1], (keys, LANES)) == iota((keys, LANES), 0), 1.0, 0.0)
        for b in range(blocks)
    ]
    ranks = jnp.dot(jnp.concatenate(hots, axis=0).astype(BF16), strict, preferred_element_type=F32)
    parts = [ranks[b * keys : (b + 1) * keys] for b in range(blocks)]
    counts = sum(part[:, LANES:] for part in parts)
    key, other = iota((keys, keys), 0), iota((keys, keys), 1)
    same = quotient(key, GROUPS) == quotient(other, GROUPS)
    sums = jnp.concatenate([jnp.where(same & (other < key), 1.0, 0.0), jnp.where(same, 1.0, 0.0)], axis=0).astype(BF16)
    sums = jnp.dot(sums, counts.astype(BF16), preferred_element_type=F32)
    carry, owned = sums[:keys], sums[keys:]
    base = 16 * uppers
    for b in range(blocks):
        rank = jnp.sum(hots[b] * (parts[b][:, :LANES] + carry), axis=0, keepdims=True)
        total = jnp.sum(hots[b] * owned, axis=0, keepdims=True)
        carry = carry + parts[b][:, LANES:]
        spot = owners[b : b + 1] * capacity + ((rank * float(capacity) + 0.5) / total).astype(jnp.int32)
        at = slice(b * LANES, (b + 1) * LANES)
        hot_ref[:, at] = hot_columns(spot & (WIDE - 1), WIDE)
        coarse, fine = split(mass_ref[:, at])
        upper = spot >> 8
        scatter_left(left_ref, at, upper, uppers, coarse, fine)
        hit = rows_of(upper.astype(F32), uppers) == packed(iota((uppers, LANES), 0))
        zero = jnp.zeros((uppers, LANES), BF16)
        cell = cells[b : b + 1]
        left_ref[base : base + uppers, at] = jnp.where(hit, rows_of((cell >> 8).astype(F32), uppers), zero)
        left_ref[base + uppers : base + 2 * uppers, at] = jnp.where(
            hit, rows_of((cell & (WIDE - 1)).astype(F32), uppers), zero
        )
        left_ref[base + 2 * uppers : base + 3 * uppers, at] = jnp.where(hit, 1.0, 0.0).astype(BF16)
    placed = contract_lanes(left_ref[...], hot_ref[...])
    cell = placed[base : base + uppers] * float(WIDE) + placed[base + uppers : base + 2 * uppers]
    cell = jnp.where(placed[base + 2 * uppers : base + 3 * uppers] > 0.5, cell, -1.0)
    for u in range(uppers):
        mass = placed[8 * u : 8 * u + 8] + placed[8 * (uppers + u) : 8 * (uppers + u) + 8]
        for half in range(2):
            row = 9 * (2 * u + half)
            lanes = slice(half * LANES, (half + 1) * LANES)
            out_ref[row : row + 8, :] = mass[:, lanes]
            out_ref[row + 8 : row + 9, :] = cell[u : u + 1, lanes]


def prepare_kernel(
    owner_total, capacity,
    cells_hbm, parcels_hbm, crossing_hbm, mass_hbm, owner_hbm, cell_hbm,
    up_hbm, down_hbm, yup_hbm, ydown_hbm, advanced_hbm, hot_hbm, filled_hbm,
    cells_ref, parcels_ref, crossing_ref, mass_ref, owner_ref, cell_ref,
    leave_ref, yup_ref, ydown_ref, advanced_ref, hot_ref, filled_ref,
    parts_ref, left_ref, spot_ref, sems,
):
    size_x, size_y, size_z = cells_hbm.shape[1:]
    face = slice(0, COUNT + 1)
    tail = slice(COUNT + 1, up_hbm.shape[0])
    pairs = [
        (crossing_hbm, crossing_ref),
        (owner_hbm, owner_ref),
        (cell_hbm, cell_ref),
        (mass_hbm, mass_ref),
        (parcels_hbm, parcels_ref),
        (cells_hbm, cells_ref),
        (cells_ref.at[face, size_x - 1], up_hbm.at[face]),
        (cells_ref.at[face, 0], down_hbm.at[face]),
        (filled_ref, filled_hbm),
        (hot_ref, hot_hbm),
        (advanced_ref, advanced_hbm),
        (leave_ref.at[0], up_hbm.at[tail]),
        (leave_ref.at[1], down_hbm.at[tail]),
        (yup_ref, yup_hbm),
        (ydown_ref, ydown_hbm),
    ]
    copies = [pltpu.make_async_copy(source, target, sems.at[i]) for i, (source, target) in enumerate(pairs)]
    for copy in copies[:6]:
        copy.start()
    cross = crossing_ref.shape[1]
    slot_total = parcels_ref.shape[1]
    copies[0].wait()
    for side in range(2):
        for first in range(0, cross, LANES):
            lower = crossing_ref[side : side + 1, first : first + LANES] & (WIDE - 1)
            hot_ref[:, side * cross + first : side * cross + first + LANES] = hot_columns(lower, WIDE)
    copies[9].start()
    copies[4].wait()

    def advance_pair(i, unused):
        for number in range(2):
            blocks = []
            for half in range(2):
                at = pl.ds(pl.multiple_of((4 * i + 2 * number + half) * LANES, LANES), LANES)
                block = advance_block(parcels_ref[:, at])
                advanced_ref[:, at] = block
                blocks.append(block)
            parts_ref[pl.ds(pl.multiple_of((2 * i + number) * 8, 8), 8), :] = jnp.concatenate(blocks, axis=1)
        return unused

    lax.fori_loop(0, slot_total // (4 * LANES), advance_pair, 0, unroll=4)
    copies[10].start()

    halves_y, halves_z = size_y // 8, size_z // LANES
    part_rows = parts_ref.shape[0]
    step_rows = min(256, part_rows)
    for rows in range(0, part_rows, step_rows):
        coarse, fine = split(parts_ref[rows : rows + step_rows])
        for side in range(2):
            for first in range(0, cross, WIDE):
                upper = jnp.broadcast_to(crossing_ref[side : side + 1, first : first + WIDE] >> 8, (8, WIDE))
                hot = hot_ref[:, side * cross + first : side * cross + first + WIDE]
                picked = jnp.dot(coarse, hot, preferred_element_type=F32) + jnp.dot(
                    fine, hot, preferred_element_type=F32
                )
                spots = []
                for offset in range(0, WIDE, LANES):
                    layer, rest = divmod((first + offset) // LANES, halves_y * halves_z)
                    half_y, half_z = divmod(rest, halves_z)
                    spots.append((side, layer, slice(8 * half_y, 8 * half_y + 8), slice(LANES * half_z, LANES * (half_z + 1))))
                if rows:
                    total = jnp.concatenate([leave_ref[spot] for spot in spots], axis=1)
                else:
                    total = jnp.zeros((8, WIDE), F32)
                for i in range(0, step_rows, 8):
                    total = jnp.where(upper == (rows + i) // 8, picked[i : i + 8], total)
                for number, spot in enumerate(spots):
                    leave_ref[spot] = total[:, number * LANES : (number + 1) * LANES]
    copies[11].start()
    copies[12].start()

    copies[5].wait()
    copies[6].start()
    copies[7].start()
    for c in range(COUNT + 1):
        source = c if c < COUNT else COUNT + 1
        yup_ref[c] = cells_ref[source, :, size_y - 1, :]
        ydown_ref[c] = cells_ref[source, :, 0, :]
    copies[13].start()
    copies[14].start()
    for copy in copies[1:4]:
        copy.wait()
    bucket_into(owner_total, capacity, size_x * size_y * size_z, mass_ref, owner_ref, cell_ref, filled_ref, left_ref, spot_ref)
    copies[8].start()
    for copy in copies[6:]:
        copy.wait()


def prepare(cells, parcels, crossing, mass, owner, cell, owner_total, capacity):
    size_x, size_y, size_z = cells.shape[1:]
    extra = 8 * crossing.shape[1] // (size_y * size_z)
    places = owner_total * capacity
    shape = jax.ShapeDtypeStruct
    face = shape((COUNT + 1 + extra, size_y, size_z), F32)
    side = shape((COUNT + 1, size_x, size_z), F32)
    advanced = shape(parcels.shape, F32)
    hot = shape((WIDE, crossing.size), BF16)
    filled = shape((9 * places // LANES, LANES), F32)
    operands = (cells, parcels, crossing, mass, owner, cell)
    scratch = [pltpu.VMEM(a.shape, a.dtype) for a in operands]
    scratch += [pltpu.VMEM((2, extra, size_y, size_z), F32)]
    scratch += [pltpu.VMEM(a.shape, a.dtype) for a in (side, side, advanced, hot, filled)]
    scratch += [
        pltpu.VMEM((8 * parcels.shape[1] // WIDE, WIDE), F32),
        pltpu.VMEM((19 * places // WIDE, mass.shape[1]), BF16),
        pltpu.VMEM((WIDE, mass.shape[1]), BF16),
        pltpu.SemaphoreType.DMA((15,)),
    ]
    return call(
        functools.partial(prepare_kernel, owner_total, capacity),
        [face, face, side, side, advanced, hot, filled], operands, scratch,
        flops=2 << 30, moved_bytes=6 << 20, grant=ALL,
    )


def arrive_kernel(unused, advanced_ref, hot_ref, crossing_ref, before_ref, after_ref, out_hbm, out_ref, left_ref, sems):
    cross = crossing_ref.shape[1]
    uppers = advanced_ref.shape[1] // WIDE
    size_y, size_z = before_ref.shape[1:]
    halves_y, halves_z = size_y // 8, size_z // LANES
    for side, come_ref in ((0, before_ref), (1, after_ref)):
        for first in range(0, cross, LANES):
            layer, rest = divmod(first // LANES, halves_y * halves_z)
            half_y, half_z = divmod(rest, halves_z)
            block = come_ref[COUNT + 1 + layer, 8 * half_y : 8 * half_y + 8, LANES * half_z : LANES * (half_z + 1)]
            coarse, fine = split(block)
            upper = crossing_ref[side : side + 1, first : first + LANES] >> 8
            at = slice(side * cross + first, side * cross + first + LANES)
            scatter_left(left_ref, at, upper, uppers, coarse, fine)
            hit = rows_of(upper.astype(F32), uppers) == packed(iota((uppers, LANES), 0))
            left_ref[16 * uppers :, at] = jnp.where(hit, 1.0, 0.0).astype(BF16)
    hit = contract_lanes(left_ref[16 * uppers :], hot_ref[...])
    step = min(32, uppers)
    outs = []
    for u in range(0, uppers, step):
        total = contract_lanes(left_ref[8 * u : 8 * (u + step)], hot_ref[...]) + contract_lanes(
            left_ref[8 * (uppers + u) : 8 * (uppers + u + step)], hot_ref[...]
        )
        for i in range(step):
            at = slice((u + i) * WIDE, (u + i + 1) * WIDE)
            taken = jnp.broadcast_to(hit[u + i : u + i + 1], (8, WIDE)) > 0.5
            out_ref[:, at] = jnp.where(taken, total[8 * i : 8 * i + 8], advanced_ref[:, at])
        at = slice(u * WIDE, (u + step) * WIDE)
        out = pltpu.make_async_copy(out_ref.at[:, at], out_hbm.at[:, at], sems.at[len(outs)])
        out.start()
        outs.append(out)
    for out in outs:
        out.wait()


def arrive(earlier, advanced, hot, crossing, before, after):
    uppers = advanced.shape[1] // WIDE
    return call(
        arrive_kernel, jax.ShapeDtypeStruct(advanced.shape, F32), (earlier, advanced, hot, crossing, before, after),
        [
            pltpu.VMEM(advanced.shape, F32),
            pltpu.VMEM((17 * uppers, crossing.size), BF16),
            pltpu.SemaphoreType.DMA((-(-uppers // 32),)),
        ],
        in_specs=[ANY] + [VMEM] * 5, flops=1 << 30, moved_bytes=3 << 20,
    )


def shift_up(value, axis):
    return pltpu.roll(value, value.shape[axis] - 1, axis)


def shift_down(value, axis):
    return pltpu.roll(value, 1, axis)


def slab_update(left, center, right, side_low, side_high, rate_ref, write):
    course = center(COUNT)
    size_y, size_z = course.shape
    first_row = iota((size_y, size_z), 0) == 0
    last_row = iota((size_y, size_z), 0) == size_y - 1

    def row_up(value, edge):
        return jnp.where(last_row, edge, shift_up(value, 0))

    def row_down(value, edge):
        return jnp.where(first_row, edge, shift_down(value, 0))

    face_x = 0.5 * (course + right(COUNT))
    face_x_low = 0.5 * (left(COUNT) + course)
    course_y = center(COUNT + 1)
    face_y = 0.5 * (course_y + row_up(course_y, side_high(COUNT)))
    face_y_low = 0.5 * (row_down(course_y, side_low(COUNT)) + course_y)
    course_z = center(COUNT + 2)
    lane = iota((size_y, size_z), 1)
    face_z = jnp.where(lane == size_z - 1, 0.0, 0.5 * (course_z + shift_up(course_z, 1)))
    face_z_low = jnp.where(lane == 0, 0.0, 0.5 * (shift_down(course_z, 1) + course_z))
    from_x_up, from_x_low = jnp.minimum(face_x, 0.0), jnp.maximum(face_x_low, 0.0)
    from_y_up, from_y_low = jnp.minimum(face_y, 0.0), jnp.maximum(face_y_low, 0.0)
    from_z_up, from_z_low = jnp.minimum(face_z, 0.0), jnp.maximum(face_z_low, 0.0)
    own = 1.0 - (
        (jnp.maximum(face_x, 0.0) - jnp.minimum(face_x_low, 0.0))
        + (jnp.maximum(face_y, 0.0) - jnp.minimum(face_y_low, 0.0))
        + (jnp.maximum(face_z, 0.0) - jnp.minimum(face_z_low, 0.0))
    )

    def moved(c):
        amount = center(c)
        total = own * amount
        total = total - from_x_up * right(c) + from_x_low * left(c)
        total = total - from_y_up * row_up(amount, side_high(c)) + from_y_low * row_down(amount, side_low(c))
        return total - from_z_up * shift_up(amount, 1) + from_z_low * shift_down(amount, 1)

    vapour = moved(SECTIONS)
    beside = 1.0 + vapour
    later = None
    gained = None
    for s in reversed(range(SECTIONS)):
        section = moved(s)
        loss = rate_ref[s] * section / beside
        value = section - loss
        if later is not None:
            value = value + 0.5 * later
            gained = later if gained is None else gained + later
        write(s, value)
        later = loss
    write(SECTIONS, vapour + later + 0.5 * gained)
    for c in range(SECTIONS + 1, COUNT):
        write(c, moved(c))


def inner_kernel(
    cells_ref, low_ref, high_ref, deposit_ref, rate_ref, out_hbm, token_hbm, out_ref, token_ref, sems
):
    last = cells_ref.shape[1] - 1
    token_ref[...] = jnp.zeros(token_ref.shape, F32)
    token = pltpu.make_async_copy(token_ref, token_hbm, sems.at[0])
    token.start()

    def store(x):
        return pltpu.make_async_copy(out_ref.at[:, x], out_hbm.at[:, x], sems.at[x])

    def middle(x, unused):
        def write(c, value):
            out_ref[c, x] = value + deposit_ref[c, x] if c < SECTIONS else value

        slab_update(
            lambda c: cells_ref[c, x - 1],
            lambda c: cells_ref[c, x],
            lambda c: cells_ref[c, x + 1],
            lambda c: low_ref[c, pl.ds(x, 1), :],
            lambda c: high_ref[c, pl.ds(x, 1), :],
            rate_ref,
            write,
        )
        store(x).start()
        return unused

    lax.fori_loop(1, last, middle, 0)
    for x in range(1, last):
        store(x).wait()
    token.wait()


def inner(cells, low, high, deposited, rate):
    out = jax.ShapeDtypeStruct((COUNT,) + cells.shape[1:], F32)
    token = jax.ShapeDtypeStruct((8, LANES), F32)
    return call(
        inner_kernel, [out, token], (cells, low, high, deposited, rate),
        [pltpu.VMEM(out.shape, F32), pltpu.VMEM(token.shape, F32), pltpu.SemaphoreType.DMA((cells.shape[1],))],
        in_specs=[VMEM] * 4 + [SMEM], flops=30 << 20, moved_bytes=4 << 20,
    )


def edge_kernel(
    cells_ref, inner_hbm, before_ref, after_ref, low_ref, high_ref, deposit_ref, rate_ref, out_hbm, out_ref, sems
):
    last = cells_ref.shape[1] - 1
    copies = [
        pltpu.make_async_copy(out_ref.at[:, 0], out_hbm.at[:, 0], sems.at[0]),
        pltpu.make_async_copy(out_ref.at[:, 1], out_hbm.at[:, last], sems.at[1]),
    ]

    def layer(left, number, x, right):
        def write(c, value):
            out_ref[c, number] = value + deposit_ref[c, x] if c < SECTIONS else value

        slab_update(
            left,
            lambda c: cells_ref[c, x],
            right,
            lambda c: low_ref[c, x : x + 1, :],
            lambda c: high_ref[c, x : x + 1, :],
            rate_ref,
            write,
        )
        copies[number].start()

    layer(lambda c: before_ref[c], 0, 0, lambda c: cells_ref[c, 1])
    layer(lambda c: cells_ref[c, last - 1], 1, last, lambda c: after_ref[c])
    copies[0].wait()
    copies[1].wait()


def edges(cells, inner_cells, before, after, low, high, deposited, rate):
    size_y, size_z = cells.shape[2:]
    return call(
        edge_kernel, jax.ShapeDtypeStruct(inner_cells.shape, F32),
        (cells, inner_cells, before, after, low, high, deposited, rate),
        [
            pltpu.VMEM((COUNT, 2, size_y, size_z), F32),
            pltpu.SemaphoreType.DMA((2,)),
        ],
        in_specs=[VMEM, ANY] + [VMEM] * 5 + [SMEM], aliases={1: 0}, flops=10 << 20, moved_bytes=2 << 20,
    )


def deposit_kernel(shape, windows, routed_ref, out_ref, mass_ref, spread_ref, depth_ref):
    size_x, size_y, size_z = shape
    groups = routed_ref.shape[0] // 9
    per = groups // 8
    span = LANES // per
    lane_part = quotient(iota((8, LANES), 1), span)
    for v in range(9):
        rows = routed_ref[pl.ds(v, groups, stride=9), :]
        for q in range(per):
            total = None
            for g in range(per):
                block = rows[8 * g : 8 * g + 8]
                if g != q:
                    block = pltpu.roll(block, (span * (g - q)) % LANES, 1)
                total = block if total is None else jnp.where(lane_part == g, block, total)
            mass_ref[q, v] = total

    bounds = []
    for q in range(per):
        cell = mass_ref[q, SECTIONS].astype(jnp.int32)
        layer = quotient(cell, size_y * size_z)
        valid = cell >= 0
        bounds.append((jnp.min(jnp.where(valid, layer, size_x)), jnp.max(jnp.where(valid, layer, -1))))

    zero = jnp.zeros((size_y, LANES), BF16)

    def deposit(q, start):
        window = windows[q]
        half = SECTIONS * window * size_y
        first = jnp.minimum(start, size_x - window)
        cell = mass_ref[q, SECTIONS].astype(jnp.int32)
        plane = quotient(cell, size_z)
        depth = cell - plane * size_z
        plane = jnp.where(plane >= start * size_y, plane - first * size_y, -1)
        plane = jnp.where(cell >= 0, plane, -1).astype(F32)
        parts = [split(mass_ref[q, s]) for s in range(SECTIONS)]
        for i in range(8):
            at = slice(i * LANES, (i + 1) * LANES)
            depth_ref[q % 2, :, at] = hot_columns(depth[i : i + 1], size_z)
            plane_rows = rows_of(plane[i : i + 1], size_y)
            rows = [[rows_of(part[i : i + 1].astype(F32), size_y) for part in pair] for pair in parts]
            for w in range(window):
                hit = plane_rows == packed(iota((size_y, LANES), 0) + w * size_y)
                for s in range(SECTIONS):
                    base = (s * window + w) * size_y
                    for part in range(2):
                        spread_ref[q % 2, part * half + base : part * half + base + size_y, at] = jnp.where(
                            hit, rows[s][part], zero
                        )
        added = contract_lanes(spread_ref[q % 2, : 2 * half], depth_ref[q % 2])
        for s in range(SECTIONS):
            base = s * window * size_y
            rows = added[base : base + window * size_y] + added[half + base : half + base + window * size_y]
            at = pl.ds(first, window)
            out_ref[s, at] = out_ref[s, at] + rows.reshape(window, size_y, size_z)

    out_ref[...] = jnp.zeros(out_ref.shape, F32)
    for q in range(per):
        deposit(q, bounds[q][0] if windows[q] < size_x else 0)
    for q in range(per):
        if windows[q] < size_x:
            low, high = bounds[q]

            def more(t, unused, q=q, low=low):
                deposit(q, low + t * windows[q])
                return unused

            lax.fori_loop(1, jnp.where(high - low < windows[q], 1, 1 + (size_x - 1) // windows[q]), more, 0)


def deposit(routed, shape, windows):
    size_x, size_y, size_z = shape
    per = routed.shape[0] // 9 // 8
    return call(
        functools.partial(deposit_kernel, shape, windows), jax.ShapeDtypeStruct((SECTIONS,) + shape, F32), (routed,),
        [
            pltpu.VMEM((per, SECTIONS + 1, 8, LANES), F32),
            pltpu.VMEM((2, 2 * SECTIONS * max(windows) * size_y, 8 * LANES), BF16),
            pltpu.VMEM((2, size_z, 8 * LANES), BF16),
        ],
        in_specs=[VMEM], out_specs=VMEM, flops=1 << 30, moved_bytes=2 << 20,
    )


def ring(size):
    up = [(i, (i + 1) % size) for i in range(size)]
    return up, [(j, i) for i, j in up]


def on_device(cell_state, evap_rate, parcels, crossing, conv_mass, conv_owner, conv_cell):
    owner_total = lax.axis_size("gx") * lax.axis_size("gy")
    row_total = conv_owner.shape[0]
    capacity = 2 * row_total // owner_total
    up_x, down_x = ring(lax.axis_size("gx"))
    up_y, down_y = ring(lax.axis_size("gy"))

    send_up, send_down, side_up, side_down, advanced, hot, filled = prepare(
        cell_state, parcels, crossing, conv_mass, conv_owner.reshape(-1, LANES), conv_cell.reshape(-1, LANES),
        owner_total, capacity,
    )
    before = lax.ppermute(send_up, "gx", up_x)
    after = lax.ppermute(send_down, "gx", down_x)
    low = lax.ppermute(side_up, "gy", up_y)
    high = lax.ppermute(side_down, "gy", down_y)

    fold = LANES // capacity
    filled = filled.reshape(-1, 9, fold, capacity).transpose(0, 2, 1, 3).reshape(owner_total, 1, 9 * capacity)
    routed = lax.all_to_all(filled, ("gx", "gy"), split_axis=0, concat_axis=0, tiled=True)
    routed = routed.reshape(-1, fold, 9, capacity).transpose(0, 2, 1, 3).reshape(-1, LANES)

    layers = cell_state.shape[1]
    parts = routed.shape[0] // 9 // 8
    windows = [layers] * parts
    if fold == 1:
        windows = [layers * (min(q + 2, parts) - max(q - 1, 0)) // parts for q in range(parts)]
    deposited = deposit(routed, cell_state.shape[1:], windows)
    inner_cells, token = inner(cell_state, low, high, deposited, evap_rate)
    new_parcels = arrive(token, advanced, hot, crossing, before, after)
    new_cells = edges(cell_state, inner_cells, before, after, low, high, deposited, evap_rate)
    return (new_cells, new_parcels)


def solution(mesh):
    in_specs = (
        P(None, "gx", "gy", None),
        P(),
        P(None, ("gx", "gy")),
        P(None, ("gx", "gy")),
        P(None, ("gx", "gy")),
        P(("gx", "gy"), None),
        P(("gx", "gy")),
    )
    out_specs = (P(None, "gx", "gy", None), P(None, ("gx", "gy")))
    return jax.shard_map(
        on_device, mesh=mesh, in_specs=in_specs, out_specs=out_specs, check_vma=False
    )
```

```python
import functools

import jax
import jax.numpy as jnp
from jax import lax
from jax.experimental import pallas as pl
from jax.experimental.pallas import tpu as pltpu
from jax.sharding import PartitionSpec as P

SECTIONS = 8
SPECIES = 6
COUNT = SECTIONS + SPECIES
LANES = 128
WIDE = 256
GROUPS = 4
F32 = jnp.float32
BF16 = jnp.bfloat16
ANY = pl.BlockSpec(memory_space=pl.ANY)
SMEM = pl.BlockSpec(memory_space=pltpu.SMEM)
VMEM = pl.BlockSpec(memory_space=pltpu.VMEM)
ALL = 63 << 20
MOST = 32 << 20


def call(kernel, out_shape, operands, scratch, in_specs=None, out_specs=ANY, aliases=None, flops=0, moved_bytes=0, grant=MOST):
    many = isinstance(out_shape, (list, tuple))
    return pl.pallas_call(
        kernel,
        out_shape=out_shape,
        in_specs=in_specs or [ANY] * len(operands),
        out_specs=[out_specs] * len(out_shape) if many else out_specs,
        scratch_shapes=scratch,
        input_output_aliases=aliases or {},
        compiler_params=pltpu.CompilerParams(vmem_limit_bytes=grant),
        cost_estimate=pl.CostEstimate(flops=flops, bytes_accessed=moved_bytes, transcendentals=0),
    )(*operands)


def iota(shape, axis):
    return lax.broadcasted_iota(jnp.int32, shape, axis)


def quotient(value, count):
    return value >> (count.bit_length() - 1) if count & (count - 1) == 0 else value // count


def packed(value):
    return value.astype(F32).astype(BF16)


def split(value):
    coarse = value.astype(BF16)
    return coarse, (value - coarse.astype(F32)).astype(BF16)


def rows_of(row, count):
    return jnp.broadcast_to(row, (count, row.shape[1])).astype(BF16)


def hot_columns(lower, count):
    return jnp.where(rows_of(lower.astype(F32), count) == packed(iota((count, LANES), 0)), 1.0, 0.0).astype(BF16)


def contract_lanes(left, right):
    return lax.dot_general(left, right, (((1,), (1,)), ((), ())), preferred_element_type=F32)


def advance_block(block):
    row = iota(block.shape, 0)
    diameter = jnp.broadcast_to(block[6:7], block.shape)
    warmth = jnp.broadcast_to(block[7:8], block.shape)
    factor = 0.8 / (1.0 + diameter * diameter)
    slowed = block * (1.0 - factor)
    travel = pltpu.roll(0.5 * (block + slowed), 5, 0)
    shrunk = block * (1.0 - 0.05 * warmth)
    warmed = block + factor * (1.0 - block)
    return jnp.where(row < 3, block + travel, jnp.where(row < 6, slowed, jnp.where(row == 6, shrunk, warmed)))


def scatter_left(left_ref, at, upper, uppers, coarse, fine):
    upper = rows_of(upper.astype(F32), 16)
    twice_coarse = jnp.concatenate([coarse.astype(F32)] * 2, axis=0).astype(BF16)
    twice_fine = jnp.concatenate([fine.astype(F32)] * 2, axis=0).astype(BF16)
    zero = jnp.zeros((16, LANES), BF16)
    pair = iota((16, LANES), 0) // 8
    for u in range(0, uppers, 2):
        hit = upper == packed(pair + u)
        left_ref[8 * u : 8 * u + 16, at] = jnp.where(hit, twice_coarse, zero)
        left_ref[8 * (uppers + u) : 8 * (uppers + u) + 16, at] = jnp.where(hit, twice_fine, zero)


def bucket_into(owner_total, capacity, cell_total, mass_ref, owner_ref, cell_ref, out_ref, left_ref, hot_ref):
    blocks = owner_ref.shape[0]
    uppers = out_ref.shape[0] // 9 // 2
    strict = iota((LANES, 2 * LANES), 0) < iota((LANES, 2 * LANES), 1)
    strict = jnp.where(strict, 1.0, 0.0).astype(BF16)
    owners = owner_ref[...]
    cells = cell_ref[...]
    keys = owner_total * GROUPS
    order = owners * GROUPS + quotient(cells, cell_total // GROUPS)
    hots = [
        jnp.where(jnp.broadcast_to(order[b : b + 1], (keys, LANES)) == iota((keys, LANES), 0), 1.0, 0.0)
        for b in range(blocks)
    ]
    ranks = jnp.dot(jnp.concatenate(hots, axis=0).astype(BF16), strict, preferred_element_type=F32)
    parts = [ranks[b * keys : (b + 1) * keys] for b in range(blocks)]
    counts = sum(part[:, LANES:] for part in parts)
    key, other = iota((keys, keys), 0), iota((keys, keys), 1)
    same = quotient(key, GROUPS) == quotient(other, GROUPS)
    sums = jnp.concatenate([jnp.where(same & (other < key), 1.0, 0.0), jnp.where(same, 1.0, 0.0)], axis=0).astype(BF16)
    sums = jnp.dot(sums, counts.astype(BF16), preferred_element_type=F32)
    carry, owned = sums[:keys], sums[keys:]
    base = 16 * uppers
    for b in range(blocks):
        rank = jnp.sum(hots[b] * (parts[b][:, :LANES] + carry), axis=0, keepdims=True)
        total = jnp.sum(hots[b] * owned, axis=0, keepdims=True)
        carry = carry + parts[b][:, LANES:]
        spot = owners[b : b + 1] * capacity + ((rank * float(capacity) + 0.5) / total).astype(jnp.int32)
        at = slice(b * LANES, (b + 1) * LANES)
        hot_ref[:, at] = hot_columns(spot & (WIDE - 1), WIDE)
        coarse, fine = split(mass_ref[:, at])
        upper = spot >> 8
        scatter_left(left_ref, at, upper, uppers, coarse, fine)
        hit = rows_of(upper.astype(F32), uppers) == packed(iota((uppers, LANES), 0))
        zero = jnp.zeros((uppers, LANES), BF16)
        cell = cells[b : b + 1]
        left_ref[base : base + uppers, at] = jnp.where(hit, rows_of((cell >> 8).astype(F32), uppers), zero)
        left_ref[base + uppers : base + 2 * uppers, at] = jnp.where(
            hit, rows_of((cell & (WIDE - 1)).astype(F32), uppers), zero
        )
        left_ref[base + 2 * uppers : base + 3 * uppers, at] = jnp.where(hit, 1.0, 0.0).astype(BF16)
    placed = contract_lanes(left_ref[...], hot_ref[...])
    cell = placed[base : base + uppers] * float(WIDE) + placed[base + uppers : base + 2 * uppers]
    cell = jnp.where(placed[base + 2 * uppers : base + 3 * uppers] > 0.5, cell, -1.0)
    for u in range(uppers):
        mass = placed[8 * u : 8 * u + 8] + placed[8 * (uppers + u) : 8 * (uppers + u) + 8]
        for half in range(2):
            row = 9 * (2 * u + half)
            lanes = slice(half * LANES, (half + 1) * LANES)
            out_ref[row : row + 8, :] = mass[:, lanes]
            out_ref[row + 8 : row + 9, :] = cell[u : u + 1, lanes]


def prepare_kernel(
    owner_total, capacity,
    cells_hbm, parcels_hbm, crossing_hbm, mass_hbm, owner_hbm, cell_hbm,
    up_hbm, down_hbm, yup_hbm, ydown_hbm, advanced_hbm, hot_hbm, filled_hbm,
    cells_ref, parcels_ref, crossing_ref, mass_ref, owner_ref, cell_ref,
    leave_ref, yup_ref, ydown_ref, advanced_ref, hot_ref, filled_ref,
    parts_ref, left_ref, spot_ref, sems,
):
    size_x, size_y, size_z = cells_hbm.shape[1:]
    face = slice(0, COUNT + 1)
    tail = slice(COUNT + 1, up_hbm.shape[0])
    pairs = [
        (crossing_hbm, crossing_ref),
        (owner_hbm, owner_ref),
        (cell_hbm, cell_ref),
        (mass_hbm, mass_ref),
        (parcels_hbm, parcels_ref),
        (cells_hbm, cells_ref),
        (cells_ref.at[face, size_x - 1], up_hbm.at[face]),
        (cells_ref.at[face, 0], down_hbm.at[face]),
        (filled_ref, filled_hbm),
        (hot_ref, hot_hbm),
        (advanced_ref, advanced_hbm),
        (leave_ref.at[0], up_hbm.at[tail]),
        (leave_ref.at[1], down_hbm.at[tail]),
        (yup_ref, yup_hbm),
        (ydown_ref, ydown_hbm),
    ]
    copies = [pltpu.make_async_copy(source, target, sems.at[i]) for i, (source, target) in enumerate(pairs)]
    for copy in copies[:6]:
        copy.start()
    cross = crossing_ref.shape[1]
    slot_total = parcels_ref.shape[1]
    copies[0].wait()
    for side in range(2):
        for first in range(0, cross, LANES):
            lower = crossing_ref[side : side + 1, first : first + LANES] & (WIDE - 1)
            hot_ref[:, side * cross + first : side * cross + first + LANES] = hot_columns(lower, WIDE)
    copies[9].start()
    copies[4].wait()

    def advance_pair(i, unused):
        for number in range(2):
            blocks = []
            for half in range(2):
                at = pl.ds(pl.multiple_of((4 * i + 2 * number + half) * LANES, LANES), LANES)
                block = advance_block(parcels_ref[:, at])
                advanced_ref[:, at] = block
                blocks.append(block)
            parts_ref[pl.ds(pl.multiple_of((2 * i + number) * 8, 8), 8), :] = jnp.concatenate(blocks, axis=1)
        return unused

    lax.fori_loop(0, slot_total // (4 * LANES), advance_pair, 0, unroll=4)
    copies[10].start()
    for copy in (*copies[1:4], copies[5]):
        copy.wait()
    copies[6].start()
    copies[7].start()

    halves_y, halves_z = size_y // 8, size_z // LANES
    part_rows = parts_ref.shape[0]
    step_rows = min(256, part_rows)
    for rows in range(0, part_rows, step_rows):
        coarse, fine = split(parts_ref[rows : rows + step_rows])
        for side in range(2):
            for first in range(0, cross, WIDE):
                upper = jnp.broadcast_to(crossing_ref[side : side + 1, first : first + WIDE] >> 8, (8, WIDE))
                hot = hot_ref[:, side * cross + first : side * cross + first + WIDE]
                picked = jnp.dot(coarse, hot, preferred_element_type=F32) + jnp.dot(
                    fine, hot, preferred_element_type=F32
                )
                spots = []
                for offset in range(0, WIDE, LANES):
                    layer, rest = divmod((first + offset) // LANES, halves_y * halves_z)
                    half_y, half_z = divmod(rest, halves_z)
                    spots.append((side, layer, slice(8 * half_y, 8 * half_y + 8), slice(LANES * half_z, LANES * (half_z + 1))))
                if rows:
                    total = jnp.concatenate([leave_ref[spot] for spot in spots], axis=1)
                else:
                    total = jnp.zeros((8, WIDE), F32)
                for i in range(0, step_rows, 8):
                    total = jnp.where(upper == (rows + i) // 8, picked[i : i + 8], total)
                for number, spot in enumerate(spots):
                    leave_ref[spot] = total[:, number * LANES : (number + 1) * LANES]
    bucket_into(owner_total, capacity, size_x * size_y * size_z, mass_ref, owner_ref, cell_ref, filled_ref, left_ref, spot_ref)
    copies[8].start()
    for c in range(COUNT + 1):
        source = c if c < COUNT else COUNT + 1
        yup_ref[c] = cells_ref[source, :, size_y - 1, :]
        ydown_ref[c] = cells_ref[source, :, 0, :]
    for copy in copies[11:]:
        copy.start()
    for copy in copies[6:]:
        copy.wait()


def prepare(cells, parcels, crossing, mass, owner, cell, owner_total, capacity):
    size_x, size_y, size_z = cells.shape[1:]
    extra = 8 * crossing.shape[1] // (size_y * size_z)
    places = owner_total * capacity
    shape = jax.ShapeDtypeStruct
    face = shape((COUNT + 1 + extra, size_y, size_z), F32)
    side = shape((COUNT + 1, size_x, size_z), F32)
    advanced = shape(parcels.shape, F32)
    hot = shape((WIDE, crossing.size), BF16)
    filled = shape((9 * places // LANES, LANES), F32)
    operands = (cells, parcels, crossing, mass, owner, cell)
    scratch = [pltpu.VMEM(a.shape, a.dtype) for a in operands]
    scratch += [pltpu.VMEM((2, extra, size_y, size_z), F32)]
    scratch += [pltpu.VMEM(a.shape, a.dtype) for a in (side, side, advanced, hot, filled)]
    scratch += [
        pltpu.VMEM((8 * parcels.shape[1] // WIDE, WIDE), F32),
        pltpu.VMEM((19 * places // WIDE, mass.shape[1]), BF16),
        pltpu.VMEM((WIDE, mass.shape[1]), BF16),
        pltpu.SemaphoreType.DMA((15,)),
    ]
    return call(
        functools.partial(prepare_kernel, owner_total, capacity),
        [face, face, side, side, advanced, hot, filled], operands, scratch,
        flops=2 << 30, moved_bytes=6 << 20, grant=ALL,
    )


def arrive_kernel(unused, advanced_ref, hot_ref, crossing_ref, before_ref, after_ref, out_hbm, out_ref, left_ref, sems):
    cross = crossing_ref.shape[1]
    uppers = advanced_ref.shape[1] // WIDE
    size_y, size_z = before_ref.shape[1:]
    halves_y, halves_z = size_y // 8, size_z // LANES
    for side, come_ref in ((0, before_ref), (1, after_ref)):
        for first in range(0, cross, LANES):
            layer, rest = divmod(first // LANES, halves_y * halves_z)
            half_y, half_z = divmod(rest, halves_z)
            block = come_ref[COUNT + 1 + layer, 8 * half_y : 8 * half_y + 8, LANES * half_z : LANES * (half_z + 1)]
            coarse, fine = split(block)
            upper = crossing_ref[side : side + 1, first : first + LANES] >> 8
            at = slice(side * cross + first, side * cross + first + LANES)
            scatter_left(left_ref, at, upper, uppers, coarse, fine)
            hit = rows_of(upper.astype(F32), uppers) == packed(iota((uppers, LANES), 0))
            left_ref[16 * uppers :, at] = jnp.where(hit, 1.0, 0.0).astype(BF16)
    hit = contract_lanes(left_ref[16 * uppers :], hot_ref[...])
    step = min(32, uppers)
    outs = []
    for u in range(0, uppers, step):
        total = contract_lanes(left_ref[8 * u : 8 * (u + step)], hot_ref[...]) + contract_lanes(
            left_ref[8 * (uppers + u) : 8 * (uppers + u + step)], hot_ref[...]
        )
        for i in range(step):
            at = slice((u + i) * WIDE, (u + i + 1) * WIDE)
            taken = jnp.broadcast_to(hit[u + i : u + i + 1], (8, WIDE)) > 0.5
            out_ref[:, at] = jnp.where(taken, total[8 * i : 8 * i + 8], advanced_ref[:, at])
        at = slice(u * WIDE, (u + step) * WIDE)
        out = pltpu.make_async_copy(out_ref.at[:, at], out_hbm.at[:, at], sems.at[len(outs)])
        out.start()
        outs.append(out)
    for out in outs:
        out.wait()


def arrive(earlier, advanced, hot, crossing, before, after):
    uppers = advanced.shape[1] // WIDE
    return call(
        arrive_kernel, jax.ShapeDtypeStruct(advanced.shape, F32), (earlier, advanced, hot, crossing, before, after),
        [
            pltpu.VMEM(advanced.shape, F32),
            pltpu.VMEM((17 * uppers, crossing.size), BF16),
            pltpu.SemaphoreType.DMA((-(-uppers // 32),)),
        ],
        in_specs=[ANY] + [VMEM] * 5, flops=1 << 30, moved_bytes=3 << 20,
    )


def shift_up(value, axis):
    return pltpu.roll(value, value.shape[axis] - 1, axis)


def shift_down(value, axis):
    return pltpu.roll(value, 1, axis)


def slab_update(left, center, right, side_low, side_high, rate_ref, write):
    course = center(COUNT)
    size_y, size_z = course.shape
    first_row = iota((size_y, size_z), 0) == 0
    last_row = iota((size_y, size_z), 0) == size_y - 1

    def row_up(value, edge):
        return jnp.where(last_row, edge, shift_up(value, 0))

    def row_down(value, edge):
        return jnp.where(first_row, edge, shift_down(value, 0))

    face_x = 0.5 * (course + right(COUNT))
    face_x_low = 0.5 * (left(COUNT) + course)
    course_y = center(COUNT + 1)
    face_y = 0.5 * (course_y + row_up(course_y, side_high(COUNT)))
    face_y_low = 0.5 * (row_down(course_y, side_low(COUNT)) + course_y)
    course_z = center(COUNT + 2)
    lane = iota((size_y, size_z), 1)
    face_z = jnp.where(lane == size_z - 1, 0.0, 0.5 * (course_z + shift_up(course_z, 1)))
    face_z_low = jnp.where(lane == 0, 0.0, 0.5 * (shift_down(course_z, 1) + course_z))
    from_x_up, from_x_low = jnp.minimum(face_x, 0.0), jnp.maximum(face_x_low, 0.0)
    from_y_up, from_y_low = jnp.minimum(face_y, 0.0), jnp.maximum(face_y_low, 0.0)
    from_z_up, from_z_low = jnp.minimum(face_z, 0.0), jnp.maximum(face_z_low, 0.0)
    own = 1.0 - (
        (jnp.maximum(face_x, 0.0) - jnp.minimum(face_x_low, 0.0))
        + (jnp.maximum(face_y, 0.0) - jnp.minimum(face_y_low, 0.0))
        + (jnp.maximum(face_z, 0.0) - jnp.minimum(face_z_low, 0.0))
    )

    def moved(c):
        amount = center(c)
        total = own * amount
        total = total - from_x_up * right(c) + from_x_low * left(c)
        total = total - from_y_up * row_up(amount, side_high(c)) + from_y_low * row_down(amount, side_low(c))
        return total - from_z_up * shift_up(amount, 1) + from_z_low * shift_down(amount, 1)

    vapour = moved(SECTIONS)
    beside = 1.0 + vapour
    later = None
    gained = None
    for s in reversed(range(SECTIONS)):
        section = moved(s)
        loss = rate_ref[s] * section / beside
        value = section - loss
        if later is not None:
            value = value + 0.5 * later
            gained = later if gained is None else gained + later
        write(s, value)
        later = loss
    write(SECTIONS, vapour + later + 0.5 * gained)
    for c in range(SECTIONS + 1, COUNT):
        write(c, moved(c))


def inner_kernel(
    cells_ref, low_ref, high_ref, deposit_ref, rate_ref, out_hbm, token_hbm, out_ref, token_ref, sems
):
    last = cells_ref.shape[1] - 1
    token_ref[...] = jnp.zeros(token_ref.shape, F32)
    token = pltpu.make_async_copy(token_ref, token_hbm, sems.at[0])
    token.start()

    def store(x):
        return pltpu.make_async_copy(out_ref.at[:, x], out_hbm.at[:, x], sems.at[x])

    def middle(x, unused):
        def write(c, value):
            out_ref[c, x] = value + deposit_ref[c, x] if c < SECTIONS else value

        slab_update(
            lambda c: cells_ref[c, x - 1],
            lambda c: cells_ref[c, x],
            lambda c: cells_ref[c, x + 1],
            lambda c: low_ref[c, pl.ds(x, 1), :],
            lambda c: high_ref[c, pl.ds(x, 1), :],
            rate_ref,
            write,
        )
        store(x).start()
        return unused

    lax.fori_loop(1, last, middle, 0)
    for x in range(1, last):
        store(x).wait()
    token.wait()


def inner(cells, low, high, deposited, rate):
    out = jax.ShapeDtypeStruct((COUNT,) + cells.shape[1:], F32)
    token = jax.ShapeDtypeStruct((8, LANES), F32)
    return call(
        inner_kernel, [out, token], (cells, low, high, deposited, rate),
        [pltpu.VMEM(out.shape, F32), pltpu.VMEM(token.shape, F32), pltpu.SemaphoreType.DMA((cells.shape[1],))],
        in_specs=[VMEM] * 4 + [SMEM], flops=30 << 20, moved_bytes=4 << 20,
    )


def edge_kernel(
    cells_ref, inner_hbm, before_ref, after_ref, low_ref, high_ref, deposit_ref, rate_ref, out_hbm, out_ref, sems
):
    last = cells_ref.shape[1] - 1
    copies = [
        pltpu.make_async_copy(out_ref.at[:, 0], out_hbm.at[:, 0], sems.at[0]),
        pltpu.make_async_copy(out_ref.at[:, 1], out_hbm.at[:, last], sems.at[1]),
    ]

    def layer(left, number, x, right):
        def write(c, value):
            out_ref[c, number] = value + deposit_ref[c, x] if c < SECTIONS else value

        slab_update(
            left,
            lambda c: cells_ref[c, x],
            right,
            lambda c: low_ref[c, x : x + 1, :],
            lambda c: high_ref[c, x : x + 1, :],
            rate_ref,
            write,
        )
        copies[number].start()

    layer(lambda c: before_ref[c], 0, 0, lambda c: cells_ref[c, 1])
    layer(lambda c: cells_ref[c, last - 1], 1, last, lambda c: after_ref[c])
    copies[0].wait()
    copies[1].wait()


def edges(cells, inner_cells, before, after, low, high, deposited, rate):
    size_y, size_z = cells.shape[2:]
    return call(
        edge_kernel, jax.ShapeDtypeStruct(inner_cells.shape, F32),
        (cells, inner_cells, before, after, low, high, deposited, rate),
        [
            pltpu.VMEM((COUNT, 2, size_y, size_z), F32),
            pltpu.SemaphoreType.DMA((2,)),
        ],
        in_specs=[VMEM, ANY] + [VMEM] * 5 + [SMEM], aliases={1: 0}, flops=10 << 20, moved_bytes=2 << 20,
    )


def deposit_kernel(shape, windows, routed_ref, out_ref, mass_ref, spread_ref, depth_ref):
    size_x, size_y, size_z = shape
    groups = routed_ref.shape[0] // 9
    per = groups // 8
    span = LANES // per
    lane_part = quotient(iota((8, LANES), 1), span)
    for v in range(9):
        rows = routed_ref[pl.ds(v, groups, stride=9), :]
        for q in range(per):
            total = None
            for g in range(per):
                block = rows[8 * g : 8 * g + 8]
                if g != q:
                    block = pltpu.roll(block, (span * (g - q)) % LANES, 1)
                total = block if total is None else jnp.where(lane_part == g, block, total)
            mass_ref[q, v] = total

    bounds = []
    for q in range(per):
        cell = mass_ref[q, SECTIONS].astype(jnp.int32)
        layer = quotient(cell, size_y * size_z)
        valid = cell >= 0
        bounds.append((jnp.min(jnp.where(valid, layer, size_x)), jnp.max(jnp.where(valid, layer, -1))))

    zero = jnp.zeros((size_y, LANES), BF16)

    def deposit(q, start):
        window = windows[q]
        half = SECTIONS * window * size_y
        first = jnp.minimum(start, size_x - window)
        cell = mass_ref[q, SECTIONS].astype(jnp.int32)
        plane = quotient(cell, size_z)
        depth = cell - plane * size_z
        plane = jnp.where(plane >= start * size_y, plane - first * size_y, -1)
        plane = jnp.where(cell >= 0, plane, -1).astype(F32)
        parts = [split(mass_ref[q, s]) for s in range(SECTIONS)]
        for i in range(8):
            at = slice(i * LANES, (i + 1) * LANES)
            depth_ref[q % 2, :, at] = hot_columns(depth[i : i + 1], size_z)
            plane_rows = rows_of(plane[i : i + 1], size_y)
            rows = [[rows_of(part[i : i + 1].astype(F32), size_y) for part in pair] for pair in parts]
            for w in range(window):
                hit = plane_rows == packed(iota((size_y, LANES), 0) + w * size_y)
                for s in range(SECTIONS):
                    base = (s * window + w) * size_y
                    for part in range(2):
                        spread_ref[q % 2, part * half + base : part * half + base + size_y, at] = jnp.where(
                            hit, rows[s][part], zero
                        )
        added = contract_lanes(spread_ref[q % 2, : 2 * half], depth_ref[q % 2])
        for s in range(SECTIONS):
            base = s * window * size_y
            rows = added[base : base + window * size_y] + added[half + base : half + base + window * size_y]
            at = pl.ds(first, window)
            out_ref[s, at] = out_ref[s, at] + rows.reshape(window, size_y, size_z)

    out_ref[...] = jnp.zeros(out_ref.shape, F32)
    for q in range(per):
        deposit(q, bounds[q][0] if windows[q] < size_x else 0)
    for q in range(per):
        if windows[q] < size_x:
            low, high = bounds[q]

            def more(t, unused, q=q, low=low):
                deposit(q, low + t * windows[q])
                return unused

            lax.fori_loop(1, jnp.where(high - low < windows[q], 1, 1 + (size_x - 1) // windows[q]), more, 0)


def deposit(routed, shape, windows):
    size_x, size_y, size_z = shape
    per = routed.shape[0] // 9 // 8
    return call(
        functools.partial(deposit_kernel, shape, windows), jax.ShapeDtypeStruct((SECTIONS,) + shape, F32), (routed,),
        [
            pltpu.VMEM((per, SECTIONS + 1, 8, LANES), F32),
            pltpu.VMEM((2, 2 * SECTIONS * max(windows) * size_y, 8 * LANES), BF16),
            pltpu.VMEM((2, size_z, 8 * LANES), BF16),
        ],
        in_specs=[VMEM], out_specs=VMEM, flops=1 << 30, moved_bytes=2 << 20,
    )


def ring(size):
    up = [(i, (i + 1) % size) for i in range(size)]
    return up, [(j, i) for i, j in up]


def on_device(cell_state, evap_rate, parcels, crossing, conv_mass, conv_owner, conv_cell):
    owner_total = lax.axis_size("gx") * lax.axis_size("gy")
    row_total = conv_owner.shape[0]
    capacity = 2 * row_total // owner_total
    up_x, down_x = ring(lax.axis_size("gx"))
    up_y, down_y = ring(lax.axis_size("gy"))

    send_up, send_down, side_up, side_down, advanced, hot, filled = prepare(
        cell_state, parcels, crossing, conv_mass, conv_owner.reshape(-1, LANES), conv_cell.reshape(-1, LANES),
        owner_total, capacity,
    )
    before = lax.ppermute(send_up, "gx", up_x)
    after = lax.ppermute(send_down, "gx", down_x)
    low = lax.ppermute(side_up, "gy", up_y)
    high = lax.ppermute(side_down, "gy", down_y)

    fold = LANES // capacity
    filled = filled.reshape(-1, 9, fold, capacity).transpose(0, 2, 1, 3).reshape(owner_total, 1, 9 * capacity)
    routed = lax.all_to_all(filled, ("gx", "gy"), split_axis=0, concat_axis=0, tiled=True)
    routed = routed.reshape(-1, fold, 9, capacity).transpose(0, 2, 1, 3).reshape(-1, LANES)

    layers = cell_state.shape[1]
    parts = routed.shape[0] // 9 // 8
    windows = [layers] * parts
    if fold == 1:
        windows = [layers * (min(q + 2, parts) - max(q - 1, 0)) // parts for q in range(parts)]
    deposited = deposit(routed, cell_state.shape[1:], windows)
    inner_cells, token = inner(cell_state, low, high, deposited, evap_rate)
    new_parcels = arrive(token, advanced, hot, crossing, before, after)
    new_cells = edges(cell_state, inner_cells, before, after, low, high, deposited, evap_rate)
    return (new_cells, new_parcels)


def solution(mesh):
    in_specs = (
        P(None, "gx", "gy", None),
        P(),
        P(None, ("gx", "gy")),
        P(None, ("gx", "gy")),
        P(None, ("gx", "gy")),
        P(("gx", "gy"), None),
        P(("gx", "gy")),
    )
    out_specs = (P(None, "gx", "gy", None), P(None, ("gx", "gy")))
    return jax.shard_map(
        on_device, mesh=mesh, in_specs=in_specs, out_specs=out_specs, check_vma=False
    )
```

```python
import functools

import jax
import jax.numpy as jnp
from jax import lax
from jax.experimental import pallas as pl
from jax.experimental.pallas import tpu as pltpu
from jax.sharding import PartitionSpec as P

SECTIONS = 8
SPECIES = 6
COUNT = SECTIONS + SPECIES
LANES = 128
WIDE = 256
GROUPS = 2
F32 = jnp.float32
BF16 = jnp.bfloat16
ANY = pl.BlockSpec(memory_space=pl.ANY)
SMEM = pl.BlockSpec(memory_space=pltpu.SMEM)
VMEM = pl.BlockSpec(memory_space=pltpu.VMEM)
ALL = 63 << 20
MOST = 32 << 20


def call(kernel, out_shape, operands, scratch, in_specs=None, out_specs=ANY, aliases=None, flops=0, moved_bytes=0, grant=MOST):
    many = isinstance(out_shape, (list, tuple))
    return pl.pallas_call(
        kernel,
        out_shape=out_shape,
        in_specs=in_specs or [ANY] * len(operands),
        out_specs=[out_specs] * len(out_shape) if many else out_specs,
        scratch_shapes=scratch,
        input_output_aliases=aliases or {},
        compiler_params=pltpu.CompilerParams(vmem_limit_bytes=grant),
        cost_estimate=pl.CostEstimate(flops=flops, bytes_accessed=moved_bytes, transcendentals=0),
    )(*operands)


def iota(shape, axis):
    return lax.broadcasted_iota(jnp.int32, shape, axis)


def quotient(value, count):
    return value >> (count.bit_length() - 1) if count & (count - 1) == 0 else value // count


def packed(value):
    return value.astype(F32).astype(BF16)


def split(value):
    coarse = value.astype(BF16)
    return coarse, (value - coarse.astype(F32)).astype(BF16)


def rows_of(row, count):
    return jnp.broadcast_to(row, (count, row.shape[1])).astype(BF16)


def hot_columns(lower, count):
    return jnp.where(rows_of(lower.astype(F32), count) == packed(iota((count, LANES), 0)), 1.0, 0.0).astype(BF16)


def contract_lanes(left, right):
    return lax.dot_general(left, right, (((1,), (1,)), ((), ())), preferred_element_type=F32)


def advance_block(block):
    row = iota(block.shape, 0)
    diameter = jnp.broadcast_to(block[6:7], block.shape)
    warmth = jnp.broadcast_to(block[7:8], block.shape)
    factor = 0.8 / (1.0 + diameter * diameter)
    slowed = block * (1.0 - factor)
    travel = pltpu.roll(0.5 * (block + slowed), 5, 0)
    shrunk = block * (1.0 - 0.05 * warmth)
    warmed = block + factor * (1.0 - block)
    return jnp.where(row < 3, block + travel, jnp.where(row < 6, slowed, jnp.where(row == 6, shrunk, warmed)))


def scatter_left(left_ref, at, upper, uppers, coarse, fine):
    upper = rows_of(upper.astype(F32), 16)
    twice_coarse = jnp.concatenate([coarse.astype(F32)] * 2, axis=0).astype(BF16)
    twice_fine = jnp.concatenate([fine.astype(F32)] * 2, axis=0).astype(BF16)
    zero = jnp.zeros((16, LANES), BF16)
    pair = iota((16, LANES), 0) // 8
    for u in range(0, uppers, 2):
        hit = upper == packed(pair + u)
        left_ref[8 * u : 8 * u + 16, at] = jnp.where(hit, twice_coarse, zero)
        left_ref[8 * (uppers + u) : 8 * (uppers + u) + 16, at] = jnp.where(hit, twice_fine, zero)


def bucket_into(owner_total, capacity, cell_total, mass_ref, owner_ref, cell_ref, out_ref, left_ref, hot_ref):
    blocks = owner_ref.shape[0]
    uppers = out_ref.shape[0] // 9 // 2
    strict = iota((LANES, 2 * LANES), 0) < iota((LANES, 2 * LANES), 1)
    strict = jnp.where(strict, 1.0, 0.0).astype(BF16)
    owners = owner_ref[...]
    cells = cell_ref[...]
    keys = owner_total * GROUPS
    order = owners * GROUPS + quotient(cells, cell_total // GROUPS)
    hots = [
        jnp.where(jnp.broadcast_to(order[b : b + 1], (keys, LANES)) == iota((keys, LANES), 0), 1.0, 0.0)
        for b in range(blocks)
    ]
    ranks = jnp.dot(jnp.concatenate(hots, axis=0).astype(BF16), strict, preferred_element_type=F32)
    parts = [ranks[b * keys : (b + 1) * keys] for b in range(blocks)]
    counts = sum(part[:, LANES:] for part in parts)
    key, other = iota((keys, keys), 0), iota((keys, keys), 1)
    same = quotient(key, GROUPS) == quotient(other, GROUPS)
    sums = jnp.concatenate([jnp.where(same & (other < key), 1.0, 0.0), jnp.where(same, 1.0, 0.0)], axis=0).astype(BF16)
    sums = jnp.dot(sums, counts.astype(BF16), preferred_element_type=F32)
    carry, owned = sums[:keys], sums[keys:]
    base = 16 * uppers
    for b in range(blocks):
        rank = jnp.sum(hots[b] * (parts[b][:, :LANES] + carry), axis=0, keepdims=True)
        total = jnp.sum(hots[b] * owned, axis=0, keepdims=True)
        carry = carry + parts[b][:, LANES:]
        spot = owners[b : b + 1] * capacity + ((rank * float(capacity) + 0.5) / total).astype(jnp.int32)
        at = slice(b * LANES, (b + 1) * LANES)
        hot_ref[:, at] = hot_columns(spot & (WIDE - 1), WIDE)
        coarse, fine = split(mass_ref[:, at])
        upper = spot >> 8
        scatter_left(left_ref, at, upper, uppers, coarse, fine)
        hit = rows_of(upper.astype(F32), uppers) == packed(iota((uppers, LANES), 0))
        zero = jnp.zeros((uppers, LANES), BF16)
        cell = cells[b : b + 1]
        left_ref[base : base + uppers, at] = jnp.where(hit, rows_of((cell >> 8).astype(F32), uppers), zero)
        left_ref[base + uppers : base + 2 * uppers, at] = jnp.where(
            hit, rows_of((cell & (WIDE - 1)).astype(F32), uppers), zero
        )
        left_ref[base + 2 * uppers : base + 3 * uppers, at] = jnp.where(hit, 1.0, 0.0).astype(BF16)
    placed = contract_lanes(left_ref[...], hot_ref[...])
    cell = placed[base : base + uppers] * float(WIDE) + placed[base + uppers : base + 2 * uppers]
    cell = jnp.where(placed[base + 2 * uppers : base + 3 * uppers] > 0.5, cell, -1.0)
    for u in range(uppers):
        mass = placed[8 * u : 8 * u + 8] + placed[8 * (uppers + u) : 8 * (uppers + u) + 8]
        for half in range(2):
            row = 9 * (2 * u + half)
            lanes = slice(half * LANES, (half + 1) * LANES)
            out_ref[row : row + 8, :] = mass[:, lanes]
            out_ref[row + 8 : row + 9, :] = cell[u : u + 1, lanes]


def prepare_kernel(
    owner_total, capacity,
    cells_hbm, parcels_hbm, crossing_hbm, mass_hbm, owner_hbm, cell_hbm,
    up_hbm, down_hbm, yup_hbm, ydown_hbm, advanced_hbm, hot_hbm, filled_hbm,
    cells_ref, parcels_ref, crossing_ref, mass_ref, owner_ref, cell_ref,
    leave_ref, yup_ref, ydown_ref, advanced_ref, hot_ref, filled_ref,
    parts_ref, left_ref, spot_ref, sems,
):
    size_x, size_y, size_z = cells_hbm.shape[1:]
    face = slice(0, COUNT + 1)
    tail = slice(COUNT + 1, up_hbm.shape[0])
    pairs = [
        (crossing_hbm, crossing_ref),
        (owner_hbm, owner_ref),
        (cell_hbm, cell_ref),
        (mass_hbm, mass_ref),
        (parcels_hbm, parcels_ref),
        (cells_hbm, cells_ref),
        (cells_ref.at[face, size_x - 1], up_hbm.at[face]),
        (cells_ref.at[face, 0], down_hbm.at[face]),
        (filled_ref, filled_hbm),
        (hot_ref, hot_hbm),
        (advanced_ref, advanced_hbm),
        (leave_ref.at[0], up_hbm.at[tail]),
        (leave_ref.at[1], down_hbm.at[tail]),
        (yup_ref, yup_hbm),
        (ydown_ref, ydown_hbm),
    ]
    copies = [pltpu.make_async_copy(source, target, sems.at[i]) for i, (source, target) in enumerate(pairs)]
    for copy in copies[:6]:
        copy.start()
    cross = crossing_ref.shape[1]
    slot_total = parcels_ref.shape[1]
    copies[0].wait()
    for side in range(2):
        for first in range(0, cross, LANES):
            lower = crossing_ref[side : side + 1, first : first + LANES] & (WIDE - 1)
            hot_ref[:, side * cross + first : side * cross + first + LANES] = hot_columns(lower, WIDE)
    copies[9].start()
    copies[4].wait()

    def advance_pair(i, unused):
        for number in range(2):
            blocks = []
            for half in range(2):
                at = pl.ds(pl.multiple_of((4 * i + 2 * number + half) * LANES, LANES), LANES)
                block = advance_block(parcels_ref[:, at])
                advanced_ref[:, at] = block
                blocks.append(block)
            parts_ref[pl.ds(pl.multiple_of((2 * i + number) * 8, 8), 8), :] = jnp.concatenate(blocks, axis=1)
        return unused

    lax.fori_loop(0, slot_total // (4 * LANES), advance_pair, 0, unroll=4)
    copies[10].start()
    for copy in (*copies[1:4], copies[5]):
        copy.wait()
    copies[6].start()
    copies[7].start()

    halves_y, halves_z = size_y // 8, size_z // LANES
    part_rows = parts_ref.shape[0]
    step_rows = min(256, part_rows)
    for rows in range(0, part_rows, step_rows):
        coarse, fine = split(parts_ref[rows : rows + step_rows])
        for side in range(2):
            for first in range(0, cross, WIDE):
                upper = jnp.broadcast_to(crossing_ref[side : side + 1, first : first + WIDE] >> 8, (8, WIDE))
                hot = hot_ref[:, side * cross + first : side * cross + first + WIDE]
                picked = jnp.dot(coarse, hot, preferred_element_type=F32) + jnp.dot(
                    fine, hot, preferred_element_type=F32
                )
                spots = []
                for offset in range(0, WIDE, LANES):
                    layer, rest = divmod((first + offset) // LANES, halves_y * halves_z)
                    half_y, half_z = divmod(rest, halves_z)
                    spots.append((side, layer, slice(8 * half_y, 8 * half_y + 8), slice(LANES * half_z, LANES * (half_z + 1))))
                if rows:
                    total = jnp.concatenate([leave_ref[spot] for spot in spots], axis=1)
                else:
                    total = jnp.zeros((8, WIDE), F32)
                for i in range(0, step_rows, 8):
                    total = jnp.where(upper == (rows + i) // 8, picked[i : i + 8], total)
                for number, spot in enumerate(spots):
                    leave_ref[spot] = total[:, number * LANES : (number + 1) * LANES]
    bucket_into(owner_total, capacity, size_x * size_y * size_z, mass_ref, owner_ref, cell_ref, filled_ref, left_ref, spot_ref)
    copies[8].start()
    for c in range(COUNT + 1):
        source = c if c < COUNT else COUNT + 1
        yup_ref[c] = cells_ref[source, :, size_y - 1, :]
        ydown_ref[c] = cells_ref[source, :, 0, :]
    for copy in copies[11:]:
        copy.start()
    for copy in copies[6:]:
        copy.wait()


def prepare(cells, parcels, crossing, mass, owner, cell, owner_total, capacity):
    size_x, size_y, size_z = cells.shape[1:]
    extra = 8 * crossing.shape[1] // (size_y * size_z)
    places = owner_total * capacity
    shape = jax.ShapeDtypeStruct
    face = shape((COUNT + 1 + extra, size_y, size_z), F32)
    side = shape((COUNT + 1, size_x, size_z), F32)
    advanced = shape(parcels.shape, F32)
    hot = shape((WIDE, crossing.size), BF16)
    filled = shape((9 * places // LANES, LANES), F32)
    operands = (cells, parcels, crossing, mass, owner, cell)
    scratch = [pltpu.VMEM(a.shape, a.dtype) for a in operands]
    scratch += [pltpu.VMEM((2, extra, size_y, size_z), F32)]
    scratch += [pltpu.VMEM(a.shape, a.dtype) for a in (side, side, advanced, hot, filled)]
    scratch += [
        pltpu.VMEM((8 * parcels.shape[1] // WIDE, WIDE), F32),
        pltpu.VMEM((19 * places // WIDE, mass.shape[1]), BF16),
        pltpu.VMEM((WIDE, mass.shape[1]), BF16),
        pltpu.SemaphoreType.DMA((15,)),
    ]
    return call(
        functools.partial(prepare_kernel, owner_total, capacity),
        [face, face, side, side, advanced, hot, filled], operands, scratch,
        flops=2 << 30, moved_bytes=6 << 20, grant=ALL,
    )


def arrive_into(advanced_ref, hot_ref, crossing_ref, before_ref, after_ref, out_hbm, out_ref, left_ref, sems):
    cross = crossing_ref.shape[1]
    uppers = advanced_ref.shape[1] // WIDE
    size_y, size_z = before_ref.shape[1:]
    halves_y, halves_z = size_y // 8, size_z // LANES
    for side, come_ref in ((0, before_ref), (1, after_ref)):
        for first in range(0, cross, LANES):
            layer, rest = divmod(first // LANES, halves_y * halves_z)
            half_y, half_z = divmod(rest, halves_z)
            block = come_ref[COUNT + 1 + layer, 8 * half_y : 8 * half_y + 8, LANES * half_z : LANES * (half_z + 1)]
            coarse, fine = split(block)
            upper = crossing_ref[side : side + 1, first : first + LANES] >> 8
            at = slice(side * cross + first, side * cross + first + LANES)
            scatter_left(left_ref, at, upper, uppers, coarse, fine)
            hit = rows_of(upper.astype(F32), uppers) == packed(iota((uppers, LANES), 0))
            left_ref[16 * uppers :, at] = jnp.where(hit, 1.0, 0.0).astype(BF16)
    hit = contract_lanes(left_ref[16 * uppers :], hot_ref[...])
    step = min(32, uppers)
    outs = []
    for u in range(0, uppers, step):
        total = contract_lanes(left_ref[8 * u : 8 * (u + step)], hot_ref[...]) + contract_lanes(
            left_ref[8 * (uppers + u) : 8 * (uppers + u + step)], hot_ref[...]
        )
        for i in range(step):
            at = slice((u + i) * WIDE, (u + i + 1) * WIDE)
            taken = jnp.broadcast_to(hit[u + i : u + i + 1], (8, WIDE)) > 0.5
            out_ref[:, at] = jnp.where(taken, total[8 * i : 8 * i + 8], advanced_ref[:, at])
        at = slice(u * WIDE, (u + step) * WIDE)
        out = pltpu.make_async_copy(out_ref.at[:, at], out_hbm.at[:, at], sems.at[len(outs)])
        out.start()
        outs.append(out)
    return outs


def shift_up(value, axis):
    return pltpu.roll(value, value.shape[axis] - 1, axis)


def shift_down(value, axis):
    return pltpu.roll(value, 1, axis)


def slab_update(left, center, right, side_low, side_high, rate_ref, write):
    course = center(COUNT)
    size_y, size_z = course.shape
    first_row = iota((size_y, size_z), 0) == 0
    last_row = iota((size_y, size_z), 0) == size_y - 1

    def row_up(value, edge):
        return jnp.where(last_row, edge, shift_up(value, 0))

    def row_down(value, edge):
        return jnp.where(first_row, edge, shift_down(value, 0))

    face_x = 0.5 * (course + right(COUNT))
    face_x_low = 0.5 * (left(COUNT) + course)
    course_y = center(COUNT + 1)
    face_y = 0.5 * (course_y + row_up(course_y, side_high(COUNT)))
    face_y_low = 0.5 * (row_down(course_y, side_low(COUNT)) + course_y)
    course_z = center(COUNT + 2)
    lane = iota((size_y, size_z), 1)
    face_z = jnp.where(lane == size_z - 1, 0.0, 0.5 * (course_z + shift_up(course_z, 1)))
    face_z_low = jnp.where(lane == 0, 0.0, 0.5 * (shift_down(course_z, 1) + course_z))
    from_x_up, from_x_low = jnp.minimum(face_x, 0.0), jnp.maximum(face_x_low, 0.0)
    from_y_up, from_y_low = jnp.minimum(face_y, 0.0), jnp.maximum(face_y_low, 0.0)
    from_z_up, from_z_low = jnp.minimum(face_z, 0.0), jnp.maximum(face_z_low, 0.0)
    own = 1.0 - (
        (jnp.maximum(face_x, 0.0) - jnp.minimum(face_x_low, 0.0))
        + (jnp.maximum(face_y, 0.0) - jnp.minimum(face_y_low, 0.0))
        + (jnp.maximum(face_z, 0.0) - jnp.minimum(face_z_low, 0.0))
    )

    def moved(c):
        amount = center(c)
        total = own * amount
        total = total - from_x_up * right(c) + from_x_low * left(c)
        total = total - from_y_up * row_up(amount, side_high(c)) + from_y_low * row_down(amount, side_low(c))
        return total - from_z_up * shift_up(amount, 1) + from_z_low * shift_down(amount, 1)

    vapour = moved(SECTIONS)
    beside = 1.0 + vapour
    later = None
    gained = None
    for s in reversed(range(SECTIONS)):
        section = moved(s)
        loss = rate_ref[s] * section / beside
        value = section - loss
        if later is not None:
            value = value + 0.5 * later
            gained = later if gained is None else gained + later
        write(s, value)
        later = loss
    write(SECTIONS, vapour + later + 0.5 * gained)
    for c in range(SECTIONS + 1, COUNT):
        write(c, moved(c))


def inner_kernel(
    cells_ref, low_ref, high_ref, deposit_ref, rate_ref, out_hbm, out_ref, sems
):
    last = cells_ref.shape[1] - 1

    def store(x):
        return pltpu.make_async_copy(out_ref.at[:, x], out_hbm.at[:, x], sems.at[x])

    def middle(x, unused):
        def write(c, value):
            out_ref[c, x] = value + deposit_ref[c, x] if c < SECTIONS else value

        slab_update(
            lambda c: cells_ref[c, x - 1],
            lambda c: cells_ref[c, x],
            lambda c: cells_ref[c, x + 1],
            lambda c: low_ref[c, pl.ds(x, 1), :],
            lambda c: high_ref[c, pl.ds(x, 1), :],
            rate_ref,
            write,
        )
        store(x).start()
        return unused

    lax.fori_loop(1, last, middle, 0)
    for x in range(1, last):
        store(x).wait()


def inner(cells, low, high, deposited, rate):
    out = jax.ShapeDtypeStruct((COUNT,) + cells.shape[1:], F32)
    return call(
        inner_kernel, out, (cells, low, high, deposited, rate),
        [pltpu.VMEM(out.shape, F32), pltpu.SemaphoreType.DMA((cells.shape[1],))],
        in_specs=[VMEM] * 4 + [SMEM], flops=30 << 20, moved_bytes=4 << 20,
    )


def last_kernel(
    cells_ref, inner_hbm, before_ref, after_ref, low_ref, high_ref, deposit_ref, rate_ref,
    advanced_ref, hot_ref, crossing_ref, out_hbm, parcels_hbm, out_ref, parcels_ref, left_ref, sems, parcel_sems,
):
    last = cells_ref.shape[1] - 1
    copies = [
        pltpu.make_async_copy(out_ref.at[:, 0], out_hbm.at[:, 0], sems.at[0]),
        pltpu.make_async_copy(out_ref.at[:, 1], out_hbm.at[:, last], sems.at[1]),
    ]

    def layer(left, number, x, right):
        def write(c, value):
            out_ref[c, number] = value + deposit_ref[c, x] if c < SECTIONS else value

        slab_update(
            left,
            lambda c: cells_ref[c, x],
            right,
            lambda c: low_ref[c, x : x + 1, :],
            lambda c: high_ref[c, x : x + 1, :],
            rate_ref,
            write,
        )
        copies[number].start()

    layer(lambda c: before_ref[c], 0, 0, lambda c: cells_ref[c, 1])
    layer(lambda c: cells_ref[c, last - 1], 1, last, lambda c: after_ref[c])
    copies += arrive_into(
        advanced_ref, hot_ref, crossing_ref, before_ref, after_ref, parcels_hbm, parcels_ref, left_ref, parcel_sems
    )
    for copy in copies:
        copy.wait()


def finish(cells, inner_cells, before, after, low, high, deposited, rate, advanced, hot, crossing):
    size_y, size_z = cells.shape[2:]
    uppers = advanced.shape[1] // WIDE
    return call(
        last_kernel, [jax.ShapeDtypeStruct(inner_cells.shape, F32), jax.ShapeDtypeStruct(advanced.shape, F32)],
        (cells, inner_cells, before, after, low, high, deposited, rate, advanced, hot, crossing),
        [
            pltpu.VMEM((COUNT, 2, size_y, size_z), F32),
            pltpu.VMEM(advanced.shape, F32),
            pltpu.VMEM((17 * uppers, crossing.size), BF16),
            pltpu.SemaphoreType.DMA((2,)),
            pltpu.SemaphoreType.DMA((-(-uppers // 32),)),
        ],
        in_specs=[VMEM, ANY] + [VMEM] * 5 + [SMEM] + [VMEM] * 3, aliases={1: 0},
        flops=1 << 30, moved_bytes=5 << 20,
    )


def deposit_kernel(shape, windows, routed_ref, out_ref, mass_ref, spread_ref, depth_ref):
    size_x, size_y, size_z = shape
    groups = routed_ref.shape[0] // 9
    per = groups // 8
    span = LANES // per
    lane_part = quotient(iota((8, LANES), 1), span)
    for v in range(9):
        rows = routed_ref[pl.ds(v, groups, stride=9), :]
        for q in range(per):
            total = None
            for g in range(per):
                block = rows[8 * g : 8 * g + 8]
                if g != q:
                    block = pltpu.roll(block, (span * (g - q)) % LANES, 1)
                total = block if total is None else jnp.where(lane_part == g, block, total)
            mass_ref[q, v] = total

    bounds = []
    for q in range(per):
        cell = mass_ref[q, SECTIONS].astype(jnp.int32)
        layer = quotient(cell, size_y * size_z)
        valid = cell >= 0
        bounds.append((jnp.min(jnp.where(valid, layer, size_x)), jnp.max(jnp.where(valid, layer, -1))))

    zero = jnp.zeros((size_y, LANES), BF16)

    def deposit(q, start):
        window = windows[q]
        half = SECTIONS * window * size_y
        first = jnp.minimum(start, size_x - window)
        cell = mass_ref[q, SECTIONS].astype(jnp.int32)
        plane = quotient(cell, size_z)
        depth = cell - plane * size_z
        plane = jnp.where(plane >= start * size_y, plane - first * size_y, -1)
        plane = jnp.where(cell >= 0, plane, -1).astype(F32)
        parts = [split(mass_ref[q, s]) for s in range(SECTIONS)]
        for i in range(8):
            at = slice(i * LANES, (i + 1) * LANES)
            depth_ref[q % 2, :, at] = hot_columns(depth[i : i + 1], size_z)
            plane_rows = rows_of(plane[i : i + 1], size_y)
            rows = [[rows_of(part[i : i + 1].astype(F32), size_y) for part in pair] for pair in parts]
            for w in range(window):
                hit = plane_rows == packed(iota((size_y, LANES), 0) + w * size_y)
                for s in range(SECTIONS):
                    base = (s * window + w) * size_y
                    for part in range(2):
                        spread_ref[q % 2, part * half + base : part * half + base + size_y, at] = jnp.where(
                            hit, rows[s][part], zero
                        )
        added = contract_lanes(spread_ref[q % 2, : 2 * half], depth_ref[q % 2])
        for s in range(SECTIONS):
            base = s * window * size_y
            rows = added[base : base + window * size_y] + added[half + base : half + base + window * size_y]
            at = pl.ds(first, window)
            out_ref[s, at] = out_ref[s, at] + rows.reshape(window, size_y, size_z)

    out_ref[...] = jnp.zeros(out_ref.shape, F32)
    for q in range(per):
        deposit(q, bounds[q][0] if windows[q] < size_x else 0)
    for q in range(per):
        if windows[q] < size_x:
            low, high = bounds[q]

            def more(t, unused, q=q, low=low):
                deposit(q, low + t * windows[q])
                return unused

            lax.fori_loop(1, jnp.where(high - low < windows[q], 1, 1 + (size_x - 1) // windows[q]), more, 0)


def deposit(routed, shape, windows):
    size_x, size_y, size_z = shape
    per = routed.shape[0] // 9 // 8
    return call(
        functools.partial(deposit_kernel, shape, windows), jax.ShapeDtypeStruct((SECTIONS,) + shape, F32), (routed,),
        [
            pltpu.VMEM((per, SECTIONS + 1, 8, LANES), F32),
            pltpu.VMEM((2, 2 * SECTIONS * max(windows) * size_y, 8 * LANES), BF16),
            pltpu.VMEM((2, size_z, 8 * LANES), BF16),
        ],
        in_specs=[VMEM], out_specs=VMEM, flops=1 << 30, moved_bytes=2 << 20,
    )


def ring(size):
    up = [(i, (i + 1) % size) for i in range(size)]
    return up, [(j, i) for i, j in up]


def on_device(cell_state, evap_rate, parcels, crossing, conv_mass, conv_owner, conv_cell):
    owner_total = lax.axis_size("gx") * lax.axis_size("gy")
    row_total = conv_owner.shape[0]
    capacity = 2 * row_total // owner_total
    up_x, down_x = ring(lax.axis_size("gx"))
    up_y, down_y = ring(lax.axis_size("gy"))

    send_up, send_down, side_up, side_down, advanced, hot, filled = prepare(
        cell_state, parcels, crossing, conv_mass, conv_owner.reshape(-1, LANES), conv_cell.reshape(-1, LANES),
        owner_total, capacity,
    )
    before = lax.ppermute(send_up, "gx", up_x)
    after = lax.ppermute(send_down, "gx", down_x)
    low = lax.ppermute(side_up, "gy", up_y)
    high = lax.ppermute(side_down, "gy", down_y)

    fold = LANES // capacity
    filled = filled.reshape(-1, 9, fold, capacity).transpose(0, 2, 1, 3).reshape(owner_total, 1, 9 * capacity)
    routed = lax.all_to_all(filled, ("gx", "gy"), split_axis=0, concat_axis=0, tiled=True)
    routed = routed.reshape(-1, fold, 9, capacity).transpose(0, 2, 1, 3).reshape(-1, LANES)

    layers = cell_state.shape[1]
    parts = routed.shape[0] // 9 // 8
    windows = [layers] * parts
    if fold == 1:
        spans = [(max(q * GROUPS - 1, 0) // parts, ((q + 1) * GROUPS) // parts + 1) for q in range(parts)]
        windows = [layers * (min(high, GROUPS) - low) // GROUPS for low, high in spans]
    deposited = deposit(routed, cell_state.shape[1:], windows)
    inner_cells = inner(cell_state, low, high, deposited, evap_rate)
    new_cells, new_parcels = finish(
        cell_state, inner_cells, before, after, low, high, deposited, evap_rate, advanced, hot, crossing
    )
    return (new_cells, new_parcels)


def solution(mesh):
    in_specs = (
        P(None, "gx", "gy", None),
        P(),
        P(None, ("gx", "gy")),
        P(None, ("gx", "gy")),
        P(None, ("gx", "gy")),
        P(("gx", "gy"), None),
        P(("gx", "gy")),
    )
    out_specs = (P(None, "gx", "gy", None), P(None, ("gx", "gy")))
    return jax.shard_map(
        on_device, mesh=mesh, in_specs=in_specs, out_specs=out_specs, check_vma=False
    )
```

```python
import functools

import jax
import jax.numpy as jnp
from jax import lax
from jax.experimental import pallas as pl
from jax.experimental.pallas import tpu as pltpu
from jax.sharding import PartitionSpec as P

SECTIONS = 8
SPECIES = 6
COUNT = SECTIONS + SPECIES
LANES = 128
WIDE = 256
GROUPS = 2
F32 = jnp.float32
BF16 = jnp.bfloat16
ANY = pl.BlockSpec(memory_space=pl.ANY)
SMEM = pl.BlockSpec(memory_space=pltpu.SMEM)
VMEM = pl.BlockSpec(memory_space=pltpu.VMEM)
ALL = 63 << 20
MOST = 32 << 20


def call(kernel, out_shape, operands, scratch, in_specs=None, out_specs=ANY, aliases=None, flops=0, moved_bytes=0, grant=MOST):
    many = isinstance(out_shape, (list, tuple))
    return pl.pallas_call(
        kernel,
        out_shape=out_shape,
        in_specs=in_specs or [ANY] * len(operands),
        out_specs=[out_specs] * len(out_shape) if many else out_specs,
        scratch_shapes=scratch,
        input_output_aliases=aliases or {},
        compiler_params=pltpu.CompilerParams(vmem_limit_bytes=grant),
        cost_estimate=pl.CostEstimate(flops=flops, bytes_accessed=moved_bytes, transcendentals=0),
    )(*operands)


def iota(shape, axis):
    return lax.broadcasted_iota(jnp.int32, shape, axis)


def quotient(value, count):
    return value >> (count.bit_length() - 1) if count & (count - 1) == 0 else value // count


def packed(value):
    return value.astype(F32).astype(BF16)


def split(value):
    coarse = value.astype(BF16)
    return coarse, (value - coarse.astype(F32)).astype(BF16)


def rows_of(row, count):
    return jnp.broadcast_to(row, (count, row.shape[1])).astype(BF16)


def hot_columns(lower, count):
    return jnp.where(rows_of(lower.astype(F32), count) == packed(iota((count, LANES), 0)), 1.0, 0.0).astype(BF16)


def contract_lanes(left, right):
    return lax.dot_general(left, right, (((1,), (1,)), ((), ())), preferred_element_type=F32)


def advance_block(block):
    row = iota(block.shape, 0)
    diameter = jnp.broadcast_to(block[6:7], block.shape)
    warmth = jnp.broadcast_to(block[7:8], block.shape)
    factor = 0.8 / (1.0 + diameter * diameter)
    slowed = block * (1.0 - factor)
    travel = pltpu.roll(0.5 * (block + slowed), 5, 0)
    shrunk = block * (1.0 - 0.05 * warmth)
    warmed = block + factor * (1.0 - block)
    return jnp.where(row < 3, block + travel, jnp.where(row < 6, slowed, jnp.where(row == 6, shrunk, warmed)))


def scatter_left(left_ref, at, upper, uppers, coarse, fine):
    upper = rows_of(upper.astype(F32), 16)
    twice_coarse = jnp.concatenate([coarse.astype(F32)] * 2, axis=0).astype(BF16)
    twice_fine = jnp.concatenate([fine.astype(F32)] * 2, axis=0).astype(BF16)
    zero = jnp.zeros((16, LANES), BF16)
    pair = iota((16, LANES), 0) // 8
    for u in range(0, uppers, 2):
        hit = upper == packed(pair + u)
        left_ref[8 * u : 8 * u + 16, at] = jnp.where(hit, twice_coarse, zero)
        left_ref[8 * (uppers + u) : 8 * (uppers + u) + 16, at] = jnp.where(hit, twice_fine, zero)


def bucket_into(owner_total, capacity, cell_total, mass_ref, owner_ref, cell_ref, out_ref, left_ref, hot_ref):
    blocks = owner_ref.shape[0]
    uppers = out_ref.shape[0] // 9 // 2
    strict = iota((LANES, 2 * LANES), 0) < iota((LANES, 2 * LANES), 1)
    strict = jnp.where(strict, 1.0, 0.0).astype(BF16)
    owners = owner_ref[...]
    cells = cell_ref[...]
    keys = owner_total * GROUPS
    order = owners * GROUPS + quotient(cells, cell_total // GROUPS)
    hots = [
        jnp.where(jnp.broadcast_to(order[b : b + 1], (keys, LANES)) == iota((keys, LANES), 0), 1.0, 0.0)
        for b in range(blocks)
    ]
    ranks = jnp.dot(jnp.concatenate(hots, axis=0).astype(BF16), strict, preferred_element_type=F32)
    parts = [ranks[b * keys : (b + 1) * keys] for b in range(blocks)]
    counts = sum(part[:, LANES:] for part in parts)
    key, other = iota((keys, keys), 0), iota((keys, keys), 1)
    same = quotient(key, GROUPS) == quotient(other, GROUPS)
    sums = jnp.concatenate([jnp.where(same & (other < key), 1.0, 0.0), jnp.where(same, 1.0, 0.0)], axis=0).astype(BF16)
    sums = jnp.dot(sums, counts.astype(BF16), preferred_element_type=F32)
    carry, owned = sums[:keys], sums[keys:]
    base = 16 * uppers
    for b in range(blocks):
        rank = jnp.sum(hots[b] * (parts[b][:, :LANES] + carry), axis=0, keepdims=True)
        total = jnp.sum(hots[b] * owned, axis=0, keepdims=True)
        carry = carry + parts[b][:, LANES:]
        spot = owners[b : b + 1] * capacity + ((rank * float(capacity) + 0.5) / total).astype(jnp.int32)
        at = slice(b * LANES, (b + 1) * LANES)
        hot_ref[:, at] = hot_columns(spot & (WIDE - 1), WIDE)
        coarse, fine = split(mass_ref[:, at])
        upper = spot >> 8
        scatter_left(left_ref, at, upper, uppers, coarse, fine)
        hit = rows_of(upper.astype(F32), uppers) == packed(iota((uppers, LANES), 0))
        zero = jnp.zeros((uppers, LANES), BF16)
        cell = cells[b : b + 1]
        left_ref[base : base + uppers, at] = jnp.where(hit, rows_of((cell >> 8).astype(F32), uppers), zero)
        left_ref[base + uppers : base + 2 * uppers, at] = jnp.where(
            hit, rows_of((cell & (WIDE - 1)).astype(F32), uppers), zero
        )
        left_ref[base + 2 * uppers : base + 3 * uppers, at] = jnp.where(hit, 1.0, 0.0).astype(BF16)
    placed = contract_lanes(left_ref[...], hot_ref[...])
    cell = placed[base : base + uppers] * float(WIDE) + placed[base + uppers : base + 2 * uppers]
    cell = jnp.where(placed[base + 2 * uppers : base + 3 * uppers] > 0.5, cell, -1.0)
    for u in range(uppers):
        mass = placed[8 * u : 8 * u + 8] + placed[8 * (uppers + u) : 8 * (uppers + u) + 8]
        for half in range(2):
            row = 9 * (2 * u + half)
            lanes = slice(half * LANES, (half + 1) * LANES)
            out_ref[row : row + 8, :] = mass[:, lanes]
            out_ref[row + 8 : row + 9, :] = cell[u : u + 1, lanes]


def prepare_kernel(
    owner_total, capacity,
    cells_hbm, parcels_hbm, crossing_hbm, mass_hbm, owner_hbm, cell_hbm,
    up_hbm, down_hbm, yup_hbm, ydown_hbm, advanced_hbm, hot_hbm, filled_hbm,
    cells_ref, parcels_ref, crossing_ref, mass_ref, owner_ref, cell_ref,
    leave_ref, yup_ref, ydown_ref, advanced_ref, hot_ref, filled_ref,
    parts_ref, left_ref, spot_ref, sems,
):
    size_x, size_y, size_z = cells_hbm.shape[1:]
    face = slice(0, COUNT + 1)
    tail = slice(COUNT + 1, up_hbm.shape[0])
    pairs = [
        (crossing_hbm, crossing_ref),
        (owner_hbm, owner_ref),
        (cell_hbm, cell_ref),
        (mass_hbm, mass_ref),
        (parcels_hbm, parcels_ref),
        (cells_hbm, cells_ref),
        (cells_ref.at[face, size_x - 1], up_hbm.at[face]),
        (cells_ref.at[face, 0], down_hbm.at[face]),
        (filled_ref, filled_hbm),
        (hot_ref, hot_hbm),
        (advanced_ref, advanced_hbm),
        (leave_ref.at[0], up_hbm.at[tail]),
        (leave_ref.at[1], down_hbm.at[tail]),
        (yup_ref, yup_hbm),
        (ydown_ref, ydown_hbm),
    ]
    copies = [pltpu.make_async_copy(source, target, sems.at[i]) for i, (source, target) in enumerate(pairs)]
    for copy in copies[:6]:
        copy.start()
    cross = crossing_ref.shape[1]
    slot_total = parcels_ref.shape[1]
    copies[0].wait()
    for side in range(2):
        for first in range(0, cross, LANES):
            lower = crossing_ref[side : side + 1, first : first + LANES] & (WIDE - 1)
            hot_ref[:, side * cross + first : side * cross + first + LANES] = hot_columns(lower, WIDE)
    copies[9].start()
    copies[4].wait()

    def advance_pair(i, unused):
        for number in range(2):
            blocks = []
            for half in range(2):
                at = pl.ds(pl.multiple_of((4 * i + 2 * number + half) * LANES, LANES), LANES)
                block = advance_block(parcels_ref[:, at])
                advanced_ref[:, at] = block
                blocks.append(block)
            parts_ref[pl.ds(pl.multiple_of((2 * i + number) * 8, 8), 8), :] = jnp.concatenate(blocks, axis=1)
        return unused

    lax.fori_loop(0, slot_total // (4 * LANES), advance_pair, 0, unroll=4)
    copies[10].start()
    for copy in (*copies[1:4], copies[5]):
        copy.wait()
    copies[6].start()
    copies[7].start()

    halves_y, halves_z = size_y // 8, size_z // LANES
    part_rows = parts_ref.shape[0]
    step_rows = min(256, part_rows)
    for rows in range(0, part_rows, step_rows):
        coarse, fine = split(parts_ref[rows : rows + step_rows])
        for side in range(2):
            for first in range(0, cross, WIDE):
                upper = jnp.broadcast_to(crossing_ref[side : side + 1, first : first + WIDE] >> 8, (8, WIDE))
                hot = hot_ref[:, side * cross + first : side * cross + first + WIDE]
                picked = jnp.dot(coarse, hot, preferred_element_type=F32) + jnp.dot(
                    fine, hot, preferred_element_type=F32
                )
                spots = []
                for offset in range(0, WIDE, LANES):
                    layer, rest = divmod((first + offset) // LANES, halves_y * halves_z)
                    half_y, half_z = divmod(rest, halves_z)
                    spots.append((side, layer, slice(8 * half_y, 8 * half_y + 8), slice(LANES * half_z, LANES * (half_z + 1))))
                if rows:
                    total = jnp.concatenate([leave_ref[spot] for spot in spots], axis=1)
                else:
                    total = jnp.zeros((8, WIDE), F32)
                for i in range(0, step_rows, 8):
                    total = jnp.where(upper == (rows + i) // 8, picked[i : i + 8], total)
                for number, spot in enumerate(spots):
                    leave_ref[spot] = total[:, number * LANES : (number + 1) * LANES]
    bucket_into(owner_total, capacity, size_x * size_y * size_z, mass_ref, owner_ref, cell_ref, filled_ref, left_ref, spot_ref)
    copies[8].start()
    for c in range(COUNT + 1):
        source = c if c < COUNT else COUNT + 1
        yup_ref[c] = cells_ref[source, :, size_y - 1, :]
        ydown_ref[c] = cells_ref[source, :, 0, :]
    for copy in copies[11:]:
        copy.start()
    for copy in copies[6:]:
        copy.wait()


def prepare(cells, parcels, crossing, mass, owner, cell, owner_total, capacity):
    size_x, size_y, size_z = cells.shape[1:]
    extra = 8 * crossing.shape[1] // (size_y * size_z)
    places = owner_total * capacity
    shape = jax.ShapeDtypeStruct
    face = shape((COUNT + 1 + extra, size_y, size_z), F32)
    side = shape((COUNT + 1, size_x, size_z), F32)
    advanced = shape(parcels.shape, F32)
    hot = shape((WIDE, crossing.size), BF16)
    filled = shape((9 * places // LANES, LANES), F32)
    operands = (cells, parcels, crossing, mass, owner, cell)
    scratch = [pltpu.VMEM(a.shape, a.dtype) for a in operands]
    scratch += [pltpu.VMEM((2, extra, size_y, size_z), F32)]
    scratch += [pltpu.VMEM(a.shape, a.dtype) for a in (side, side, advanced, hot, filled)]
    scratch += [
        pltpu.VMEM((8 * parcels.shape[1] // WIDE, WIDE), F32),
        pltpu.VMEM((19 * places // WIDE, mass.shape[1]), BF16),
        pltpu.VMEM((WIDE, mass.shape[1]), BF16),
        pltpu.SemaphoreType.DMA((15,)),
    ]
    return call(
        functools.partial(prepare_kernel, owner_total, capacity),
        [face, face, side, side, advanced, hot, filled], operands, scratch,
        flops=2 << 30, moved_bytes=6 << 20, grant=ALL,
    )


def arrive_into(advanced_ref, hot_ref, crossing_ref, before_ref, after_ref, out_hbm, out_ref, left_refs, sems):
    cross = crossing_ref.shape[1]
    uppers = advanced_ref.shape[1] // WIDE
    size_y, size_z = before_ref.shape[1:]
    halves_y, halves_z = size_y // 8, size_z // LANES
    step = min(32, uppers)
    totals = [0.0] * (uppers // step)
    hit = 0.0
    for side, (come_ref, left_ref) in enumerate(zip((before_ref, after_ref), left_refs)):
        for first in range(0, cross, LANES):
            layer, rest = divmod(first // LANES, halves_y * halves_z)
            half_y, half_z = divmod(rest, halves_z)
            block = come_ref[COUNT + 1 + layer, 8 * half_y : 8 * half_y + 8, LANES * half_z : LANES * (half_z + 1)]
            coarse, fine = split(block)
            upper = crossing_ref[side : side + 1, first : first + LANES] >> 8
            at = slice(first, first + LANES)
            scatter_left(left_ref, at, upper, uppers, coarse, fine)
            taken = rows_of(upper.astype(F32), uppers) == packed(iota((uppers, LANES), 0))
            left_ref[16 * uppers :, at] = jnp.where(taken, 1.0, 0.0).astype(BF16)
        hot = hot_ref[:, side * cross : (side + 1) * cross]
        hit = hit + contract_lanes(left_ref[16 * uppers :], hot)
        for number, u in enumerate(range(0, uppers, step)):
            totals[number] = (
                totals[number]
                + contract_lanes(left_ref[8 * u : 8 * (u + step)], hot)
                + contract_lanes(left_ref[8 * (uppers + u) : 8 * (uppers + u + step)], hot)
            )
    outs = []
    for number, u in enumerate(range(0, uppers, step)):
        for i in range(step):
            at = slice((u + i) * WIDE, (u + i + 1) * WIDE)
            taken = jnp.broadcast_to(hit[u + i : u + i + 1], (8, WIDE)) > 0.5
            out_ref[:, at] = jnp.where(taken, totals[number][8 * i : 8 * i + 8], advanced_ref[:, at])
        at = slice(u * WIDE, (u + step) * WIDE)
        out = pltpu.make_async_copy(out_ref.at[:, at], out_hbm.at[:, at], sems.at[number])
        out.start()
        outs.append(out)
    return outs


def shift_up(value, axis):
    return pltpu.roll(value, value.shape[axis] - 1, axis)


def shift_down(value, axis):
    return pltpu.roll(value, 1, axis)


def slab_update(left, center, right, side_low, side_high, rate_ref, write):
    course = center(COUNT)
    size_y, size_z = course.shape
    first_row = iota((size_y, size_z), 0) == 0
    last_row = iota((size_y, size_z), 0) == size_y - 1

    def row_up(value, edge):
        return jnp.where(last_row, edge, shift_up(value, 0))

    def row_down(value, edge):
        return jnp.where(first_row, edge, shift_down(value, 0))

    face_x = 0.5 * (course + right(COUNT))
    face_x_low = 0.5 * (left(COUNT) + course)
    course_y = center(COUNT + 1)
    face_y = 0.5 * (course_y + row_up(course_y, side_high(COUNT)))
    face_y_low = 0.5 * (row_down(course_y, side_low(COUNT)) + course_y)
    course_z = center(COUNT + 2)
    lane = iota((size_y, size_z), 1)
    face_z = jnp.where(lane == size_z - 1, 0.0, 0.5 * (course_z + shift_up(course_z, 1)))
    face_z_low = jnp.where(lane == 0, 0.0, 0.5 * (shift_down(course_z, 1) + course_z))
    from_x_up, from_x_low = jnp.minimum(face_x, 0.0), jnp.maximum(face_x_low, 0.0)
    from_y_up, from_y_low = jnp.minimum(face_y, 0.0), jnp.maximum(face_y_low, 0.0)
    from_z_up, from_z_low = jnp.minimum(face_z, 0.0), jnp.maximum(face_z_low, 0.0)
    own = 1.0 - (
        (jnp.maximum(face_x, 0.0) - jnp.minimum(face_x_low, 0.0))
        + (jnp.maximum(face_y, 0.0) - jnp.minimum(face_y_low, 0.0))
        + (jnp.maximum(face_z, 0.0) - jnp.minimum(face_z_low, 0.0))
    )

    def moved(c):
        amount = center(c)
        total = own * amount
        total = total - from_x_up * right(c) + from_x_low * left(c)
        total = total - from_y_up * row_up(amount, side_high(c)) + from_y_low * row_down(amount, side_low(c))
        return total - from_z_up * shift_up(amount, 1) + from_z_low * shift_down(amount, 1)

    vapour = moved(SECTIONS)
    beside = 1.0 + vapour
    later = None
    gained = None
    for s in reversed(range(SECTIONS)):
        section = moved(s)
        loss = rate_ref[s] * section / beside
        value = section - loss
        if later is not None:
            value = value + 0.5 * later
            gained = later if gained is None else gained + later
        write(s, value)
        later = loss
    write(SECTIONS, vapour + later + 0.5 * gained)
    for c in range(SECTIONS + 1, COUNT):
        write(c, moved(c))


def inner_kernel(
    cells_ref, low_ref, high_ref, deposit_ref, rate_ref, out_hbm, out_ref, sems
):
    last = cells_ref.shape[1] - 1

    def store(x):
        return pltpu.make_async_copy(out_ref.at[:, x], out_hbm.at[:, x], sems.at[x])

    def middle(x, unused):
        def write(c, value):
            out_ref[c, x] = value + deposit_ref[c, x] if c < SECTIONS else value

        slab_update(
            lambda c: cells_ref[c, x - 1],
            lambda c: cells_ref[c, x],
            lambda c: cells_ref[c, x + 1],
            lambda c: low_ref[c, pl.ds(x, 1), :],
            lambda c: high_ref[c, pl.ds(x, 1), :],
            rate_ref,
            write,
        )
        store(x).start()
        return unused

    lax.fori_loop(1, last, middle, 0)
    for x in range(1, last):
        store(x).wait()


def inner(cells, low, high, deposited, rate):
    out = jax.ShapeDtypeStruct((COUNT,) + cells.shape[1:], F32)
    return call(
        inner_kernel, out, (cells, low, high, deposited, rate),
        [pltpu.VMEM(out.shape, F32), pltpu.SemaphoreType.DMA((cells.shape[1],))],
        in_specs=[VMEM] * 4 + [SMEM], flops=30 << 20, moved_bytes=4 << 20,
    )


def last_kernel(
    cells_ref, inner_hbm, before_ref, after_ref, low_ref, high_ref, deposit_ref, rate_ref,
    advanced_ref, hot_ref, crossing_ref, out_hbm, parcels_hbm, out_ref, parcels_ref, left_before_ref, left_after_ref, sems, parcel_sems,
):
    last = cells_ref.shape[1] - 1
    copies = [
        pltpu.make_async_copy(out_ref.at[:, 0], out_hbm.at[:, 0], sems.at[0]),
        pltpu.make_async_copy(out_ref.at[:, 1], out_hbm.at[:, last], sems.at[1]),
    ]

    def layer(left, number, x, right):
        def write(c, value):
            out_ref[c, number] = value + deposit_ref[c, x] if c < SECTIONS else value

        slab_update(
            left,
            lambda c: cells_ref[c, x],
            right,
            lambda c: low_ref[c, x : x + 1, :],
            lambda c: high_ref[c, x : x + 1, :],
            rate_ref,
            write,
        )
        copies[number].start()

    layer(lambda c: before_ref[c], 0, 0, lambda c: cells_ref[c, 1])
    layer(lambda c: cells_ref[c, last - 1], 1, last, lambda c: after_ref[c])
    copies += arrive_into(
        advanced_ref, hot_ref, crossing_ref, before_ref, after_ref, parcels_hbm, parcels_ref,
        (left_before_ref, left_after_ref), parcel_sems,
    )
    for copy in copies:
        copy.wait()


def finish(cells, inner_cells, before, after, low, high, deposited, rate, advanced, hot, crossing):
    size_y, size_z = cells.shape[2:]
    uppers = advanced.shape[1] // WIDE
    return call(
        last_kernel, [jax.ShapeDtypeStruct(inner_cells.shape, F32), jax.ShapeDtypeStruct(advanced.shape, F32)],
        (cells, inner_cells, before, after, low, high, deposited, rate, advanced, hot, crossing),
        [
            pltpu.VMEM((COUNT, 2, size_y, size_z), F32),
            pltpu.VMEM(advanced.shape, F32),
            pltpu.VMEM((17 * uppers, crossing.shape[1]), BF16),
            pltpu.VMEM((17 * uppers, crossing.shape[1]), BF16),
            pltpu.SemaphoreType.DMA((2,)),
            pltpu.SemaphoreType.DMA((-(-uppers // 32),)),
        ],
        in_specs=[VMEM, ANY] + [VMEM] * 5 + [SMEM] + [VMEM] * 3, aliases={1: 0},
        flops=1 << 30, moved_bytes=5 << 20,
    )


def deposit_kernel(shape, windows, routed_ref, out_ref, mass_ref, spread_ref, depth_ref):
    size_x, size_y, size_z = shape
    groups = routed_ref.shape[0] // 9
    per = groups // 8
    span = LANES // per
    lane_part = quotient(iota((8, LANES), 1), span)
    for v in range(9):
        rows = routed_ref[pl.ds(v, groups, stride=9), :]
        for q in range(per):
            total = None
            for g in range(per):
                block = rows[8 * g : 8 * g + 8]
                if g != q:
                    block = pltpu.roll(block, (span * (g - q)) % LANES, 1)
                total = block if total is None else jnp.where(lane_part == g, block, total)
            mass_ref[q, v] = total

    bounds = []
    for q in range(per):
        cell = mass_ref[q, SECTIONS].astype(jnp.int32)
        layer = quotient(cell, size_y * size_z)
        valid = cell >= 0
        bounds.append((jnp.min(jnp.where(valid, layer, size_x)), jnp.max(jnp.where(valid, layer, -1))))

    zero = jnp.zeros((size_y, LANES), BF16)

    def deposit(q, start):
        window = windows[q]
        half = SECTIONS * window * size_y
        first = jnp.minimum(start, size_x - window)
        cell = mass_ref[q, SECTIONS].astype(jnp.int32)
        plane = quotient(cell, size_z)
        depth = cell - plane * size_z
        plane = jnp.where(plane >= start * size_y, plane - first * size_y, -1)
        plane = jnp.where(cell >= 0, plane, -1).astype(F32)
        parts = [split(mass_ref[q, s]) for s in range(SECTIONS)]
        for i in range(8):
            at = slice(i * LANES, (i + 1) * LANES)
            depth_ref[q % 2, :, at] = hot_columns(depth[i : i + 1], size_z)
            plane_rows = rows_of(plane[i : i + 1], size_y)
            rows = [[rows_of(part[i : i + 1].astype(F32), size_y) for part in pair] for pair in parts]
            for w in range(window):
                hit = plane_rows == packed(iota((size_y, LANES), 0) + w * size_y)
                for s in range(SECTIONS):
                    base = (s * window + w) * size_y
                    for part in range(2):
                        spread_ref[q % 2, part * half + base : part * half + base + size_y, at] = jnp.where(
                            hit, rows[s][part], zero
                        )
        added = contract_lanes(spread_ref[q % 2, : 2 * half], depth_ref[q % 2])
        for s in range(SECTIONS):
            base = s * window * size_y
            rows = added[base : base + window * size_y] + added[half + base : half + base + window * size_y]
            at = pl.ds(first, window)
            out_ref[s, at] = out_ref[s, at] + rows.reshape(window, size_y, size_z)

    out_ref[...] = jnp.zeros(out_ref.shape, F32)
    for q in range(per):
        deposit(q, bounds[q][0] if windows[q] < size_x else 0)
    for q in range(per):
        if windows[q] < size_x:
            low, high = bounds[q]

            def more(t, unused, q=q, low=low):
                deposit(q, low + t * windows[q])
                return unused

            lax.fori_loop(1, jnp.where(high - low < windows[q], 1, 1 + (size_x - 1) // windows[q]), more, 0)


def deposit(routed, shape, windows):
    size_x, size_y, size_z = shape
    per = routed.shape[0] // 9 // 8
    return call(
        functools.partial(deposit_kernel, shape, windows), jax.ShapeDtypeStruct((SECTIONS,) + shape, F32), (routed,),
        [
            pltpu.VMEM((per, SECTIONS + 1, 8, LANES), F32),
            pltpu.VMEM((2, 2 * SECTIONS * max(windows) * size_y, 8 * LANES), BF16),
            pltpu.VMEM((2, size_z, 8 * LANES), BF16),
        ],
        in_specs=[VMEM], out_specs=VMEM, flops=1 << 30, moved_bytes=2 << 20,
    )


def ring(size):
    up = [(i, (i + 1) % size) for i in range(size)]
    return up, [(j, i) for i, j in up]


def on_device(cell_state, evap_rate, parcels, crossing, conv_mass, conv_owner, conv_cell):
    owner_total = lax.axis_size("gx") * lax.axis_size("gy")
    row_total = conv_owner.shape[0]
    capacity = 2 * row_total // owner_total
    up_x, down_x = ring(lax.axis_size("gx"))
    up_y, down_y = ring(lax.axis_size("gy"))

    send_up, send_down, side_up, side_down, advanced, hot, filled = prepare(
        cell_state, parcels, crossing, conv_mass, conv_owner.reshape(-1, LANES), conv_cell.reshape(-1, LANES),
        owner_total, capacity,
    )
    before = lax.ppermute(send_up, "gx", up_x)
    after = lax.ppermute(send_down, "gx", down_x)
    low = lax.ppermute(side_up, "gy", up_y)
    high = lax.ppermute(side_down, "gy", down_y)

    fold = LANES // capacity
    filled = filled.reshape(-1, 9, fold, capacity).transpose(0, 2, 1, 3).reshape(owner_total, 1, 9 * capacity)
    routed = lax.all_to_all(filled, ("gx", "gy"), split_axis=0, concat_axis=0, tiled=True)
    routed = routed.reshape(-1, fold, 9, capacity).transpose(0, 2, 1, 3).reshape(-1, LANES)

    layers = cell_state.shape[1]
    parts = routed.shape[0] // 9 // 8
    windows = [layers] * parts
    if fold == 1:
        spans = [(max(q * GROUPS - 1, 0) // parts, ((q + 1) * GROUPS) // parts + 1) for q in range(parts)]
        windows = [layers * (min(high, GROUPS) - low) // GROUPS for low, high in spans]
    deposited = deposit(routed, cell_state.shape[1:], windows)
    inner_cells = inner(cell_state, low, high, deposited, evap_rate)
    new_cells, new_parcels = finish(
        cell_state, inner_cells, before, after, low, high, deposited, evap_rate, advanced, hot, crossing
    )
    return (new_cells, new_parcels)


def solution(mesh):
    in_specs = (
        P(None, "gx", "gy", None),
        P(),
        P(None, ("gx", "gy")),
        P(None, ("gx", "gy")),
        P(None, ("gx", "gy")),
        P(("gx", "gy"), None),
        P(("gx", "gy")),
    )
    out_specs = (P(None, "gx", "gy", None), P(None, ("gx", "gy")))
    return jax.shard_map(
        on_device, mesh=mesh, in_specs=in_specs, out_specs=out_specs, check_vma=False
    )
```
